32 devices in a mesh: shard: 4 (over z), ctx: 2 (over y), tp: 4 (over x, core).
Axes of the slice: x: 2, y: 2, z: 4, core: 2. Of those that a mesh axis runs over, the one named last changes fastest.
Arguments:
- frames: bfloat16 [4, 1536, 768], P('shard', 'ctx'), may hold values from -6 to 6
- cotangent: bfloat16 [4, 1536, 768], P('shard', 'ctx'), may hold values from -6 to 6
- w_qkv: bfloat16 [2, 768, 12, 192], P(None, 'shard', 'tp'), may hold values from -2 to 2
- qv_bias: bfloat16 [2, 12, 128], P(None, 'tp', 'shard'), may hold values from -3 to 3
- w_out: bfloat16 [2, 12, 64, 768], P(None, 'tp', None, 'shard'), may hold values from -0.375 to 0.375
- w_up: bfloat16 [2, 768, 3072], P(None, 'shard', 'tp'), may hold values from -0.21875 to 0.21875
- up_bias: bfloat16 [2, 48, 64], P(None, 'tp', 'shard'), may hold values from -3 to 3
- w_down: bfloat16 [2, 3072, 768], P(None, 'tp', 'shard'), may hold values from -0.109375 to 0.109375
- norm_gains: bfloat16 [2, 2, 768], P(None, None, 'shard'), may hold values from 0.099609375 to 1.8984375
- shifts: bfloat16 [2, 4, 768], P(None, None, 'shard'), may hold values from -3 to 3
Outputs:
- out_frames: bfloat16 [4, 1536, 768], P('shard', 'ctx')
- frames_grad: bfloat16 [4, 1536, 768], P('shard', 'ctx')
- grad_w_qkv: float32 [2, 768, 12, 192], P(None, 'shard', 'tp')
- grad_qv_bias: float32 [2, 12, 128], P(None, 'tp', 'shard')
- grad_w_out: float32 [2, 12, 64, 768], P(None, 'tp', None, 'shard')
- grad_w_up: float32 [2, 768, 3072], P(None, 'shard', 'tp')
- grad_up_bias: float32 [2, 48, 64], P(None, 'tp', 'shard')
- grad_w_down: float32 [2, 3072, 768], P(None, 'tp', 'shard')
- grad_norm_gains: float32 [2, 2, 768], P(None, None, 'shard')
- grad_shifts: float32 [2, 4, 768], P(None, None, 'shard')
The draws below stay inside these ranges and needn't reach their ends.
All inputs are finite; a program needn't handle non-finite values.
Results may differ from the reference program's by a relative error of at most 0.015.
Values may be sent and summed in bfloat16 or wider, within the bound.
No kernel may reach another device: no remote copies, remote signals or barrier semaphores. Data moves between devices by JAX's collectives and lax.ppermute only.
A program may use at most 192 MiB of HBM per device.

```python
import jax
import jax.numpy as jnp
from jax import lax

D = 768
HEADS = 12
HD = 64
FF = 3072
LAYERS = 2
SEQ = 1536
CLIPS = 4


def draw_w_qkv(key, part):
    key = jax.random.fold_in(key, 7)
    base = jax.random.truncated_normal(key, -4.0, 4.0, (LAYERS, D, HEADS, 3 * HD), jnp.float32) * D ** (-0.5)
    column = jnp.arange(3 * HD)
    widen = jnp.where(column < 2 * HD, 1.25, 1.0).astype(jnp.float32)
    return jnp.clip(base * widen, -2.0, 2.0).astype(jnp.bfloat16)


def level_of(own_key, dims, cuts, least, high):
    level = 1.0
    for dim, parts in cuts:
        draws = jax.random.uniform(jax.random.fold_in(jax.random.fold_in(own_key, 6), dim), (parts,), jnp.float32, least / len(cuts), high / len(cuts))
        level = level * jnp.repeat(jnp.exp(draws), dims[dim] // parts).reshape((-1,) + (1,) * (len(dims) - 1 - dim))
    return level


def noise(key, shape, width, most, shards=(), held_as=jnp.bfloat16):
    factor_of = level_of(key, shape, shards, -0.22, 0.18) if shards else 1.0
    values = jax.random.normal(key, shape, jnp.float32) * width * factor_of
    return jnp.minimum(jnp.maximum(values, -most), most).astype(held_as)


def setup_inputs(seed: int = 0) -> dict:
    keys = jax.random.split(jax.random.key(seed), 11)
    frames = noise(keys[0], (CLIPS, SEQ, D), 1.0, 6.0, ((0, 4), (1, 2)))
    cotangent = noise(keys[1], (CLIPS, SEQ, D), 1.0, 6.0, ((0, 4), (1, 2)))
    w_qkv = draw_w_qkv(jax.random.fold_in(keys[10], 71), 0)
    qv_bias = noise(keys[3], (LAYERS, HEADS, 2 * HD), 0.5, 3.0, ((1, 4), (2, 4)))
    w_out = noise(keys[4], (LAYERS, HEADS, HD, D), (D // 3) ** -0.5, 0.375, ((1, 4), (3, 4)))
    w_up = noise(keys[5], (LAYERS, D, FF), D ** -0.5, 0.21875, ((1, 4), (2, 4)))
    up_bias = noise(keys[6], (LAYERS, FF // 64, 64), 0.5, 3.0, ((1, 4), (2, 4)))
    w_down = noise(keys[7], (LAYERS, FF, D), FF ** -0.5, 0.109375, ((1, 4), (2, 4)))
    norm_gains = jnp.clip(1.0 + 0.18 * jax.random.normal(keys[8], (LAYERS, 2, D), jnp.float32), 0.099609375, 1.8984375).astype(jnp.bfloat16)
    shifts = noise(keys[9], (LAYERS, 4, D), 0.5, 3.0, ((2, 4),))
    return {"frames": frames, "cotangent": cotangent, "w_qkv": w_qkv, "qv_bias": qv_bias, "w_out": w_out, "w_up": w_up, "up_bias": up_bias, "w_down": w_down, "norm_gains": norm_gains, "shifts": shifts}


epsilon = 1e-05

@jax.custom_vjp
def low(v):
    return lax.optimization_barrier(v.astype(jnp.bfloat16)).astype(jnp.float32)

@jax.custom_vjp
def low_back(v):
    return v

def low_keep(v):
    return (low(v), None)

def low_pass(kept, grad):
    return (grad,)

def back_keep(v):
    return (v, None)

def back_low(kept, grad):
    return (low(grad),)
low.defvjp(low_keep, low_pass)
low_back.defvjp(back_keep, back_low)

def normalize(values, gain, shift):
    centre = lax.optimization_barrier(jnp.mean(values, -1, keepdims=True))
    centred = values - centre
    spread = lax.optimization_barrier(jnp.mean(centred * centred, -1, keepdims=True))
    return centred * lax.rsqrt(spread + epsilon) * gain + shift

def attend(pieces):
    queries, key_part, value_part = pieces
    scores = low_back(jnp.einsum('qhe,khe->hqk', queries, key_part, precision=lax.Precision.HIGHEST) * HD ** (-0.5))
    probs = low(jax.nn.softmax(scores, axis=-1))
    return jnp.einsum('hqk,khe->qhe', probs, value_part, precision=lax.Precision.HIGHEST)

def encoder_layer(stream, wqkv, qvb, wout, wup, bup, wdown, gains, offsets):
    highest = lax.Precision.HIGHEST
    normed_in = low(normalize(stream, gains[0], offsets[0]))
    projected = jnp.einsum('csd,dhe->cshe', normed_in, wqkv, precision=highest)
    queries = low_back(low(projected[..., :HD] + qvb[:, :HD]))
    key_part = low_back(low(projected[..., HD:2 * HD]))
    value_part = low_back(low(projected[..., 2 * HD:] + qvb[:, HD:]))
    attended = lax.map(jax.checkpoint(attend), (queries, key_part, value_part))
    attended = low_back(low(attended))
    branch = low_back(jnp.einsum('cshe,hed->csd', attended, wout, precision=highest) + offsets[1])
    middle = stream + branch
    normed_mid = low(normalize(middle, gains[1], offsets[2]))
    pre_act = low_back(jnp.einsum('csd,df->csf', normed_mid, wup, precision=highest) + bup)
    hidden = low(jax.nn.gelu(pre_act, approximate=False))
    mlp_out = low_back(jnp.einsum('csf,fd->csd', hidden, wdown, precision=highest) + offsets[3])
    return middle + mlp_out

def forward(stream, wqkv, qvb, wout, wup, bup, wdown, gains, offsets):
    for layer_idx in range(LAYERS):
        stream = encoder_layer(stream, wqkv[layer_idx], qvb[layer_idx], wout[layer_idx], wup[layer_idx], bup[layer_idx].reshape(-1), wdown[layer_idx], gains[layer_idx], offsets[layer_idx])
    return stream

def reference(frames, cotangent, w_qkv, qv_bias, w_out, w_up, up_bias, w_down, norm_gains, shifts):
    f32 = jnp.float32
    result, pullback = jax.vjp(forward, frames.astype(f32), w_qkv.astype(f32), qv_bias.astype(f32), w_out.astype(f32), w_up.astype(f32), up_bias.astype(f32), w_down.astype(f32), norm_gains.astype(f32), shifts.astype(f32))
    grads = pullback(cotangent.astype(f32))
    return (result.astype(jnp.bfloat16), grads[0].astype(jnp.bfloat16), grads[1], grads[2], grads[3], grads[4], grads[5], grads[6], grads[7], grads[8])
```

```python
import math

import jax
import jax.numpy as jnp
from jax import lax
from jax.experimental import pallas as pl
from jax.experimental.pallas import tpu as pltpu
from jax.sharding import PartitionSpec as P

f32 = jnp.float32
bf16 = jnp.bfloat16
EPSILON = 1e-05
NN = (((1,), (0,)), ((), ()))
NT = (((1,), (1,)), ((), ()))
TN = (((0,), (0,)), ((), ()))
VMEM_BYTES = 40 * 1024 * 1024
WIDE = 128


def mm(a, b, dims=NN):
    return lax.dot_general(a, b, dims, preferred_element_type=f32)


def core_swap(x):
    return lax.ppermute(x, "tp", [(i, i ^ 1) for i in range(4)])


def x_swap(x):
    return lax.ppermute(x, "tp", [(i, i ^ 2) for i in range(4)])


def y_swap(x):
    return lax.ppermute(x, "ctx", [(0, 1), (1, 0)])


def gather_rows(x, shards):
    if shards != 4:
        return [lax.all_gather(x, "shard", axis=0, tiled=True)]
    up = [(i, (i + 1) % 4) for i in range(4)]
    down = [(i, (i - 1) % 4) for i in range(4)]
    half = x.shape[0] // 2
    below = lax.ppermute(x, "shard", up)
    above = lax.ppermute(x, "shard", down)
    far_low = lax.ppermute(below[:half], "shard", up)
    far_high = lax.ppermute(above[half:], "shard", down)
    return [x, below, above, far_low, far_high]


def piece_offsets(rows, shards):
    if shards != 4:
        return [jnp.int32(0)]
    me = lax.axis_index("shard").astype(jnp.int32)
    far = ((me + 2) % 4) * rows
    return [me * rows, ((me + 3) % 4) * rows, ((me + 1) % 4) * rows, far, far + rows // 2]


def vmem():
    return pl.BlockSpec(memory_space=pltpu.VMEM)


def run(kernel, ins, outs, scratch=(), pieces=(), scalars=None, flops=0, name=None):
    specs = [vmem() for _ in ins] + [pl.BlockSpec(memory_space=pl.ANY) for _ in pieces]
    args = list(ins) + list(pieces)
    if scalars is not None:
        specs = [pl.BlockSpec(memory_space=pltpu.SMEM)] + specs
        args = [scalars] + args
    size = sum(a.size * a.dtype.itemsize for a in args)
    size += sum(math.prod(s) * jnp.dtype(d).itemsize for s, d in outs)
    return pl.pallas_call(
        kernel,
        out_shape=[jax.ShapeDtypeStruct(s, d) for s, d in outs],
        in_specs=specs,
        out_specs=[vmem() for _ in outs],
        scratch_shapes=list(scratch),
        compiler_params=pltpu.CompilerParams(vmem_limit_bytes=VMEM_BYTES),
        cost_estimate=pl.CostEstimate(flops=int(flops), bytes_accessed=int(size), transcendentals=0),
        name=name,
    )(*args)


def weight_copies(scal, pieces, columns, dest, sems, by_parity):
    count = len(pieces) // 2
    copies = []
    for pair in range(2):
        if by_parity:
            slot = scal[8] if pair == 0 else 1 - scal[8]
        else:
            slot = pair
        for j in range(count):
            piece = pieces[pair * count + j]
            rows = piece.shape[0]
            start = pl.multiple_of(scal[j], 16)
            copies.append(
                pltpu.make_async_copy(
                    piece.at[:, columns],
                    dest.at[slot, pl.ds(start, rows), :],
                    sems.at[pair * count + j],
                )
            )
    return copies


def start_all(copies):
    for c in copies:
        c.start()


def wait_all(copies):
    for c in copies:
        c.wait()


def ln_parts(x):
    centred = x - jnp.mean(x, -1, keepdims=True)
    inv = lax.rsqrt(jnp.mean(centred * centred, -1, keepdims=True) + EPSILON)
    return centred * inv, inv


def ln_back(x, gain, dn):
    hat, inv = ln_parts(x)
    dhat = dn * gain
    dx = inv * (
        dhat
        - jnp.mean(dhat, -1, keepdims=True)
        - hat * jnp.mean(dhat * hat, -1, keepdims=True)
    )
    return dx, jnp.sum(dn * hat, 0, keepdims=True), jnp.sum(dn, 0, keepdims=True)


def split3(v):
    a = v.astype(bf16)
    r = v - a.astype(f32)
    b = r.astype(bf16)
    c = (r - b.astype(f32)).astype(bf16)
    return a, b, c


def beside(wide, column):
    a, b, c = split3(column)
    rows, size = wide.shape[0], wide.shape[1]
    return jnp.concatenate([wide, a, b, c, jnp.zeros((rows, WIDE - size - 3), bf16)], 1)


class Sizes:
    def __init__(self, mesh, frames, w_qkv, w_up):
        self.shards = mesh.shape["shard"]
        self.layers = w_qkv.shape[0]
        self.width = frames.shape[-1]
        self.rows = frames.shape[1] // 2
        self.heads = w_qkv.shape[2]
        self.hd = w_qkv.shape[3] // 3
        self.att = self.heads * self.hd
        self.hidden = w_up.shape[2]
        self.m = w_qkv.shape[1]
        self.a_cols = 4 * self.att
        self.b_cols = 2 * self.hidden


def make(z):
    R, D, A, H, HD, F = z.rows, z.width, z.att, z.heads, z.hd, z.hidden
    coef = HD ** (-0.5) / math.log(2.0)
    scale = HD ** (-0.5)
    dma = pltpu.SemaphoreType.DMA

    def proj(scal, x, vec, qb, pieces, first, prev=None):
        n = len(pieces)
        cols = pl.ds(0, z.a_cols)

        def kernel(*refs):
            it = iter(refs)
            scal_r, x_r, vec_r, qb_r = (next(it) for _ in range(4))
            extra = [] if first else [next(it) for _ in range(3)]
            piece_r = [next(it) for _ in range(n)]
            x_o = None if first else next(it)
            n_o, q0, q1, kv0, kv1, w_s, sems = (next(it) for _ in range(7))
            copies = weight_copies(scal_r, piece_r, cols, w_s, sems, True)
            start_all(copies)
            xv = x_r[...].astype(f32)
            if not first:
                xv = xv + (extra[0][...].astype(f32) + extra[1][...].astype(f32) + extra[2][5:6, :])
                x_o[...] = xv
            hat, _ = ln_parts(xv)
            nv = (hat * vec_r[0:1, :] + vec_r[2:3, :]).astype(bf16)
            n_o[...] = nv
            wait_all(copies)
            for e, (q_o, kv_o) in enumerate(((q0, kv0), (q1, kv1))):
                p = (mm(nv, w_s[e, :, : 3 * A]) + qb_r[e : e + 1, :]).astype(bf16)
                q_o[...] = p[:, :A]
                kv_o[...] = p[:, A:]

        ins = [x, vec, qb] + ([] if first else list(prev))
        outs = ([] if first else [((R, D), f32)]) + [((R, D), bf16)]
        outs += [((R, A), bf16)] * 2 + [((R, 2 * A), bf16)] * 2
        return run(
            kernel,
            ins,
            outs,
            [pltpu.VMEM((2, D, z.a_cols), bf16), dma((n,))],
            pieces,
            scal,
            4 * R * D * 3 * A,
            "project",
        )

    def aug(block, offset, fill):
        return jnp.concatenate([block[:, offset : offset + HD], fill], 1)

    def attend(q, kvs, last=False, scal=None, o_prev=None, pieces=()):
        K = 4 * R
        n = len(pieces)

        def kernel(*refs):
            it = iter(refs)
            if last:
                scal_r = next(it)
            q_r = next(it)
            kv_r = [next(it) for _ in range(4)]
            if last:
                op_r = next(it)
                piece_r = [next(it) for _ in range(n)]
            o_o, qa_o = next(it), next(it)
            if last:
                own_o, snd_o, part_o = (next(it) for _ in range(3))
            q_s, k_s, v_s, o_s = (next(it) for _ in range(4))
            if last:
                w_s, sems = next(it), next(it)
                copies = weight_copies(scal_r, piece_r, pl.ds(z.a_cols - 256, 256), w_s, sems, True)
                start_all(copies)
            ones = jnp.ones((R, HD), bf16)
            zeros = jnp.zeros((R, HD), bf16)
            for h in range(H):
                q_s[h] = aug(q_r[...], h * HD, zeros)
                for b in range(4):
                    blk = kv_r[b][...]
                    k_s[h, b * R : (b + 1) * R, :] = aug(blk, h * HD, ones)
                    v_s[h, b * R : (b + 1) * R, :] = aug(blk, A + h * HD, ones)

            def head(h, carry):
                s = mm(q_s[h], k_s[h], NT)
                top = jnp.max(s, -1, keepdims=True)
                p = jnp.exp2((s - top) * coef).astype(bf16)
                oe = mm(p, v_s[h])
                total = oe[:, HD : HD + 1]
                o_s[h] = (oe[:, :HD] / total).astype(bf16)
                lse = top + jnp.log2(total) * (1.0 / coef)
                qa_o[h] = beside(q_s[h][:, :HD], -lse)
                return carry

            lax.fori_loop(0, H, head, 0)
            o_new = jnp.concatenate([o_s[h] for h in range(H)], 1)
            o_o[...] = o_new
            if last:
                o_old = op_r[...]
                odd = scal_r[8] == 1
                own_o[...] = jnp.where(odd, o_new, o_old)
                snd_o[...] = jnp.where(odd, o_old, o_new)
                wait_all(copies)
                part = mm(o_old, w_s[0, :, 256 - A :], NT) + mm(o_new, w_s[1, :, 256 - A :], NT)
                part_o[...] = part.astype(bf16)

        ins = [q] + list(kvs) + ([o_prev] if last else [])
        outs = [((R, A), bf16), ((H, R, WIDE), bf16)]
        scratch = [
            pltpu.VMEM((H, R, WIDE), bf16),
            pltpu.VMEM((H, K, WIDE), bf16),
            pltpu.VMEM((H, K, WIDE), bf16),
            pltpu.VMEM((H, R, HD), bf16),
        ]
        if last:
            outs += [((R, A), bf16)] * 2 + [((R, D), bf16)]
            scratch += [pltpu.VMEM((2, D, 256), bf16), dma((n,))]
        return run(kernel, ins, outs, scratch, pieces, scal, 4 * H * R * K * 128, "attend")

    def feed(scal, x, pa, pb, vec, upb, pieces, cols):
        n = len(pieces)

        def kernel(scal_r, x_r, pa_r, pb_r, vec_r, upb_r, *refs):
            piece_r = refs[:n]
            y_o, swap_o, hid_o, gp_o, part_o, w_s, sems = refs[n:]
            copies = weight_copies(scal_r, piece_r, cols, w_s, sems, False)
            start_all(copies)
            y = x_r[...] + (pa_r[...].astype(f32) + pb_r[...].astype(f32) + vec_r[3:4, :])
            y_o[...] = y
            hat, _ = ln_parts(y)
            nv = (hat * vec_r[1:2, :] + vec_r[4:5, :]).astype(bf16)
            swap_o[:, :D] = nv
            wait_all(copies)
            part = None
            for s in range(2):
                u = mm(nv, w_s[s, :, :F]) + upb_r[s : s + 1, :]
                cdf = 0.5 * (1.0 + lax.erf(u * (0.5**0.5)))
                pdf = jnp.exp(-0.5 * u * u) * (1.0 / math.sqrt(2.0 * math.pi))
                hidden = (u * cdf).astype(bf16)
                gp_o[s] = (cdf + u * pdf).astype(bf16)
                if s == 0:
                    hid_o[...] = hidden
                else:
                    swap_o[:, D:] = hidden
                t = mm(hidden, w_s[s, :, F:], NT)
                part = t if part is None else part + t
            part_o[...] = part.astype(bf16)

        outs = [
            ((R, D), f32),
            ((R, D + F), bf16),
            ((R, F), bf16),
            ((2, R, F), bf16),
            ((R, D), bf16),
        ]
        return run(
            kernel,
            [x, pa, pb, vec, upb],
            outs,
            [pltpu.VMEM((2, D, 2 * F), bf16), dma((n,))],
            pieces,
            scal,
            8 * R * D * F,
            "feed",
        )

    def finish(y, pa, pb, vec):
        def kernel(y_r, pa_r, pb_r, vec_r, o):
            v = y_r[...] + (pa_r[...].astype(f32) + pb_r[...].astype(f32) + vec_r[5:6, :])
            o[...] = v.astype(bf16)

        return run(kernel, [y, pa, pb, vec], [((R, D), bf16)], name="finish")[0]

    def feed_back(scal, grad, gp, pieces, cols, before=None):
        n = len(pieces)

        def kernel(*refs):
            it = iter(refs)
            scal_r = next(it)
            if before is None:
                g_r = next(it)
            else:
                x_r, dy_r, pa_r, pb_r, vec_r = (next(it) for _ in range(5))
            gp_r = next(it)
            piece_r = [next(it) for _ in range(n)]
            swap_o, du_o, part_o, sums_o = (next(it) for _ in range(4))
            if before is not None:
                g_o, pre_o = next(it), next(it)
            w_s, sems = next(it), next(it)
            copies = weight_copies(scal_r, piece_r, cols, w_s, sems, False)
            start_all(copies)
            if before is None:
                g = g_r[...].astype(f32)
            else:
                dn = pa_r[...].astype(f32) + pb_r[...].astype(f32)
                dx, dgain, dshift = ln_back(x_r[...], vec_r[0:1, :], dn)
                g = dy_r[...] + dx
                g_o[...] = g
                pre_o[0:1, :] = dgain
                pre_o[1:2, :] = dshift
            g2 = g.astype(bf16)
            swap_o[:, :D] = g2
            sums_o[...] = jnp.sum(g2.astype(f32), 0, keepdims=True)
            wait_all(copies)
            part = None
            for s in range(2):
                dh = mm(g2, w_s[s, :, F:])
                du = (gp_r[s].astype(f32) * dh).astype(bf16)
                if s == 0:
                    du_o[...] = du
                else:
                    swap_o[:, D:] = du
                t = mm(du, w_s[s, :, :F], NT)
                part = t if part is None else part + t
            part_o[...] = part.astype(bf16)

        ins = ([grad] if before is None else list(before)) + [gp]
        outs = [((R, D + F), bf16), ((R, F), bf16), ((R, D), bf16), ((1, D), f32)]
        if before is not None:
            outs += [((R, D), f32), ((2, D), f32)]
        return run(
            kernel,
            ins,
            outs,
            [pltpu.VMEM((2, D, 2 * F), bf16), dma((n,))],
            pieces,
            scal,
            8 * R * D * F,
            "feed_back",
        )

    def feed_grads(swap_f, recv_f, hid, swap_b, recv_b, du):
        def kernel(sf, rf, h_r, sb, rb, du_r, g_o, b_o):
            g_o[:, :F] = (mm(sf[:, :D], du_r[...], TN) + mm(rf[:, :D], rb[:, D:], TN)).astype(bf16)
            g_o[:, F:] = (mm(sb[:, :D], h_r[...], TN) + mm(rb[:, :D], rf[:, D:], TN)).astype(bf16)
            b_o[...] = jnp.sum(du_r[...].astype(f32), 0, keepdims=True) + jnp.sum(
                rb[:, D:].astype(f32), 0, keepdims=True
            )

        return run(
            kernel,
            [swap_f, recv_f, hid, swap_b, recv_b, du],
            [((D, 2 * F), bf16), ((1, F), f32)],
            flops=8 * R * D * F,
            name="feed_grads",
        )

    def middle_back(scal, y, g, pa, pb, vec, o0, o1, pieces):
        n = len(pieces)

        def kernel(scal_r, y_r, g_r, pa_r, pb_r, vec_r, o0_r, o1_r, *refs):
            piece_r = refs[:n]
            dy_o, g1_o, d0_o, d1_o, sums_o, w_s, sems = refs[n:]
            copies = weight_copies(scal_r, piece_r, pl.ds(z.a_cols - 256, 256), w_s, sems, True)
            start_all(copies)
            dn = pa_r[...].astype(f32) + pb_r[...].astype(f32)
            dx, dgain, dshift = ln_back(y_r[...], vec_r[1:2, :], dn)
            dy = g_r[...].astype(f32) + dx
            dy_o[...] = dy
            g1 = dy.astype(bf16)
            g1_o[...] = g1
            sums_o[0:1, :] = dgain
            sums_o[1:2, :] = jnp.sum(g1.astype(f32), 0, keepdims=True)
            sums_o[2:3, :] = dshift
            wait_all(copies)
            for e, (o_r, d_o) in enumerate(((o0_r, d0_o), (o1_r, d1_o))):
                do = mm(g1, w_s[e, :, 256 - A :]).astype(bf16)
                prod = do.astype(f32) * o_r[...].astype(f32)
                for h in range(H):
                    lanes = slice(h * HD, (h + 1) * HD)
                    d_o[h] = beside(do[:, lanes], -jnp.sum(prod[:, lanes], -1, keepdims=True))

        outs = [((R, D), f32), ((R, D), bf16)] + [((H, R, WIDE), bf16)] * 2 + [((3, D), f32)]
        return run(
            kernel,
            [y, g, pa, pb, vec, o0, o1],
            outs,
            [pltpu.VMEM((2, D, 256), bf16), dma((n,))],
            pieces,
            scal,
            4 * R * D * A,
            "middle_back",
        )

    def attend_back(qa, kvs, da):
        K = 4 * R

        def kernel(qa_r, k0, k1, k2, k3, da_r, dq_o, e0, e1, e2, e3, k_s, v_s, dk_s, dv_s, dq_s):
            ones = jnp.ones((R, HD), bf16)
            for h in range(H):
                for b, kv_r in enumerate((k0, k1, k2, k3)):
                    blk = kv_r[...]
                    k_s[h, b * R : (b + 1) * R, :] = aug(blk, h * HD, ones)
                    v_s[h, b * R : (b + 1) * R, :] = aug(blk, A + h * HD, ones)

            def head(h, carry):
                qv = qa_r[h]
                dv_in = da_r[h]
                dqt = jnp.zeros((WIDE, R), f32)
                for b in range(4):
                    at = slice(b * R, (b + 1) * R)
                    kb = k_s[h, at, :]
                    p = jnp.exp2(mm(kb, qv, NT) * coef)
                    ds = (p * mm(v_s[h, at, :], dv_in, NT)).astype(bf16)
                    dv_s[h, at, :] = mm(p.astype(bf16), dv_in).astype(bf16)
                    dk_s[h, at, :] = (mm(ds, qv) * scale).astype(bf16)
                    dqt = dqt + mm(kb, ds, TN)
                dq_s[h] = (dqt.T * scale).astype(bf16)
                return carry

            lax.fori_loop(0, H, head, 0)
            dq_o[...] = jnp.concatenate([dq_s[h][:, :HD] for h in range(H)], 1)
            for b, e_o in enumerate((e0, e1, e2, e3)):
                at = slice(b * R, (b + 1) * R)
                e_o[...] = jnp.concatenate(
                    [dk_s[h, at, :HD] for h in range(H)] + [dv_s[h, at, :HD] for h in range(H)], 1
                )

        return run(
            kernel,
            [qa] + list(kvs) + [da],
            [((R, A), bf16)] + [((R, 2 * A), bf16)] * 4,
            [pltpu.VMEM((H, K, WIDE), bf16)] * 4 + [pltpu.VMEM((H, R, WIDE), bf16)],
            flops=10 * H * R * K * 128,
            name="attend_back",
        )

    def pair_sum(parts, count):
        flat = [a for group in parts for a in group]

        def kernel(*refs):
            ins, outs = refs[: len(flat)], refs[len(flat) :]
            at = 0
            for o, group in zip(outs, parts):
                total = ins[at][...].astype(f32)
                for k in range(1, len(group)):
                    total = total + ins[at + k][...].astype(f32)
                at += len(group)
                o[...] = total.astype(bf16)

        return run(kernel, flat, [(g[0].shape, bf16) for g in parts], name="pair_sum")

    def proj_back(scal, dqs, kv_parts, pieces):
        n = len(pieces)

        def kernel(scal_r, q0, q1, *refs):
            kvp = (refs[:3], refs[3:6])
            piece_r = refs[6 : 6 + n]
            own_o, snd_o, part_o, w_s, sems = refs[6 + n :]
            copies = weight_copies(scal_r, piece_r, pl.ds(0, z.a_cols), w_s, sems, True)
            start_all(copies)
            both = []
            for e, q_r in enumerate((q0, q1)):
                a, b, c = (r[...].astype(f32) for r in kvp[e])
                both.append(jnp.concatenate([q_r[...], (a + b + c).astype(bf16)], 1))
            odd = scal_r[8] == 1
            own_o[...] = jnp.where(odd, both[1], both[0])
            snd_o[...] = jnp.where(odd, both[0], both[1])
            wait_all(copies)
            part = mm(both[0], w_s[0, :, : 3 * A], NT) + mm(both[1], w_s[1, :, : 3 * A], NT)
            part_o[...] = part.astype(bf16)

        ins = list(dqs) + list(kv_parts[0]) + list(kv_parts[1])
        outs = [((R, 3 * A), bf16)] * 2 + [((R, D), bf16)]
        return run(
            kernel,
            ins,
            outs,
            [pltpu.VMEM((2, D, z.a_cols), bf16), dma((n,))],
            pieces,
            scal,
            4 * R * D * 3 * A,
            "project_back",
        )

    def proj_grads(n1, n1_r, dp, dp_r, g1, g1_r, o, o_r):
        def kernel(n_r, nr_r, p_r, pr_r, g_r, gr_r, o_i, or_i, g_o, b_o):
            first = mm(n_r[...], p_r[...], TN) + mm(nr_r[...], pr_r[...], TN)
            second = mm(g_r[...], o_i[...], TN) + mm(gr_r[...], or_i[...], TN)
            g_o[...] = jnp.concatenate([first.astype(bf16), second.astype(bf16)], 1)
            b_o[...] = jnp.sum(p_r[...].astype(f32), 0, keepdims=True) + jnp.sum(
                pr_r[...].astype(f32), 0, keepdims=True
            )

        return run(
            kernel,
            [n1, n1_r, dp, dp_r, g1, g1_r, o, o_r],
            [((D, z.a_cols), bf16), ((1, 3 * A), f32)],
            flops=4 * R * D * 4 * A,
            name="project_grads",
        )

    def input_back(x, dy, pa, pb, vec):
        def kernel(x_r, dy_r, pa_r, pb_r, vec_r, o, sums_o):
            dn = pa_r[...].astype(f32) + pb_r[...].astype(f32)
            dx, dgain, dshift = ln_back(x_r[...].astype(f32), vec_r[0:1, :], dn)
            o[...] = (dy_r[...] + dx).astype(bf16)
            sums_o[0:1, :] = dgain
            sums_o[1:2, :] = dshift

        return run(kernel, [x, dy, pa, pb, vec], [((R, D), bf16), ((2, D), f32)], name="input_back")

    return dict(locals())


def local(mesh):
    def fn(frames, cotangent, w_qkv, qv_bias, w_out, w_up, up_bias, w_down, norm_gains, shifts):
        z = Sizes(mesh, frames, w_qkv, w_up)
        assert mesh.shape["tp"] == 4 and mesh.shape["ctx"] == 2 and frames.shape[0] == 1
        k = make(z)
        L, m, R, D, A, F, H, HD, S = z.layers, z.m, z.rows, z.width, z.att, z.hidden, z.heads, z.hd, z.shards
        parity = lax.axis_index("tp") % 2
        odd = parity == 1

        qkv = w_qkv.reshape(L, m, H, 3, HD).transpose(0, 1, 3, 2, 4).reshape(L, m, 3 * A)
        own_a = jnp.concatenate([qkv, w_out.reshape(L, A, m).transpose(0, 2, 1)], -1)
        own_b = jnp.concatenate([w_up, w_down.transpose(0, 2, 1)], -1)
        offsets = piece_offsets(m, S)
        scal = jnp.stack(offsets + [jnp.int32(0)] * (8 - len(offsets)) + [parity.astype(jnp.int32)])

        def both_cores(x):
            mine = gather_rows(x, S)
            return mine + [core_swap(p) for p in mine]

        pieces_a, pieces_b, cols_b = [None] * L, [None] * L, [None] * L
        pieces_a[0] = both_cores(own_a[0])
        small = jnp.concatenate(
            [qv_bias.reshape(-1), up_bias.reshape(-1), norm_gains.reshape(-1), shifts.reshape(-1)]
        )
        small = lax.all_gather(small, "shard").astype(f32)
        cuts = [qv_bias.size, up_bias.size, norm_gains.size, shifts.size]
        cuts = [sum(cuts[: i + 1]) for i in range(4)]
        qvb = small[:, : cuts[0]].reshape(S, L, H, 2 * HD // S).transpose(1, 2, 0, 3).reshape(L, H, 2, HD)
        qvb = qvb.transpose(0, 2, 1, 3).reshape(L, 2, A)
        qb = jnp.concatenate([qvb[:, 0], jnp.zeros((L, A), f32), qvb[:, 1]], -1)
        upb = small[:, cuts[0] : cuts[1]].reshape(S, L, F // 64, 64 // S).transpose(1, 2, 0, 3).reshape(L, F)
        biases = jnp.concatenate([qb, upb], -1)
        other = core_swap(biases)
        qb_pair = jnp.stack([biases[:, : 3 * A], other[:, : 3 * A]], 1)
        qb_pair = jnp.where(odd, qb_pair[:, ::-1], qb_pair)
        upb_pair = jnp.stack([biases[:, 3 * A :], other[:, 3 * A :]], 1)
        gains = small[:, cuts[1] : cuts[2]].reshape(S, L, 2, m).transpose(1, 2, 0, 3).reshape(L, 2, D)
        offs = small[:, cuts[2] :].reshape(S, L, 4, m).transpose(1, 2, 0, 3).reshape(L, 4, D)
        vecs = jnp.concatenate([gains, offs, jnp.zeros((L, 2, D), f32)], 1)

        pieces_b[0] = both_cores(own_b[0])
        cols_b[0] = pl.ds(0, 2 * F)
        for layer in range(1, L):
            pieces_a[layer] = both_cores(jnp.concatenate([own_a[layer], own_b[layer]], -1))
            pieces_b[layer] = pieces_a[layer]
            cols_b[layer] = pl.ds(z.a_cols, 2 * F)

        def my_rows(x):
            return lax.dynamic_slice_in_dim(x.reshape(2 * R, D), parity * R, R, 0)

        stream = my_rows(frames)
        kept = []
        part = None
        for layer in range(L):
            vec = vecs[layer]
            if layer == 0:
                x = stream
                n1, q0, q1, kv0, kv1 = k["proj"](scal, x, vec, qb_pair[0], pieces_a[0], True)
            else:
                x, n1, q0, q1, kv0, kv1 = k["proj"](
                    scal, y, vec, qb_pair[layer], pieces_a[layer], False, (part, x_swap(part), vecs[layer - 1])
                )
            kvs = []
            for kv in (kv0, kv1):
                far = y_swap(kv)
                kvs.append((kv, core_swap(kv), far, core_swap(far)))
            o0, qa0 = k["attend"](q0, kvs[0])
            o1, qa1, o_own, o_snd, att_part = k["attend"](q1, kvs[1], True, scal, o0, pieces_a[layer])
            y, swap_f, hid, gp, part = k["feed"](
                scal, x, att_part, x_swap(att_part), vec, upb_pair[layer], pieces_b[layer], cols_b[layer]
            )
            kept.append((x, n1, kvs, (qa0, qa1), (o0, o1), o_own, o_snd, y, swap_f, hid, gp))
        out_rows = k["finish"](y, part, x_swap(part), vecs[L - 1])

        def whole_rows(mine):
            theirs = core_swap(mine)
            return jnp.where(
                odd, jnp.concatenate([theirs, mine], 0), jnp.concatenate([mine, theirs], 0)
            )[None]

        out_frames = whole_rows(out_rows)

        grads_a, grads_b, rows_small, cols_small = [None] * L, [None] * L, [None] * L, [None] * L
        before = None
        g = my_rows(cotangent)
        pre = None
        for layer in reversed(range(L)):
            vec = vecs[layer]
            x, n1, kvs, qas, os, o_own, o_snd, y, swap_f, hid, gp = kept[layer]
            if before is None:
                swap_b, du, part, sum_g2 = k["feed_back"](scal, g, gp, pieces_b[layer], cols_b[layer])
            else:
                swap_b, du, part, sum_g2, g, pre = k["feed_back"](
                    scal, None, gp, pieces_b[layer], cols_b[layer], before
                )
                rows_small[layer + 1] = (pre,) + rows_small[layer + 1]
            far = x_swap(part)
            grad_b, d_upb = k["feed_grads"](swap_f, core_swap(swap_f), hid, swap_b, core_swap(swap_b), du)
            grads_b[layer] = grad_b
            dy, g1, d0, d1, mid = k["middle_back"](
                scal, y, g, part, far, vec, os[0], os[1], pieces_a[layer]
            )
            dqs, kv_parts = [], []
            for e in range(2):
                dq, own, near, y_own, y_near = k["attend_back"](qas[e], kvs[e], (d0, d1)[e])
                pair = core_swap(jnp.stack([near, y_near]))
                cross = k["pair_sum"]([[y_own, pair[1]]], 1)[0]
                dqs.append(dq)
                kv_parts.append((own, pair[0], y_swap(cross)))
            dp, dp_snd, part = k["proj_back"](scal, dqs, kv_parts, pieces_a[layer])
            far = x_swap(part)
            grad_a, d_qvb = k["proj_grads"](
                n1, core_swap(n1), dp, core_swap(dp_snd), g1, core_swap(g1), o_own, core_swap(o_snd)
            )
            grads_a[layer] = grad_a
            before = (x, dy, part, far, vec)
            rows_small[layer] = (mid, sum_g2)
            cols_small[layer] = (d_qvb, d_upb)
        grad_rows, pre = k["input_back"](*before)
        rows_small[0] = (pre,) + rows_small[0]
        frames_grad = whole_rows(grad_rows)

        def reduce(grad):
            mine = lax.psum_scatter(grad, "shard", scatter_dimension=0, tiled=True)
            return mine.astype(f32) + y_swap(mine).astype(f32)

        outs_qkv, outs_out, outs_up, outs_down = [], [], [], []
        for layer in range(L):
            ga, gb = reduce(grads_a[layer]), reduce(grads_b[layer])
            outs_qkv.append(ga[:, : 3 * A].reshape(m, 3, H, HD).transpose(0, 2, 1, 3).reshape(m, H, 3 * HD))
            outs_out.append(ga[:, 3 * A :].T.reshape(H, HD, m))
            outs_up.append(gb[:, :F])
            outs_down.append(gb[:, F:].T)

        wide = []
        for layer in range(L):
            pre, mid, sum_g2 = rows_small[layer]
            wide.append(jnp.concatenate([pre[0:1], mid[0:1], pre[1:2], mid[1:3], sum_g2], 0))
        wide = jnp.stack(wide)
        wide = wide + core_swap(wide)
        qvs = jnp.stack([jnp.concatenate([c[0][0, :A], c[0][0, 2 * A :]]) for c in cols_small])
        ups = jnp.stack([c[1][0] for c in cols_small])
        wide = wide.reshape(L, 6, S, m).transpose(2, 0, 1, 3).reshape(S, -1)
        qvs = qvs.reshape(L, 2, H, HD).transpose(0, 2, 1, 3).reshape(L, H, S, 2 * HD // S)
        qvs = qvs.transpose(2, 0, 1, 3).reshape(S, -1)
        ups = ups.reshape(L, F // 64, S, 64 // S).transpose(2, 0, 1, 3).reshape(S, -1)
        tiny = jnp.concatenate([wide, qvs, ups], 1)
        tiny = lax.psum(tiny, ("shard", "ctx"))
        tiny = lax.dynamic_index_in_dim(tiny, lax.axis_index("shard"), 0, keepdims=False)
        n_wide, n_qv = L * 6 * m, L * H * 2 * HD // S
        wide = tiny[:n_wide].reshape(L, 6, m)
        g_qvb = tiny[n_wide : n_wide + n_qv].reshape(L, H, 2 * HD // S)
        g_upb = tiny[n_wide + n_qv :].reshape(L, F // 64, 64 // S)
        return (
            out_frames,
            frames_grad,
            jnp.stack(outs_qkv),
            g_qvb,
            jnp.stack(outs_out),
            jnp.stack(outs_up),
            g_upb,
            jnp.stack(outs_down),
            wide[:, :2],
            wide[:, 2:],
        )

    return fn


def solution(mesh):
    specs = (
        P("shard", "ctx", None),
        P("shard", "ctx", None),
        P(None, "shard", "tp", None),
        P(None, "tp", "shard"),
        P(None, "tp", None, "shard"),
        P(None, "shard", "tp"),
        P(None, "tp", "shard"),
        P(None, "tp", "shard"),
        P(None, None, "shard"),
        P(None, None, "shard"),
    )
    return jax.shard_map(local(mesh), mesh=mesh, in_specs=specs, out_specs=specs, check_vma=False)
```

```python
import math

import jax
import jax.numpy as jnp
from jax import lax
from jax.experimental import pallas as pl
from jax.experimental.pallas import tpu as pltpu
from jax.sharding import Mesh
from jax.sharding import PartitionSpec as P

f32 = jnp.float32
bf16 = jnp.bfloat16
EPSILON = 1e-05
NN = (((1,), (0,)), ((), ()))
NT = (((1,), (1,)), ((), ()))
TN = (((0,), (0,)), ((), ()))
VMEM_MIB = {
    "attend": 10,
    "attend_back": 8.5,
    "feed": 13,
    "feed_back": 12,
    "feed_grads": 9,
    "feed_out": 5,
    "input_back": 7,
    "middle_back": 7,
    "pair_grads": 5,
    "project": 6,
    "project_back": 8.5,
    "project_grads": 5,
    "project_out": 4.5,
}
WIDE = 128
TAIL = 16
COST = 500_000_000


def mm(a, b, dims=NN):
    return lax.dot_general(a, b, dims, preferred_element_type=f32)


def core_swap(x):
    return lax.ppermute(x, "tc", [(0, 1), (1, 0)])


def x_swap(x):
    return lax.ppermute(x, "tx", [(0, 1), (1, 0)])


def y_swap(x):
    return lax.ppermute(x, "ctx", [(0, 1), (1, 0)])


def after(x, *others):
    return lax.optimization_barrier((x,) + others)[0]


def ring(shift):
    return [(i, (i + shift) % 4) for i in range(4)]


def ring_scalars(shards):
    me = lax.axis_index("shard").astype(jnp.int32)
    zero = jnp.int32(0)
    order = [me, (me + shards - 1) % shards, (me + 1) % shards, (me + 2) % shards]
    return jnp.stack([zero] * 8 + [lax.axis_index("tc").astype(jnp.int32)] + order + [zero] * 3)


class Pieces:
    def __init__(self, x, tail=0):
        self.rows = x.shape[0] - tail
        self.mine = [x] + [lax.ppermute(x, "shard", ring(s)) for s in (1, 3, 2)]
        self.arrays = self.mine + [core_swap(p) for p in self.mine]

    def copies(self, scal, refs, columns, dest, sems):
        out = []
        for k, ref in enumerate(refs):
            slot = scal[8] if k < 4 else 1 - scal[8]
            to = dest.at[slot, scal[9 + k % 4]]
            out.append(pltpu.make_async_copy(ref.at[pl.ds(0, self.rows), columns], to, sems.at[k]))
        return out

    def tails(self, scal, refs, dest, sems):
        out = []
        for k, ref in enumerate(refs):
            slot = scal[8] if k < 4 else 1 - scal[8]
            to = dest.at[slot, scal[9 + k % 4]]
            out.append(pltpu.make_async_copy(ref.at[pl.ds(self.rows, TAIL), :], to, sems.at[k]))
        return out


class Gathered:
    def __init__(self, x, shards, tail=0):
        self.rows = x.shape[0] - tail
        whole = lax.all_gather(x, ("shard", "tc"), axis=0, tiled=False)
        self.arrays = [whole.reshape((shards, 2) + x.shape)]

    def copies(self, scal, refs, columns, dest, sems):
        ref = refs[0]
        return [
            pltpu.make_async_copy(ref.at[:, c, pl.ds(0, self.rows), columns], dest.at[c], sems.at[c])
            for c in range(2)
        ]

    def tails(self, scal, refs, dest, sems):
        ref = refs[0]
        return [
            pltpu.make_async_copy(ref.at[:, c, pl.ds(self.rows, TAIL), :], dest.at[c], sems.at[c])
            for c in range(2)
        ]


def vmem():
    return pl.BlockSpec(memory_space=pltpu.VMEM)


class Far:
    def __init__(self, array):
        self.array = array


class Reading:
    def __init__(self, buffer, copy):
        self.buffer, self.copy, self.waited = buffer, copy, False

    def need(self):
        if not self.waited:
            self.copy.wait()
            self.waited = True
        return self.buffer

    def __getitem__(self, index):
        return self.need()[index]

    @property
    def shape(self):
        return self.buffer.shape


class Writing:
    def __init__(self, buffer, copy):
        self.buffer, self.copy, self.sent = buffer, copy, False

    def __setitem__(self, index, value):
        self.buffer[index] = value

    @property
    def at(self):
        return self.buffer.at

    def send(self):
        if not self.sent:
            self.copy.start()
            self.sent = True


def send(*refs):
    for r in refs:
        if isinstance(r, Writing):
            r.send()


def need(*refs):
    for r in refs:
        if isinstance(r, Reading):
            r.need()


FAR = "far"


def run(kernel, ins, outs, scratch=(), w=None, scalars=None, name=None, us=1.0):
    pieces = [] if w is None else w.arrays
    n_in, n_out, n_pieces = len(ins), len(outs), len(pieces)
    far_in = [i for i, a in enumerate(ins) if isinstance(a, Far)]
    far_out = [i for i, o in enumerate(outs) if len(o) == 3]
    any_space = pl.BlockSpec(memory_space=pl.ANY)
    specs, args = [], []
    if scalars is not None:
        specs.append(pl.BlockSpec(memory_space=pltpu.SMEM))
        args.append(scalars)
    for a in ins:
        if isinstance(a, Far):
            specs.append(any_space)
            args.append(pltpu.with_memory_space_constraint(a.array, pltpu.HBM))
        else:
            specs.append(vmem())
            args.append(a)
    for p in pieces:
        specs.append(any_space)
        args.append(pltpu.with_memory_space_constraint(p, pltpu.HBM))
    first = len(args) - n_in - n_pieces
    shapes = [
        pltpu.HBM(o[0], o[1]) if len(o) == 3 else jax.ShapeDtypeStruct(o[0], o[1]) for o in outs
    ]
    buffers = [pltpu.VMEM(ins[i].array.shape, ins[i].array.dtype) for i in far_in]
    buffers += [pltpu.VMEM(outs[i][0], outs[i][1]) for i in far_out]
    sems = [pltpu.SemaphoreType.DMA((len(buffers),))] if buffers else []

    def wrapped(*refs):
        refs = list(refs)
        n_all = len(args) + n_out + len(scratch)
        own, extra = refs[:n_all], refs[n_all:]
        reads, writes = [], []
        for k, i in enumerate(far_in):
            copy = pltpu.make_async_copy(own[first + i], extra[k], extra[-1].at[k])
            copy.start()
            own[first + i] = Reading(extra[k], copy)
            reads.append(own[first + i])
        for k, i in enumerate(far_out):
            k += len(far_in)
            at = len(args) + i
            own[at] = Writing(extra[k], pltpu.make_async_copy(extra[k], own[at], extra[-1].at[k]))
            writes.append(own[at])
        kernel(*own)
        for w in writes:
            w.send()
        for r in reads:
            r.need()
        for w in writes:
            w.copy.wait()

    return pl.pallas_call(
        wrapped,
        out_shape=shapes,
        in_specs=specs,
        out_specs=[any_space if len(o) == 3 else vmem() for o in outs],
        scratch_shapes=list(scratch) + buffers + sems,
        compiler_params=pltpu.CompilerParams(vmem_limit_bytes=int(VMEM_MIB.get(name, 4) * 1024 * 1024)),
        cost_estimate=pl.CostEstimate(flops=int(us * COST), bytes_accessed=1000, transcendentals=0),
        name=name,
    )(*args)


def spread(shard, shards, units):
    part = 64 // shards
    bits, low = part.bit_length() - 1, part - 1
    i = lax.broadcasted_iota(jnp.int32, (units // shards, units), 0)
    j = lax.broadcasted_iota(jnp.int32, (units // shards, units), 1)
    same = ((j >> 6) == (i >> bits)) & ((j & 63) == shard * part + (i & low))
    return jnp.where(same, 1.0, 0.0).astype(bf16)


def start_all(copies):
    for c in copies:
        c.start()


def wait_all(copies):
    for c in copies:
        c.wait()


def ln_parts(x):
    centred = x - jnp.mean(x, -1, keepdims=True)
    inv = lax.rsqrt(jnp.mean(centred * centred, -1, keepdims=True) + EPSILON)
    return centred * inv, inv


def ln_back(x, gain, dn):
    hat, inv = ln_parts(x)
    dhat = dn * gain
    dx = inv * (
        dhat
        - jnp.mean(dhat, -1, keepdims=True)
        - hat * jnp.mean(dhat * hat, -1, keepdims=True)
    )
    return dx, jnp.sum(dn * hat, 0, keepdims=True), jnp.sum(dn, 0, keepdims=True)


def split3(v):
    a = v.astype(bf16)
    r = v - a.astype(f32)
    b = r.astype(bf16)
    c = (r - b.astype(f32)).astype(bf16)
    return a, b, c


def beside(wide, column):
    a, b, c = split3(column)
    rows, size = wide.shape[0], wide.shape[1]
    return jnp.concatenate([wide, a, b, c, jnp.zeros((rows, WIDE - size - 3), bf16)], 1)


class Sizes:
    def __init__(self, mesh, frames, w_qkv, w_up):
        self.shards = mesh.shape["shard"]
        self.layers = w_qkv.shape[0]
        self.width = frames.shape[-1]
        self.rows = frames.shape[1] // 2
        self.heads = w_qkv.shape[2]
        self.hd = w_qkv.shape[3] // 3
        self.att = self.heads * self.hd
        self.hidden = w_up.shape[2]
        self.m = w_qkv.shape[1]
        self.a_cols = 4 * self.att
        self.b_cols = 2 * self.hidden


def make(z):
    R, D, A, H, HD, F = z.rows, z.width, z.att, z.heads, z.hd, z.hidden
    L, S, M = z.layers, z.shards, z.m
    coef = HD ** (-0.5) / math.log(2.0)
    scale = HD ** (-0.5)
    dma = pltpu.SemaphoreType.DMA
    q_at, u_at = M, M + 2 * A // S

    def weight_scratch(columns):
        return [pltpu.VMEM((2, S, M, columns), bf16), dma((8,))]

    def weight(w_s, c, start, stop):
        return w_s[c, :, :, start:stop].reshape(D, stop - start)

    def proj(scal, x, layer, w, biases=None, prev=None):
        first = biases is None
        n = len(w.arrays)
        part = 2 * HD // S

        def kernel(*refs):
            it = iter(refs)
            scal_r, x_r = next(it), next(it)
            if not first:
                vec_r, qb_r, pa_r, pb_r = (next(it) for _ in range(4))
            piece_r = [next(it) for _ in range(n)]
            n_o, q0, q1, kv0, kv1 = (next(it) for _ in range(5))
            if first:
                vec_r, qb_r, tail_o = (next(it) for _ in range(3))
            else:
                x_o = next(it)
            w_s, sems = next(it), next(it)
            if first:
                tail_sems = next(it)
                tails = w.tails(scal_r, piece_r, tail_o, tail_sems)
                start_all(tails)
            copies = w.copies(scal_r, piece_r, pl.ds(0, z.a_cols), w_s, sems)
            start_all(copies)
            xv = x_r[...].astype(f32)
            if not first:
                at = 6 * (layer - 1) + 5
                xv = xv + (pa_r[...].astype(f32) + pb_r[...].astype(f32) + vec_r[at : at + 1, :])
                x_o[...] = xv
            hat, _ = ln_parts(xv)
            if first:
                wait_all(tails)
                vec_r[...] = jnp.concatenate([tail_o[0, t][:, :M] for t in range(S)], 1).astype(f32)
                for l in range(L):
                    for p in range(2):
                        rows = [tail_o[p, t].astype(f32)[l : l + 1, q_at:u_at] for t in range(S)]
                        seq = []
                        for side in range(2):
                            for h in range(H):
                                seq += [
                                    rows[t][:, h * part : (h + 1) * part]
                                    for t in range(side * S // 2, (side + 1) * S // 2)
                                ]
                            if side == 0:
                                seq.append(jnp.zeros((1, A), f32))
                        qb_r[2 * l + p : 2 * l + p + 1, :] = jnp.concatenate(seq, 1)
            g = 6 * layer
            nv = (hat * vec_r[g : g + 1, :] + vec_r[g + 2 : g + 3, :]).astype(bf16)
            n_o[...] = nv
            send(n_o)
            wait_all(copies)
            for e, (q_o, kv_o) in enumerate(((q0, kv0), (q1, kv1))):
                b = 2 * layer + e
                p = (mm(nv, weight(w_s, e, 0, 3 * A)) + qb_r[b : b + 1, :]).astype(bf16)
                q_o[...] = p[:, :A]
                kv_o[...] = p[:, A:]
                send(kv_o)

        ins = [x] + ([] if first else list(biases) + list(prev))
        outs = [((R, D), bf16)] + [((R, A), bf16)] * 2 + [((R, 2 * A), bf16, FAR)] * 2
        scratch = weight_scratch(z.a_cols)
        if first:
            outs += [((TAIL, D), f32), ((2 * L, 3 * A), f32), ((2, S, TAIL, z.a_cols), bf16)]
            scratch += [dma((8,))]
        else:
            outs += [((R, D), f32)]
        return run(kernel, ins, outs, scratch, w, scal, "project", 3.5)

    def aug(block, offset, fill):
        return jnp.concatenate([block[:, offset : offset + HD], fill], 1)

    def attend(q, kvs, scal=None, o_prev=None, w=None):
        K = 4 * R
        last = w is not None
        n = len(w.arrays) if last else 0

        def kernel(*refs):
            it = iter(refs)
            if last:
                scal_r = next(it)
            q_r = next(it)
            kv_r = [next(it) for _ in range(4)]
            if last:
                op_r = next(it)
                piece_r = [next(it) for _ in range(n)]
            o_o, qa_o = next(it), next(it)
            if last:
                own_o, snd_o, part_o = (next(it) for _ in range(3))
            q_s, k_s, v_s, o_s = (next(it) for _ in range(4))
            if last:
                w_s, sems = next(it), next(it)
                copies = w.copies(scal_r, piece_r, pl.ds(z.a_cols - 256, 256), w_s, sems)
                start_all(copies)
            ones = jnp.ones((R, HD), bf16)
            zeros = jnp.zeros((R, HD), bf16)
            for h in range(H):
                q_s[h] = aug(q_r[...], h * HD, zeros)
                for b in range(4):
                    blk = kv_r[b][...]
                    k_s[h, b * R : (b + 1) * R, :] = aug(blk, h * HD, ones)
                    v_s[h, b * R : (b + 1) * R, :] = aug(blk, A + h * HD, ones)

            def head(h, carry):
                s = mm(q_s[h], k_s[h], NT)
                top = jnp.max(s, -1, keepdims=True)
                p = jnp.exp2((s - top) * coef).astype(bf16)
                oe = mm(p, v_s[h])
                total = oe[:, HD : HD + 1]
                o_s[h] = (oe[:, :HD] / total).astype(bf16)
                lse = top + jnp.log2(total) * (1.0 / coef)
                qa_o[h] = beside(q_s[h][:, :HD], -lse)
                return carry

            lax.fori_loop(0, H, head, 0)
            o_new = jnp.concatenate([o_s[h] for h in range(H)], 1)
            o_o[...] = o_new
            if last:
                o_old = op_r[...]
                odd = scal_r[8] == 1
                own_o[...] = jnp.where(odd, o_new, o_old)
                snd_o[...] = jnp.where(odd, o_old, o_new)
                send(snd_o)
                wait_all(copies)
                part = mm(o_old, weight(w_s, 0, 256 - A, 256), NT) + mm(o_new, weight(w_s, 1, 256 - A, 256), NT)
                part_o[...] = part.astype(bf16)

        ins = [q] + list(kvs) + ([o_prev] if last else [])
        outs = [((R, A), bf16), ((H, R, WIDE), bf16)]
        scratch = [
            pltpu.VMEM((H, R, WIDE), bf16),
            pltpu.VMEM((H, K, WIDE), bf16),
            pltpu.VMEM((H, K, WIDE), bf16),
            pltpu.VMEM((H, R, HD), bf16),
        ]
        if last:
            outs += [((R, A), bf16), ((R, A), bf16), ((R, D), bf16, FAR)]
            scratch += weight_scratch(256)
        return run(kernel, ins, outs, scratch, w, scal, "attend", 6)

    def feed(scal, x, pa, pb, vec, tails, layer, w):
        n = len(w.arrays)
        g = 6 * layer

        def kernel(scal_r, x_r, pa_r, pb_r, vec_r, tail_r, *refs):
            piece_r = refs[:n]
            y_o, n_o, *hid_gp, part_o, w_s, sems = refs[n:]
            copies = w.copies(scal_r, piece_r, pl.ds(0, 2 * F), w_s, sems)
            start_all(copies)
            y = x_r[...].astype(f32) + (
                pa_r[...].astype(f32) + pb_r[...].astype(f32) + vec_r[g + 3 : g + 4, :]
            )
            y_o[...] = y
            hat, _ = ln_parts(y)
            nv = (hat * vec_r[g + 1 : g + 2, :] + vec_r[g + 4 : g + 5, :]).astype(bf16)
            n_o[...] = nv
            send(n_o)
            bias = [None, None]
            for t in range(S):
                e = spread(t, S, F)
                for s in range(2):
                    add = mm(tail_r[s, t][:, u_at : u_at + F // S], e)
                    bias[s] = add if t == 0 else bias[s] + add
            part = None
            for s in range(2):
                copies[s].wait()
                u = mm(nv, weight(w_s, s, 0, F)) + bias[s][layer : layer + 1, :]
                cdf = 0.5 * (1.0 + lax.erf(u * (0.5**0.5)))
                pdf = jnp.exp(-0.5 * u * u) * (1.0 / math.sqrt(2.0 * math.pi))
                hidden = (u * cdf).astype(bf16)
                hid_gp[s][...] = hidden
                hid_gp[2 + s][...] = (cdf + u * pdf).astype(bf16)
                send(hid_gp[s], hid_gp[2 + s])
                t = mm(hidden, weight(w_s, s, F, 2 * F), NT)
                part = t if part is None else part + t
            part_o[...] = part.astype(bf16)

        outs = [
            ((R, D), f32),
            ((R, D), bf16, FAR),
            ((R, F), bf16, FAR),
            ((R, F), bf16, FAR),
            ((R, F), bf16, FAR),
            ((R, F), bf16, FAR),
            ((R, D), bf16, FAR),
        ]
        return run(
            kernel, [x, pa, pb, vec, tails], outs, weight_scratch(2 * F), w, scal, "feed", 6
        )

    def finish(y, pa, pb, vec):
        at = 6 * (L - 1) + 5

        def kernel(y_r, pa_r, pb_r, vec_r, o):
            v = y_r[...] + (pa_r[...].astype(f32) + pb_r[...].astype(f32) + vec_r[at : at + 1, :])
            o[...] = v.astype(bf16)

        return run(kernel, [y, pa, pb, vec], [((R, D), bf16, FAR)], name="finish")

    def feed_back(scal, grad, gp, layer, w, before=None):
        n = len(w.arrays)
        up = 6 * (layer + 1)

        def kernel(*refs):
            it = iter(refs)
            scal_r = next(it)
            if before is None:
                g_r = next(it)
            else:
                x_r, dy_r, pa_r, pb_r, vec_r = (next(it) for _ in range(5))
            gp_r = (next(it), next(it))
            piece_r = [next(it) for _ in range(n)]
            g2_o, du_o, part_o, sums_o = (next(it) for _ in range(4))
            if before is not None:
                g_o, pre_o = next(it), next(it)
            w_s, sems = next(it), next(it)
            copies = w.copies(scal_r, piece_r, pl.ds(0, 2 * F), w_s, sems)
            start_all(copies)
            if before is None:
                g = g_r[...].astype(f32)
            else:
                dn = pa_r[...].astype(f32) + pb_r[...].astype(f32)
                dx, dgain, dshift = ln_back(x_r[...], vec_r[up : up + 1, :], dn)
                g = dy_r[...] + dx
                g_o[...] = g
                pre_o[0:1, :] = dgain
                pre_o[1:2, :] = dshift
            g2 = g.astype(bf16)
            g2_o[...] = g2
            sums_o[...] = jnp.sum(g2.astype(f32), 0, keepdims=True)
            part = None
            for s in range(2):
                copies[s].wait()
                dh = mm(g2, weight(w_s, s, F, 2 * F))
                du = (gp_r[s][...].astype(f32) * dh).astype(bf16)
                du_o[:, s * F : (s + 1) * F] = du
                t = mm(du, weight(w_s, s, 0, F), NT)
                part = t if part is None else part + t
            part_o[...] = part.astype(bf16)

        ins = ([grad] if before is None else list(before)) + [Far(gp[0]), Far(gp[1])]
        outs = [((R, D), bf16), ((R, 2 * F), bf16), ((R, D), bf16, FAR), ((1, D), f32)]
        if before is not None:
            outs += [((R, D), f32), ((2, D), f32)]
        return run(kernel, ins, outs, weight_scratch(2 * F), w, scal, "feed_back", 6)

    def blocks_out(scal_r, full, outs):
        if S == 4:
            for o, at in zip(outs, (9, 11, 10, 12)):
                o[...] = full[scal_r[at]]
        else:
            outs[0][...] = full[...]

    def block_shapes(rows, columns):
        return [((rows, columns), bf16, FAR)] * 4 if S == 4 else [((S, rows, columns), bf16, FAR)]

    def feed_grads(n2, hid, g2, du):
        def kernel(n_r, h0, h1, g_r, du_r, g_o, b_o):
            for s, h_r in enumerate((h0, h1)):
                at = slice(s * F, (s + 1) * F)
                d = du_r[:, at]
                g_o[:, s, :, :F] = mm(n_r[...], d, TN).astype(bf16).reshape(S, M, F)
                g_o[:, s, :, F:] = mm(g_r[...], h_r[...], TN).astype(bf16).reshape(S, M, F)
                b_o[s : s + 1, :] = jnp.sum(d.astype(f32), 0, keepdims=True)

        return run(
            kernel,
            [Far(n2), Far(hid[0]), Far(hid[1]), g2, du],
            [((S, 2, M, 2 * F), bf16, FAR), ((2, F), f32)],
            name="feed_grads",
            us=3,
        )

    def middle_back(scal, y, g, pa, pb, vec, o0, o1, layer, w):
        n = len(w.arrays)
        gain = 6 * layer + 1

        def kernel(scal_r, y_r, g_r, pa_r, pb_r, vec_r, o0_r, o1_r, *refs):
            piece_r = refs[:n]
            dy_o, g1_o, d0_o, d1_o, sums_o, w_s, sems = refs[n:]
            copies = w.copies(scal_r, piece_r, pl.ds(z.a_cols - 256, 256), w_s, sems)
            start_all(copies)
            dn = pa_r[...].astype(f32) + pb_r[...].astype(f32)
            dx, dgain, dshift = ln_back(y_r[...], vec_r[gain : gain + 1, :], dn)
            dy = g_r[...].astype(f32) + dx
            dy_o[...] = dy
            g1 = dy.astype(bf16)
            g1_o[...] = g1
            send(g1_o)
            sums_o[0:1, :] = dgain
            sums_o[1:2, :] = jnp.sum(g1.astype(f32), 0, keepdims=True)
            sums_o[2:3, :] = dshift
            wait_all(copies)
            for e, (o_r, d_o) in enumerate(((o0_r, d0_o), (o1_r, d1_o))):
                do = mm(g1, weight(w_s, e, 256 - A, 256)).astype(bf16)
                prod = do.astype(f32) * o_r[...].astype(f32)
                for h in range(H):
                    lanes = slice(h * HD, (h + 1) * HD)
                    d_o[h] = beside(do[:, lanes], -jnp.sum(prod[:, lanes], -1, keepdims=True))

        outs = [((R, D), f32), ((R, D), bf16, FAR)] + [((H, R, WIDE), bf16)] * 2 + [((3, D), f32)]
        return run(
            kernel,
            [y, g, pa, pb, vec, o0, o1],
            outs,
            weight_scratch(256),
            w,
            scal,
            "middle_back",
            4,
        )

    def attend_back(qa, kvs, da):
        K = 4 * R

        def kernel(qa_r, k0, k1, k2, k3, da_r, dq_o, e0, e2, snd, k_s, v_s, dk_s, dv_s, dq_s):
            ones = jnp.ones((R, HD), bf16)
            for h in range(H):
                for b, kv_r in enumerate((k0, k1, k2, k3)):
                    blk = kv_r[...]
                    k_s[h, b * R : (b + 1) * R, :] = aug(blk, h * HD, ones)
                    v_s[h, b * R : (b + 1) * R, :] = aug(blk, A + h * HD, ones)

            def head(h, carry):
                qv = qa_r[h]
                dv_in = da_r[h]
                dqt = jnp.zeros((WIDE, R), f32)
                for b in range(4):
                    at = slice(b * R, (b + 1) * R)
                    kb = k_s[h, at, :]
                    p = jnp.exp2(mm(kb, qv, NT) * coef)
                    ds = (p * mm(v_s[h, at, :], dv_in, NT)).astype(bf16)
                    dv_s[h, at, :] = mm(p.astype(bf16), dv_in).astype(bf16)
                    dk_s[h, at, :] = (mm(ds, qv) * scale).astype(bf16)
                    dqt = dqt + mm(kb, ds, TN)
                dq_s[h] = (dqt.T * scale).astype(bf16)
                return carry

            lax.fori_loop(0, H, head, 0)
            dq_o[...] = jnp.concatenate([dq_s[h][:, :HD] for h in range(H)], 1)
            for b in range(4):
                at = slice(b * R, (b + 1) * R)
                e_o = (e0, snd.at[0], e2, snd.at[1])[b]
                e_o[...] = jnp.concatenate(
                    [dk_s[h, at, :HD] for h in range(H)] + [dv_s[h, at, :HD] for h in range(H)], 1
                )

        return run(
            kernel,
            [qa] + list(kvs) + [da],
            [((R, A), bf16)] + [((R, 2 * A), bf16)] * 2 + [((2, R, 2 * A), bf16, FAR)],
            [pltpu.VMEM((H, K, WIDE), bf16)] * 4 + [pltpu.VMEM((H, R, WIDE), bf16)],
            name="attend_back",
            us=6,
        )

    def cross_sum(own, pair):
        def kernel(a, b, o):
            o[...] = (a[...].astype(f32) + b[1].astype(f32)).astype(bf16)

        return run(kernel, [own, pair], [(own.shape, bf16, FAR)], name="cross_sum")[0]

    def proj_back(scal, dqs, kv_parts, layer, w, x=None):
        n = len(w.arrays)

        def kernel(scal_r, q0, q1, a0, p0, c0, a1, p1, c1, *refs):
            refs = list(refs)
            if x is not None:
                x_r = refs.pop(0)
            piece_r, refs = refs[:n], refs[n:]
            own_o, snd_o, part_o, b_o = refs[:4]
            w_s, sems = refs[-2:]
            copies = w.copies(scal_r, piece_r, pl.ds(0, z.a_cols), w_s, sems)
            start_all(copies)
            both = []
            for e, (q_r, a, p, c) in enumerate(((q0, a0, p0, c0), (q1, a1, p1, c1))):
                total = a[...].astype(f32) + p[0].astype(f32) + c[...].astype(f32)
                both.append(jnp.concatenate([q_r[...], total.astype(bf16)], 1))
                b_o[e : e + 1, :] = jnp.sum(both[e].astype(f32), 0, keepdims=True)
            if x is None:
                own_o[...], snd_o[...] = both
            else:
                odd = scal_r[8] == 1
                own_o[...] = jnp.where(odd, both[1], both[0])
                snd_o[...] = jnp.where(odd, both[0], both[1])
                send(snd_o)
                hat, _ = ln_parts(x_r[...].astype(f32))
            wait_all(copies)
            part = mm(both[0], weight(w_s, 0, 0, 3 * A), NT) + mm(both[1], weight(w_s, 1, 0, 3 * A), NT)
            part_o[...] = part.astype(bf16)
            if x is not None:
                send(part_o)
                refs[4][0:1, :] = jnp.sum(part * hat, 0, keepdims=True)
                refs[4][1:2, :] = jnp.sum(part, 0, keepdims=True)

        ins = list(dqs)
        for own, pair, cross in kv_parts:
            ins += [own, pair, cross]
        snd = ((R, 3 * A), bf16) if x is None else ((R, 3 * A), bf16, FAR)
        outs = [((R, 3 * A), bf16), snd, ((R, D), bf16, FAR), ((2, 3 * A), f32)]
        if x is not None:
            ins.append(x)
            outs.append(((2, D), f32))
        return run(kernel, ins, outs, weight_scratch(z.a_cols), w, scal, "project_back", 4)

    def proj_grads(scal, n1, n1_r, dp, dp_r, g1, g1_r, o, o_r):
        def kernel(scal_r, n_r, nr_r, p_r, pr_r, g_r, gr_r, o_i, or_i, *refs):
            first = mm(n_r[...], p_r[...], TN) + mm(nr_r[...], pr_r[...], TN)
            second = mm(g_r[...], o_i[...], TN) + mm(gr_r[...], or_i[...], TN)
            both = jnp.concatenate([first.astype(bf16), second.astype(bf16)], 1)
            refs[-1][...] = both.reshape(S, M, z.a_cols)
            if S == 4:
                refs[3][...] = refs[-1][scal_r[12], : M // 2, :]
                refs[4][...] = refs[-1][scal_r[12], M // 2 :, :]
                send(refs[3], refs[4])
                for o_, at in zip(refs[:3], (9, 11, 10)):
                    o_[...] = refs[-1][scal_r[at]]
            else:
                refs[0][...] = refs[-1][...]

        far = [((M // 2, z.a_cols), bf16, FAR)] * 2 if S == 4 else []
        return run(
            kernel,
            [n1, n1_r, dp, dp_r, g1, g1_r, o, o_r],
            (block_shapes(M, z.a_cols)[:3] if S == 4 else block_shapes(M, z.a_cols)) + far,
            [pltpu.VMEM((S, M, z.a_cols), bf16)],
            scalars=scal,
            name="project_grads",
            us=3,
        )

    def pair_grads(n1, dp0, dp1, g1, o0, o1):
        def kernel(n_r, p0, p1, g_r, o0_r, o1_r, out):
            for c, (p_r, o_r) in enumerate(((p0, o0_r), (p1, o1_r))):
                first = mm(n_r[...], p_r[...], TN).astype(bf16)
                second = mm(g_r[...], o_r[...], TN).astype(bf16)
                out[:, c] = jnp.concatenate([first, second], 1).reshape(S, M, z.a_cols)

        return run(
            kernel,
            [n1, dp0, dp1, g1, o0, o1],
            [((S, 2, M, z.a_cols), bf16, FAR)],
            name="pair_grads",
            us=3,
        )[0]

    def pass_on(up, down, low, high):
        def kernel(up_r, down_r, low_r, high_r, up_o, down_o):
            half = M // 2
            up_o[:half, :] = (up_r[:half, :].astype(f32) + low_r[...].astype(f32)).astype(bf16)
            up_o[half:, :] = up_r[half:, :]
            send(up_o)
            down_o[:half, :] = down_r[:half, :]
            down_o[half:, :] = (down_r[half:, :].astype(f32) + high_r[...].astype(f32)).astype(bf16)

        return run(
            kernel, [up, down, low, high], [((M, z.a_cols), bf16, FAR)] * 2, name="pass_on"
        )

    def small_grads(scal, mine, theirs):
        tall = 6 * L

        def kernel(scal_r, a_r, b_r, *refs):
            outs, all_s = refs[:-1], refs[-1]
            total = a_r[...] + b_r[...]
            odd = scal_r[8] == 1
            part = 2 * HD // S

            def pick(at):
                return jnp.where(odd, total[at + 1 : at + 2, :], total[at : at + 1, :])

            units = [pick(tall + 2 * l) for l in range(L)]
            units = jnp.concatenate(units + [jnp.zeros((TAIL - L, D), f32)], 0)[:, :F].astype(bf16)
            heads = [pick(tall + 2 * L + 2 * l) for l in range(L)]
            for t in range(S):
                side, place = divmod(t, S // 2)
                rows = []
                for row in heads:
                    cut = row[:, side * 2 * A : side * 2 * A + A]
                    at = place * part
                    rows.append(
                        jnp.concatenate([cut[:, h * HD + at : h * HD + at + part] for h in range(H)], 1)
                    )
                qv = jnp.concatenate(rows + [jnp.zeros((TAIL - L, 2 * A // S), f32)], 0)
                up = mm(units, spread(t, S, F), NT)
                rest = jnp.zeros((TAIL, z.a_cols - u_at - F // S), f32)
                all_s[t] = jnp.concatenate([total[:TAIL, t * M : (t + 1) * M], qv, up, rest], 1).astype(bf16)
            blocks_out(scal_r, all_s, outs)

        return run(
            kernel,
            [mine, theirs],
            block_shapes(TAIL, z.a_cols),
            [pltpu.VMEM((S, TAIL, z.a_cols), bf16)],
            scalars=scal,
            name="small_grads",
        )

    def pack_small(wide, ups, heads, pre_r):
        def kernel(*refs):
            o = refs[-1]
            o[...] = jnp.zeros((-(-10 * L // 8) * 8, D), f32)
            for l in range(L):
                pre_i, mid_i, last_i = refs[3 * l : 3 * l + 3]
                first = pre_i[...]
                if l == 0:
                    first = first + refs[5 * L][...]
                at = 6 * l
                o[at : at + 1, :] = first[0:1]
                o[at + 1 : at + 2, :] = mid_i[0:1, :]
                o[at + 2 : at + 3, :] = first[1:2]
                o[at + 3 : at + 5, :] = mid_i[1:3, :]
                o[at + 5 : at + 6, :] = last_i[...]
                o[6 * L + 2 * l : 6 * L + 2 * l + 2, :F] = refs[3 * L + l][...]
                o[8 * L + 2 * l : 8 * L + 2 * l + 2, : 3 * A] = refs[4 * L + l][...]

        flat = [a for row in wide for a in row] + list(ups) + list(heads) + [pre_r]
        flat = [Far(a) for a in flat]
        return run(kernel, flat, [((-(-10 * L // 8) * 8, D), f32, FAR)], name="pack_small")[0]

    def join_rows(scal, mine, theirs):
        def kernel(scal_r, a, b, o):
            start = pl.multiple_of(scal_r[8] * R, 16)
            o[pl.ds(start, R), :] = a[...]
            o[pl.ds(pl.multiple_of(R - start, 16), R), :] = b[...]

        return run(kernel, [mine, theirs], [((2 * R, D), bf16, FAR)], scalars=scal, name="join_rows")[0]

    def sum_blocks(blocks):
        def kernel(*refs):
            total = refs[0][...].astype(f32)
            for r in refs[1:-1]:
                total = total + r[...].astype(f32)
            refs[-1][...] = total.astype(bf16)

        return run(kernel, list(blocks), [(blocks[0].shape, bf16, FAR)], name="sum_blocks")[0]

    def feed_out(pairs):
        def kernel(*refs):
            up_o, down_o = refs[-2:]
            for l in range(L):
                total = refs[2 * l][...].astype(f32) + refs[2 * l + 1][...].astype(f32)
                up_o[l] = total[:, :F]
                down_o[l] = total[:, F:]

        return run(
            kernel,
            [a for p in pairs for a in p],
            [((L, M, F), f32, FAR), ((L, M, F), f32, FAR)],
            name="feed_out",
        )

    def proj_out(pairs, small):
        def kernel(*refs):
            qkv_o, out_o, qvb_o, upb_o, gain_o, shift_o = refs[-6:]
            for l in range(L):
                total = refs[2 * l][...].astype(f32) + refs[2 * l + 1][...].astype(f32)
                for h in range(H):
                    cuts = [total[:, i * A + h * HD : i * A + (h + 1) * HD] for i in range(3)]
                    qkv_o[l, h] = jnp.concatenate(cuts, 1)
                out_o[l] = total[:, 3 * A :].T
            tiny = refs[2 * L][...].astype(f32) + refs[2 * L + 1][...].astype(f32)
            part, unit = 2 * HD // S, 64 // S
            for l in range(L):
                gain_o[l] = tiny[6 * l : 6 * l + 2, :M]
                shift_o[l] = tiny[6 * l + 2 : 6 * l + 6, :M]
                for h in range(H):
                    qvb_o[h, l : l + 1, :] = tiny[l : l + 1, q_at + h * part : q_at + (h + 1) * part]
                for r in range(F // 64):
                    upb_o[r, l : l + 1, :] = tiny[l : l + 1, u_at + r * unit : u_at + (r + 1) * unit]

        return run(
            kernel,
            [a for p in list(pairs) + [small] for a in p],
            [
                ((L, H, M, 3 * HD), f32, FAR),
                ((L, A, M), f32, FAR),
                ((H, L, 2 * HD // S), f32),
                ((F // 64, L, 64 // S), f32),
                ((L, 2, M), f32),
                ((L, 4, M), f32),
            ],
            name="project_out",
        )

    def input_back(x, dy, pa, pb, vec):
        def kernel(x_r, dy_r, pa_r, pb_r, vec_r, o, sums_o):
            dn = pa_r[...].astype(f32) + pb_r[...].astype(f32)
            dx, dgain, dshift = ln_back(x_r[...].astype(f32), vec_r[0:1, :], dn)
            o[...] = (dy_r[...] + dx).astype(bf16)
            sums_o[0:1, :] = dgain
            sums_o[1:2, :] = dshift

        return run(kernel, [x, dy, pa, pb, vec], [((R, D), bf16, FAR), ((2, D), f32)], name="input_back")

    return dict(locals())


def local(mesh):
    def fn(frames, cotangent, w_qkv, qv_bias, w_out, w_up, up_bias, w_down, norm_gains, shifts):
        z = Sizes(mesh, frames, w_qkv, w_up)
        assert frames.shape[0] == 1
        k = make(z)
        L, m, R, D, A, F, H, HD, S = z.layers, z.m, z.rows, z.width, z.att, z.hidden, z.heads, z.hd, z.shards
        core = lax.axis_index("tc")
        scal = ring_scalars(S)

        def part_a(l, *then):
            qkv = after(w_qkv[l], *then).reshape(m, H, 3, HD).transpose(0, 2, 1, 3).reshape(m, 3 * A)
            return jnp.concatenate([qkv, after(w_out[l], *then).reshape(A, m).T], -1)

        def part_b(l, *then):
            return jnp.concatenate([after(w_up[l], *then), after(w_down[l], *then).T], -1)

        vec_rows = jnp.concatenate([norm_gains, shifts], 1).reshape(6 * L, m)
        bias_rows = jnp.concatenate([qv_bias.reshape(L, -1), up_bias.reshape(L, -1)], 1)
        bias_rows = jnp.pad(bias_rows, ((0, TAIL - L), (0, z.a_cols - m - bias_rows.shape[1])))
        tail = jnp.concatenate([jnp.pad(vec_rows, ((0, TAIL - 6 * L), (0, 0))), bias_rows], 1)
        message = jnp.concatenate([part_a(0), tail], 0)
        w_a = [Pieces(message, TAIL) if S == 4 else Gathered(message, S, TAIL)]
        w_b = [Gathered(after(part_b(0, message), *w_a[0].arrays[1:4]), S)]

        def my_rows(x):
            return lax.dynamic_slice_in_dim(x.reshape(2 * R, D), core * R, R, 0)

        kept = []
        x = my_rows(frames)
        for layer in range(L):
            if layer == 0:
                n1, q0, q1, kv0, kv1, vec, qb, tails = k["proj"](scal, x, 0, w_a[0])
            else:
                n1, q0, q1, kv0, kv1, x = k["proj"](scal, y, layer, w_a[layer], (vec, qb), (part, x_swap(part)))
            kvs = []
            for kv in (kv0, kv1):
                far = y_swap(kv)
                kvs.append((kv, core_swap(kv), far, core_swap(far)))
            if layer + 1 < L:
                next_a, next_b = part_a(layer + 1, n1), part_b(layer + 1, n1)
                q0 = after(q0, next_a)
            q0 = after(q0, kvs[1][2])
            o0, qa0 = k["attend"](q0, kvs[0])
            o1, qa1, o_own, o_snd, att_part = k["attend"](q1, kvs[1], scal, o0, w_a[layer])
            far = x_swap(att_part)
            n1_r = o_rcv = None
            if layer == 0:
                n1_r, o_rcv = core_swap(n1), core_swap(o_snd)
                x = after(x, n1_r, o_rcv)
            if layer + 1 < L:
                w_a.append(Gathered(after(next_a, kvs[0][2]), S))
                w_b.append(Gathered(after(next_b, o0), S))
            y, n2, *hid_gp, part = k["feed"](
                scal, x, att_part, far, vec, tails, layer, w_b[layer]
            )
            hid, gp = hid_gp[:2], hid_gp[2:]
            kept.append((x, n1, n1_r, kvs, (qa0, qa1), (o0, o1), o_own, o_rcv, y, n2, hid, gp))

        def whole_rows(mine):
            return k["join_rows"](scal, mine, core_swap(mine))[None]

        def send_blocks(blocks):
            if S == 4:
                return [blocks[0]] + [lax.ppermute(b, "shard", ring(s)) for b, s in zip(blocks[1:], (1, 3, 2))]
            return [lax.psum_scatter(blocks[0], "shard", scatter_dimension=0, tiled=True)[0]]

        def scatter(grad):
            flat = grad.reshape(2 * S * m, grad.shape[-1])
            return lax.psum_scatter(flat, ("shard", "tc"), scatter_dimension=0, tiled=True)

        def first_hops(blocks):
            if S != 4:
                return []
            return [lax.ppermute(blocks[3], "shard", ring(1)), lax.ppermute(blocks[4], "shard", ring(3))]

        def last_hops(blocks, hops):
            if S != 4:
                return [lax.psum_scatter(blocks[0], "shard", scatter_dimension=0, tiled=True)[0]]
            up, down = k["pass_on"](blocks[1], blocks[2], *hops)
            return [blocks[0], lax.ppermute(up, "shard", ring(1)), lax.ppermute(down, "shard", ring(3))]

        y_last, part_last = y, part
        g = my_rows(cotangent)
        wide, d_qv, d_up = [None] * L, [None] * L, [None] * L
        sum_a, sum_b = [None] * L, [None] * L
        before = None
        for layer in reversed(range(L)):
            x, n1, n1_r, kvs, qas, os, o_own, o_rcv, y, n2, hid, gp = kept[layer]
            if before is None:
                g2, du, part, sum_g2 = k["feed_back"](scal, g, gp, layer, w_b[layer])
            else:
                gp = [after(gp[0], grad_a), gp[1]]
                g2, du, part, sum_g2, g, pre = k["feed_back"](scal, None, gp, layer, w_b[layer], before)
                wide[layer + 1] = [pre] + wide[layer + 1]
            far = x_swap(part)
            grad_b, d_up[layer] = k["feed_grads"](n2, hid, g2, du)
            y = after(y, grad_b)
            if before is not None:
                sum_b[layer + 1] = (part_b_sum, y_swap(after(part_b_sum, part)))
                y = after(y, sum_b[layer + 1][1])
            dy, g1, d0, d1, mid = k["middle_back"](
                scal, y, g, part, far, vec, os[0], os[1], layer, w_a[layer]
            )
            part_b_sum = scatter(after(grad_b, d0))
            if layer == 0:
                g1_r = core_swap(g1)
                qas = (qas[0], after(qas[1], g1_r, part_a_sum))
            dqs, kv_parts, hold, far_kv = [], [], None, None
            for e in range(2):
                qa = qas[e]
                if e == 1:
                    qa = after(qa, hold)
                dq, own, y_own, snd = k["attend_back"](qa, kvs[e], (d0, d1)[e])
                if far_kv is not None:
                    snd = after(snd, far_kv)
                pair = core_swap(snd)
                hold = k["cross_sum"](y_own, pair)
                far_kv = y_swap(hold)
                dqs.append(dq)
                kv_parts.append((own, pair, far_kv))
            if before is None:
                part_last = after(part_last, dy)
                far_last = x_swap(part_last)
                dqs[0] = after(dqs[0], far_last)
            dp, dp_snd, part, d_qv[layer], *pre = k["proj_back"](
                scal, dqs, kv_parts, layer, w_a[layer], *([x] if layer == 0 else [])
            )
            far = x_swap(part)
            if layer > 0:
                grad_a = k["pair_grads"](n1, dp, dp_snd, g1, *os)
                part_a_sum = scatter(after(grad_a, part_b_sum, far))
            else:
                sum_a[1] = (part_a_sum, y_swap(after(part_a_sum, part)))
                blocks = k["proj_grads"](scal, n1, n1_r, dp, core_swap(dp_snd), g1, g1_r, o_own, o_rcv)
            wide[layer] = pre + [mid, sum_g2]
            before = (x, dy, part, far, vec)
        before = (x, after(dy, blocks[0]), part, far, vec)
        hops = first_hops(blocks)
        got_a = last_hops(blocks, hops)
        grad_rows, _ = k["input_back"](*before)
        frames_grad = whole_rows(grad_rows)
        pre = after(wide[0][0], blocks[0])
        sums = k["pack_small"](wide, d_up, d_qv, x_swap(pre))
        got_small = send_blocks(k["small_grads"](scal, sums, core_swap(sums)))
        mine = k["sum_blocks"](got_a)
        sum_a[0] = (mine, y_swap(mine))
        small = k["sum_blocks"](got_small)
        part_b_sum = after(part_b_sum, part)
        sum_b[0] = (part_b_sum, y_swap(part_b_sum))
        out_frames = whole_rows(k["finish"](y_last, part_last, far_last, vec)[0])
        outs_up, outs_down = k["feed_out"](sum_b)
        outs_qkv, outs_out, g_qvb, g_upb, g_gains, g_shifts = k["proj_out"](sum_a, (small, y_swap(small)))
        return (
            out_frames,
            frames_grad,
            outs_qkv.transpose(0, 2, 1, 3),
            g_qvb.transpose(1, 0, 2),
            outs_out.reshape(L, H, HD, m),
            outs_up,
            g_upb.transpose(1, 0, 2),
            outs_down.transpose(0, 2, 1),
            g_gains,
            g_shifts,
        )

    return fn


def solution(mesh):
    assert mesh.axis_names == ("shard", "ctx", "tp") and mesh.shape["tp"] == 4 and mesh.shape["ctx"] == 2
    split = Mesh(mesh.devices.reshape(mesh.shape["shard"], 2, 2, 2), ("shard", "ctx", "tx", "tc"))
    tp = ("tx", "tc")
    specs = (
        P("shard", "ctx", None),
        P("shard", "ctx", None),
        P(None, "shard", tp, None),
        P(None, tp, "shard"),
        P(None, tp, None, "shard"),
        P(None, "shard", tp),
        P(None, tp, "shard"),
        P(None, tp, "shard"),
        P(None, None, "shard"),
        P(None, None, "shard"),
    )
    return jax.shard_map(local(split), mesh=split, in_specs=specs, out_specs=specs, check_vma=False)
```

```python
import math

import jax
import jax.numpy as jnp
from jax import lax
from jax.experimental import pallas as pl
from jax.experimental.pallas import tpu as pltpu
from jax.sharding import Mesh
from jax.sharding import PartitionSpec as P

f32 = jnp.float32
bf16 = jnp.bfloat16
EPSILON = 1e-05
NN = (((1,), (0,)), ((), ()))
NT = (((1,), (1,)), ((), ()))
TN = (((0,), (0,)), ((), ()))
VMEM_MIB = {
    "attend_far": 13,
    "attend_near": 10,
    "attend_back": 14,
    "feed": 16,
    "feed_back": 16,
    "feed_grads": 12,
    "own_grads": 9,
    "feed_out": 7.6,
    "finish": 6,
    "input_back": 10,
    "middle_back": 11,
    "pack_first": 6,
    "pair_grads": 9,
    "project": 9.5,
    "project_back": 9.5,
    "project_grads": 13,
    "project_out": 5,
}
WIDE = 128
TAIL = 16
COST = 500_000_000


def mm(a, b, dims=NN):
    return lax.dot_general(a, b, dims, preferred_element_type=f32)


def core_swap(x):
    return lax.ppermute(x, "tc", [(0, 1), (1, 0)])


def x_swap(x):
    return lax.ppermute(x, "tx", [(0, 1), (1, 0)])


def y_swap(x):
    return lax.ppermute(x, "ctx", [(0, 1), (1, 0)])


def after(x, *others):
    return lax.optimization_barrier((x,) + others)[0]


def ring(shift):
    return [(i, (i + shift) % 4) for i in range(4)]


def ring_scalars(shards):
    me = lax.axis_index("shard").astype(jnp.int32)
    zero = jnp.int32(0)
    order = [me, (me + shards - 1) % shards, (me + 1) % shards, (me + 2) % shards]
    return jnp.stack([zero] * 8 + [lax.axis_index("tc").astype(jnp.int32)] + order + [zero] * 3)


class Pieces:
    def __init__(self, x, tail=0):
        self.rows = x.shape[0] - tail
        self.mine = [x] + [lax.ppermute(x, "shard", ring(s)) for s in (1, 3, 2)]
        self.arrays = self.mine + [core_swap(p) for p in self.mine]

    def copies(self, scal, refs, columns, dest, sems):
        out = []
        for k, ref in enumerate(refs):
            slot = scal[8] if k < 4 else 1 - scal[8]
            to = dest.at[slot, scal[9 + k % 4]]
            out.append(pltpu.make_async_copy(ref.at[pl.ds(0, self.rows), columns], to, sems.at[k]))
        return out

    def tails(self, scal, refs, dest, sems):
        out = []
        for k, ref in enumerate(refs):
            slot = scal[8] if k < 4 else 1 - scal[8]
            to = dest.at[slot, scal[9 + k % 4]]
            out.append(pltpu.make_async_copy(ref.at[pl.ds(self.rows, TAIL), :], to, sems.at[k]))
        return out


class Gathered:
    def __init__(self, x, shards, tail=0):
        self.rows = x.shape[0] - tail
        whole = lax.all_gather(x, ("shard", "tc"), axis=0, tiled=False)
        self.arrays = [whole.reshape((shards, 2) + x.shape)]

    def copies(self, scal, refs, columns, dest, sems):
        ref = refs[0]
        return [
            pltpu.make_async_copy(ref.at[:, c, pl.ds(0, self.rows), columns], dest.at[c], sems.at[c])
            for c in range(2)
        ]

    def tails(self, scal, refs, dest, sems):
        ref = refs[0]
        return [
            pltpu.make_async_copy(ref.at[:, c, pl.ds(self.rows, TAIL), :], dest.at[c], sems.at[c])
            for c in range(2)
        ]


def vmem():
    return pl.BlockSpec(memory_space=pltpu.VMEM)


class Far:
    def __init__(self, array):
        self.array = array


class Reading:
    def __init__(self, buffer, copy):
        self.buffer, self.copy, self.waited = buffer, copy, False

    def need(self):
        if not self.waited:
            self.copy.wait()
            self.waited = True
        return self.buffer

    def __getitem__(self, index):
        return self.need()[index]

    @property
    def shape(self):
        return self.buffer.shape


class Writing:
    def __init__(self, buffer, copy):
        self.buffer, self.copy, self.sent = buffer, copy, False

    def __setitem__(self, index, value):
        self.buffer[index] = value

    @property
    def at(self):
        return self.buffer.at

    def send(self):
        if not self.sent:
            self.copy.start()
            self.sent = True


def send(*refs):
    for r in refs:
        if isinstance(r, Writing):
            r.send()


def need(*refs):
    for r in refs:
        if isinstance(r, Reading):
            r.need()


FAR = "far"


def run(kernel, ins, outs, scratch=(), w=None, scalars=None, name=None, us=1.0):
    pieces = [] if w is None else w.arrays
    n_in, n_out, n_pieces = len(ins), len(outs), len(pieces)
    far_in = [i for i, a in enumerate(ins) if isinstance(a, Far)]
    far_out = [i for i, o in enumerate(outs) if len(o) == 3]
    any_space = pl.BlockSpec(memory_space=pl.ANY)
    specs, args = [], []
    if scalars is not None:
        specs.append(pl.BlockSpec(memory_space=pltpu.SMEM))
        args.append(scalars)
    for a in ins:
        if isinstance(a, Far):
            specs.append(any_space)
            args.append(pltpu.with_memory_space_constraint(a.array, pltpu.HBM))
        else:
            specs.append(vmem())
            args.append(a)
    for p in pieces:
        specs.append(any_space)
        args.append(pltpu.with_memory_space_constraint(p, pltpu.HBM))
    first = len(args) - n_in - n_pieces
    shapes = [
        pltpu.HBM(o[0], o[1]) if len(o) == 3 else jax.ShapeDtypeStruct(o[0], o[1]) for o in outs
    ]
    buffers = [pltpu.VMEM(ins[i].array.shape, ins[i].array.dtype) for i in far_in]
    buffers += [pltpu.VMEM(outs[i][0], outs[i][1]) for i in far_out]
    sems = [pltpu.SemaphoreType.DMA((len(buffers),))] if buffers else []

    def wrapped(*refs):
        refs = list(refs)
        n_all = len(args) + n_out + len(scratch)
        own, extra = refs[:n_all], refs[n_all:]
        reads, writes = [], []
        for k, i in enumerate(far_in):
            copy = pltpu.make_async_copy(own[first + i], extra[k], extra[-1].at[k])
            copy.start()
            own[first + i] = Reading(extra[k], copy)
            reads.append(own[first + i])
        for k, i in enumerate(far_out):
            k += len(far_in)
            at = len(args) + i
            own[at] = Writing(extra[k], pltpu.make_async_copy(extra[k], own[at], extra[-1].at[k]))
            writes.append(own[at])
        kernel(*own)
        for w in writes:
            w.send()
        for r in reads:
            r.need()
        for w in writes:
            w.copy.wait()

    return pl.pallas_call(
        wrapped,
        out_shape=shapes,
        in_specs=specs,
        out_specs=[any_space if len(o) == 3 else vmem() for o in outs],
        scratch_shapes=list(scratch) + buffers + sems,
        compiler_params=pltpu.CompilerParams(vmem_limit_bytes=int(VMEM_MIB.get(name, 4) * 1024 * 1024)),
        cost_estimate=pl.CostEstimate(flops=int(us * COST), bytes_accessed=1000, transcendentals=0),
        name=name,
    )(*args)


def spread(shard, shards, units):
    part = 64 // shards
    bits, low = part.bit_length() - 1, part - 1
    i = lax.broadcasted_iota(jnp.int32, (units // shards, units), 0)
    j = lax.broadcasted_iota(jnp.int32, (units // shards, units), 1)
    same = ((j >> 6) == (i >> bits)) & ((j & 63) == shard * part + (i & low))
    return jnp.where(same, 1.0, 0.0).astype(bf16)


def start_all(copies):
    for c in copies:
        c.start()


def wait_all(copies):
    for c in copies:
        c.wait()


def ln_parts(x):
    centred = x - jnp.mean(x, -1, keepdims=True)
    inv = lax.rsqrt(jnp.mean(centred * centred, -1, keepdims=True) + EPSILON)
    return centred * inv, inv


def ln_back(x, gain, dn):
    hat, inv = ln_parts(x)
    dhat = dn * gain
    dx = inv * (
        dhat
        - jnp.mean(dhat, -1, keepdims=True)
        - hat * jnp.mean(dhat * hat, -1, keepdims=True)
    )
    return dx, jnp.sum(dn * hat, 0, keepdims=True), jnp.sum(dn, 0, keepdims=True)


def split3(v):
    a = v.astype(bf16)
    r = v - a.astype(f32)
    b = r.astype(bf16)
    c = (r - b.astype(f32)).astype(bf16)
    return a, b, c


def beside(wide, column):
    a, b, c = split3(column)
    rows, size = wide.shape[0], wide.shape[1]
    return jnp.concatenate([wide, a, b, c, jnp.zeros((rows, WIDE - size - 3), bf16)], 1)


class Sizes:
    def __init__(self, mesh, frames, w_qkv, w_up):
        self.shards = mesh.shape["shard"]
        self.layers = w_qkv.shape[0]
        self.width = frames.shape[-1]
        self.rows = frames.shape[1] // 2
        self.heads = w_qkv.shape[2]
        self.hd = w_qkv.shape[3] // 3
        self.att = self.heads * self.hd
        self.hidden = w_up.shape[2]
        self.m = w_qkv.shape[1]
        self.a_cols = 4 * self.att
        self.b_cols = 2 * self.hidden


def make(z):
    R, D, A, H, HD, F = z.rows, z.width, z.att, z.heads, z.hd, z.hidden
    L, S, M = z.layers, z.shards, z.m
    coef = HD ** (-0.5) / math.log(2.0)
    scale = HD ** (-0.5)
    dma = pltpu.SemaphoreType.DMA
    q_at, u_at = M, M + 2 * A // S

    def weight_scratch(columns):
        return [pltpu.VMEM((2, S, M, columns), bf16), dma((8,))]

    def weight(w_s, c, start, stop):
        return w_s[c, :, :, start:stop].reshape(D, stop - start)

    def pack_first(w_qkv, w_out, qv_bias, up_bias, norm_gains, shifts):
        nq, nu = 2 * HD // S, 64 // S

        def kernel(w_r, o_r, qv_r, up_r, g_r, s_r, out):
            for side in range(3):
                cuts = [w_r[h][:, side * HD : (side + 1) * HD] for h in range(H)]
                out[:M, side * A : (side + 1) * A] = jnp.concatenate(cuts, 1)
            out[:M, 3 * A :] = o_r[...].astype(f32).T.astype(bf16)
            vecs = []
            for l in range(L):
                vecs += [g_r[l].astype(f32), s_r[l].astype(f32)]
            vecs = jnp.concatenate(vecs + [jnp.zeros((TAIL - 6 * L, M), f32)], 0)
            rows = []
            for l in range(L):
                q, u = qv_r[l].astype(f32), up_r[l].astype(f32)
                cuts = [q[h : h + 1, :] for h in range(H)] + [u[r : r + 1, :] for r in range(F // 64)]
                rows.append(jnp.concatenate(cuts, 1))
            rows = jnp.concatenate(rows + [jnp.zeros((TAIL - L, H * nq + F // 64 * nu), f32)], 0)
            rest = jnp.zeros((TAIL, z.a_cols - M - rows.shape[1]), f32)
            out[M:, :] = jnp.concatenate([vecs, rows, rest], 1).astype(bf16)

        return run(
            kernel,
            [w_qkv.transpose(1, 0, 2), w_out, qv_bias, up_bias, norm_gains, shifts],
            [((M + TAIL, z.a_cols), bf16, FAR)],
            name="pack_first",
        )[0]

    def proj(scal, x, layer, w, biases=None, prev=None):
        first = biases is None
        n = len(w.arrays)
        part = 2 * HD // S

        def kernel(*refs):
            it = iter(refs)
            scal_r, x_r = next(it), next(it)
            if not first:
                vec_r, qb_r, pa_r, pb_r = (next(it) for _ in range(4))
            piece_r = [next(it) for _ in range(n)]
            n_o, q_o, kv_o = (next(it) for _ in range(3))
            if first:
                vec_r, qb_r, tail_o = (next(it) for _ in range(3))
            else:
                x_o = next(it)
            w_s, sems = next(it), next(it)
            if first:
                tail_sems = next(it)
                tails = w.tails(scal_r, piece_r, tail_o, tail_sems)
                start_all(tails)
            copies = w.copies(scal_r, piece_r, pl.ds(0, z.a_cols), w_s, sems)
            start_all(copies)
            xv = x_r[...].astype(f32)
            if not first:
                at = 6 * (layer - 1) + 5
                xv = xv + (pa_r[...].astype(f32) + pb_r[...].astype(f32) + vec_r[at : at + 1, :])
                x_o[...] = xv
                send(x_o)
            hat, _ = ln_parts(xv)
            if first:
                wait_all(tails)
                vec_r[...] = jnp.concatenate([tail_o[0, t][:, :M] for t in range(S)], 1).astype(f32)
                for l in range(L):
                    for p in range(2):
                        rows = [tail_o[p, t].astype(f32)[l : l + 1, q_at:u_at] for t in range(S)]
                        seq = []
                        for side in range(2):
                            for h in range(H):
                                seq += [
                                    rows[t][:, h * part : (h + 1) * part]
                                    for t in range(side * S // 2, (side + 1) * S // 2)
                                ]
                            if side == 0:
                                seq.append(jnp.zeros((1, A), f32))
                        qb_r[2 * l + p : 2 * l + p + 1, :] = jnp.concatenate(seq, 1)
            g = 6 * layer
            nv = (hat * vec_r[g : g + 1, :] + vec_r[g + 2 : g + 3, :]).astype(bf16)
            n_o[...] = nv
            send(n_o)
            wait_all(copies)
            both = []
            for e in range(2):
                b = 2 * layer + e
                p = (mm(nv, weight(w_s, e, 0, 3 * A)) + qb_r[b : b + 1, :]).astype(bf16)
                kv_o[:, e * 2 * A : (e + 1) * 2 * A] = p[:, A:]
                both.append(p[:, :A])
            send(kv_o)
            q_o[...] = jnp.concatenate(both, 1)

        ins = [Far(x)] + ([] if first else list(biases) + [Far(p) for p in prev])
        outs = [((R, D), bf16, FAR), ((R, 2 * A), bf16), ((R, 4 * A), bf16, FAR)]
        scratch = weight_scratch(z.a_cols)
        if first:
            outs += [((TAIL, D), f32), ((2 * L, 3 * A), f32), ((2, S, TAIL, z.a_cols), bf16)]
            scratch += [dma((8,))]
        else:
            outs += [((R, D), f32, FAR)]
        return run(kernel, ins, outs, scratch, w, scal, "project", 3.5)

    def aug(block, offset, fill):
        return jnp.concatenate([block[:, offset : offset + HD], fill], 1)

    def head_lanes(j):
        e, h = divmod(j, H)
        return j * HD, e * 2 * A + h * HD, e * 2 * A + A + h * HD

    def load_heads(kv_refs, k_s, v_s):
        ones = jnp.ones((R, HD), bf16)
        for b, ref in enumerate(kv_refs):
            blk = ref[...]
            for j in range(2 * H):
                _, k_at, v_at = head_lanes(j)
                k_s[j, b * R : (b + 1) * R, :] = aug(blk, k_at, ones)
                v_s[j, b * R : (b + 1) * R, :] = aug(blk, v_at, ones)

    def attend_near(q, kvs):
        K = 2 * R

        def kernel(q_r, kv0, kv1, acc_o, q_s, k_s, v_s):
            zeros = jnp.zeros((R, HD), bf16)
            for j in range(2 * H):
                q_s[j] = aug(q_r[...], j * HD, zeros)
            load_heads((kv0, kv1), k_s, v_s)

            def head(j, carry):
                s = mm(q_s[j], k_s[j], NT)
                top = jnp.max(s, -1, keepdims=True)
                oe = mm(jnp.exp2((s - top) * coef).astype(bf16), v_s[j])
                acc_o[j] = jnp.concatenate(
                    [oe[:, : HD + 1], top, jnp.zeros((R, WIDE - HD - 2), f32)], 1
                )
                return carry

            lax.fori_loop(0, 2 * H, head, 0)

        return run(
            kernel,
            [q] + list(kvs),
            [((2 * H, R, WIDE), f32)],
            [pltpu.VMEM((2 * H, R, WIDE), bf16)] + [pltpu.VMEM((2 * H, K, WIDE), bf16)] * 2,
            name="attend_near",
            us=6,
        )[0]

    def attend_far(scal, q, kvs, acc, w):
        K = 2 * R
        n = len(w.arrays)

        def kernel(scal_r, q_r, kv2, kv3, acc_r, *refs):
            piece_r = refs[:n]
            o0_o, o1_o, qa_o, own_o, snd_o, part_o, q_s, k_s, v_s, o_s, w_s, sems = refs[n:]
            copies = w.copies(scal_r, piece_r, pl.ds(z.a_cols - 256, 256), w_s, sems)
            start_all(copies)
            zeros = jnp.zeros((R, HD), bf16)
            for j in range(2 * H):
                q_s[j] = aug(q_r[...], j * HD, zeros)
            load_heads((kv2, kv3), k_s, v_s)

            def head(j, carry):
                s = mm(q_s[j], k_s[j], NT)
                old = acc_r[j]
                old_top = old[:, HD + 1 : HD + 2]
                top = jnp.maximum(jnp.max(s, -1, keepdims=True), old_top)
                oe = mm(jnp.exp2((s - top) * coef).astype(bf16), v_s[j])
                oe = oe + old * jnp.exp2((old_top - top) * coef)
                total = oe[:, HD : HD + 1]
                o_s[j] = (oe[:, :HD] / total).astype(bf16)
                lse = top + jnp.log2(total) * (1.0 / coef)
                qa_o.buffer[j] = beside(q_s[j][:, :HD], -lse)
                return carry

            lax.fori_loop(0, 2 * H, head, 0)
            send(qa_o)
            o0 = jnp.concatenate([o_s[j] for j in range(H)], 1)
            o1 = jnp.concatenate([o_s[H + j] for j in range(H)], 1)
            wait_all(copies)
            part = mm(o0, weight(w_s, 0, 256 - A, 256), NT) + mm(o1, weight(w_s, 1, 256 - A, 256), NT)
            part_o[...] = part.astype(bf16)
            send(part_o)
            odd = scal_r[8] == 1
            o0_o[...] = o0
            o1_o[...] = o1
            own_o[...] = jnp.where(odd, o1, o0)
            snd_o[...] = jnp.where(odd, o0, o1)

        return run(
            kernel,
            [q] + list(kvs) + [acc],
            [((R, A), bf16, FAR)] * 2
            + [((2 * H, R, WIDE), bf16, FAR)]
            + [((R, A), bf16, FAR)] * 2
            + [((R, D), bf16, FAR)],
            [pltpu.VMEM((2 * H, R, WIDE), bf16)]
            + [pltpu.VMEM((2 * H, K, WIDE), bf16)] * 2
            + [pltpu.VMEM((2 * H, R, HD), bf16)]
            + weight_scratch(256),
            w,
            scal,
            "attend_far",
            8,
        )

    def feed(scal, x, pa, pb, vec, tails, layer, w):
        n = len(w.arrays)
        g = 6 * layer

        def kernel(scal_r, x_r, pa_r, pb_r, vec_r, tail_r, *refs):
            piece_r = refs[:n]
            y_o, n_o, *hid_gp, part_o, w_s, sems = refs[n:]
            copies = w.copies(scal_r, piece_r, pl.ds(0, 2 * F), w_s, sems)
            start_all(copies)
            y = x_r[...].astype(f32) + (
                pa_r[...].astype(f32) + pb_r[...].astype(f32) + vec_r[g + 3 : g + 4, :]
            )
            y_o[...] = y
            send(y_o)
            hat, _ = ln_parts(y)
            nv = (hat * vec_r[g + 1 : g + 2, :] + vec_r[g + 4 : g + 5, :]).astype(bf16)
            n_o[...] = nv
            send(n_o)
            bias = [None, None]
            for t in range(S):
                e = spread(t, S, F)
                for s in range(2):
                    add = mm(tail_r[s, t][:, u_at : u_at + F // S], e)
                    bias[s] = add if t == 0 else bias[s] + add
            part, hiddens = None, []
            for s in range(2):
                copies[s].wait()
                u = mm(nv, weight(w_s, s, 0, F)) + bias[s][layer : layer + 1, :]
                cdf = 0.5 * (1.0 + lax.erf(u * (0.5**0.5)))
                pdf = jnp.exp(-0.5 * u * u) * (1.0 / math.sqrt(2.0 * math.pi))
                hidden = (u * cdf).astype(bf16)
                hid_gp[2 + s][...] = (cdf + u * pdf).astype(bf16)
                send(hid_gp[2 + s])
                hiddens.append(hidden)
                t = mm(hidden, weight(w_s, s, F, 2 * F), NT)
                part = t if part is None else part + t
            part_o[...] = part.astype(bf16)
            send(part_o)
            odd = scal_r[8] == 1
            hid_gp[0][...] = jnp.where(odd, hiddens[1], hiddens[0])
            hid_gp[1][...] = jnp.where(odd, hiddens[0], hiddens[1])

        outs = [
            ((R, D), f32, FAR),
            ((R, D), bf16, FAR),
            ((R, F), bf16, FAR),
            ((R, F), bf16, FAR),
            ((R, F), bf16, FAR),
            ((R, F), bf16, FAR),
            ((R, D), bf16, FAR),
        ]
        return run(
            kernel, [Far(x), Far(pa), Far(pb), vec, tails], outs, weight_scratch(2 * F), w, scal, "feed", 6
        )

    def finish(y, pa, pb, vec):
        at = 6 * (L - 1) + 5

        def kernel(y_r, pa_r, pb_r, vec_r, o):
            v = y_r[...] + (pa_r[...].astype(f32) + pb_r[...].astype(f32) + vec_r[at : at + 1, :])
            o[...] = v.astype(bf16)

        return run(kernel, [Far(y), Far(pa), Far(pb), vec], [((R, D), bf16, FAR)], name="finish")

    def feed_back(scal, grad, gp, layer, w, before=None):
        n = len(w.arrays)
        up = 6 * (layer + 1)

        def kernel(*refs):
            it = iter(refs)
            scal_r = next(it)
            if before is None:
                g_r = next(it)
            else:
                x_r, dy_r, pa_r, pb_r, vec_r = (next(it) for _ in range(5))
            gp_r = (next(it), next(it))
            piece_r = [next(it) for _ in range(n)]
            swap_o, du_o, part_o, sums_o = (next(it) for _ in range(4))
            if before is not None:
                g_o, pre_o = next(it), next(it)
            w_s, sems = next(it), next(it)
            copies = w.copies(scal_r, piece_r, pl.ds(0, 2 * F), w_s, sems)
            start_all(copies)
            if before is None:
                g = g_r[...].astype(f32)
            else:
                dn = pa_r[...].astype(f32) + pb_r[...].astype(f32)
                dx, dgain, dshift = ln_back(x_r[...], vec_r[up : up + 1, :], dn)
                g = dy_r[...] + dx
                g_o[...] = g
                pre_o[0:1, :] = dgain
                pre_o[1:2, :] = dshift
            g2 = g.astype(bf16)
            swap_o[:, :D] = g2
            sums_o[...] = jnp.sum(g2.astype(f32), 0, keepdims=True)
            part, dus = None, []
            for s in range(2):
                copies[s].wait()
                dh = mm(g2, weight(w_s, s, F, 2 * F))
                du = (gp_r[s][...].astype(f32) * dh).astype(bf16)
                dus.append(du)
                t = mm(du, weight(w_s, s, 0, F), NT)
                part = t if part is None else part + t
            part_o[...] = part.astype(bf16)
            send(part_o)
            odd = scal_r[8] == 1
            du_o[...] = jnp.where(odd, dus[1], dus[0])
            swap_o[:, D:] = jnp.where(odd, dus[0], dus[1])

        ins = [grad] if before is None else [Far(b) for b in before[:4]] + [before[4]]
        ins += [Far(gp[0]), Far(gp[1])]
        outs = [((R, D + F), bf16, FAR), ((R, F), bf16), ((R, D), bf16, FAR), ((1, D), f32)]
        if before is not None:
            outs += [((R, D), f32), ((2, D), f32)]
        return run(kernel, ins, outs, weight_scratch(2 * F), w, scal, "feed_back", 6)

    def blocks_out(scal_r, full, outs):
        if S == 4:
            for o, at in zip(outs, (9, 11, 10, 12)):
                o[...] = full[scal_r[at]]
        else:
            outs[0][...] = full[...]

    def block_shapes(rows, columns):
        return [((rows, columns), bf16, FAR)] * 4 if S == 4 else [((S, rows, columns), bf16, FAR)]

    def feed_grads(scal, n2, n2_r, hid, hid_r, swap, swap_r, du):
        def kernel(scal_r, n_r, nr_r, h_r, hr_r, s_r, sr_r, du_r, g_o, b_o):
            other = sr_r[:, D:]
            g_o[:, :F] = (mm(n_r[...], du_r[...], TN) + mm(nr_r[...], other, TN)).astype(bf16)
            g_o[:, F:] = (mm(s_r[:, :D], h_r[...], TN) + mm(sr_r[:, :D], hr_r[...], TN)).astype(bf16)
            total = jnp.sum(du_r[...].astype(f32), 0, keepdims=True) + jnp.sum(
                other.astype(f32), 0, keepdims=True
            )
            odd = scal_r[8] == 1
            b_o[0:1, :] = jnp.where(odd, 0.0, total)
            b_o[1:2, :] = jnp.where(odd, total, 0.0)

        return run(
            kernel,
            [Far(n2), Far(n2_r), Far(hid), Far(hid_r), Far(swap), Far(swap_r), du],
            [((D, 2 * F), bf16, FAR), ((2, F), f32)],
            scalars=scal,
            name="feed_grads",
            us=3,
        )

    def middle_back(scal, y, g, pa, pb, vec, o0, o1, layer, w):
        n = len(w.arrays)
        gain = 6 * layer + 1

        def kernel(scal_r, y_r, g_r, pa_r, pb_r, vec_r, o0_r, o1_r, *refs):
            piece_r = refs[:n]
            dy_o, g1_o, d_o, sums_o, w_s, sems = refs[n:]
            copies = w.copies(scal_r, piece_r, pl.ds(z.a_cols - 256, 256), w_s, sems)
            start_all(copies)
            dn = pa_r[...].astype(f32) + pb_r[...].astype(f32)
            dx, dgain, dshift = ln_back(y_r[...], vec_r[gain : gain + 1, :], dn)
            dy = g_r[...].astype(f32) + dx
            dy_o[...] = dy
            send(dy_o)
            g1 = dy.astype(bf16)
            g1_o[...] = g1
            send(g1_o)
            sums_o[0:1, :] = dgain
            sums_o[1:2, :] = jnp.sum(g1.astype(f32), 0, keepdims=True)
            sums_o[2:3, :] = dshift
            wait_all(copies)
            for e, o_r in enumerate((o0_r, o1_r)):
                do = mm(g1, weight(w_s, e, 256 - A, 256)).astype(bf16)
                prod = do.astype(f32) * o_r[...].astype(f32)
                for h in range(H):
                    lanes = slice(h * HD, (h + 1) * HD)
                    d_o[e * H + h] = beside(do[:, lanes], -jnp.sum(prod[:, lanes], -1, keepdims=True))

        outs = [((R, D), f32, FAR), ((R, D), bf16, FAR), ((2 * H, R, WIDE), bf16), ((3, D), f32)]
        return run(
            kernel,
            [Far(y), g, Far(pa), Far(pb), vec, Far(o0), Far(o1)],
            outs,
            weight_scratch(256),
            w,
            scal,
            "middle_back",
            4,
        )

    def attend_back(qa, kvs, da, before=None):
        K = 2 * R

        def kernel(qa_r, kv0, kv1, da_r, *refs):
            refs = list(refs)
            if before is not None:
                old_r = refs.pop(0)
            dq_o, e0, e1, k_s, v_s, dk_s, dv_s, *dq_s = refs
            need(qa_r)
            load_heads((kv0, kv1), k_s, v_s)

            def head(j, carry):
                qv = qa_r[j]
                dv_in = da_r[j]
                dqt = None
                for b in range(2):
                    at = slice(b * R, (b + 1) * R)
                    kb = k_s[j, at, :]
                    p = jnp.exp2(mm(kb, qv, NT) * coef)
                    ds = (p * mm(v_s[j, at, :], dv_in, NT)).astype(bf16)
                    dv_s[j, at, :] = mm(p.astype(bf16), dv_in).astype(bf16)
                    dk_s[j, at, :] = (mm(ds, qv) * scale).astype(bf16)
                    t = mm(kb, ds, TN)
                    dqt = t if dqt is None else dqt + t
                if before is None:
                    dq_o[j] = dqt
                else:
                    dq_s[0][j] = ((dqt + old_r[j]).T * scale).astype(bf16)
                return carry

            lax.fori_loop(0, 2 * H, head, 0)
            for b, e_o in ((1, e1), (0, e0)):
                at = slice(b * R, (b + 1) * R)
                cols = []
                for e in range(2):
                    cols += [dk_s[e * H + h, at, :HD] for h in range(H)]
                    cols += [dv_s[e * H + h, at, :HD] for h in range(H)]
                e_o[...] = jnp.concatenate(cols, 1)
                send(e_o)
            if before is not None:
                dq_o[...] = jnp.concatenate([dq_s[0][j][:, :HD] for j in range(2 * H)], 1)

        ins = [Far(qa)] + [Far(a) for a in kvs] + [da]
        outs = [((R, 4 * A), bf16), ((R, 4 * A), bf16, FAR)]
        scratch = [pltpu.VMEM((2 * H, K, WIDE), bf16)] * 4
        if before is None:
            outs = [((2 * H, WIDE, R), f32)] + outs
        else:
            ins.append(before)
            outs = [((R, 2 * A), bf16)] + outs
            scratch.append(pltpu.VMEM((2 * H, R, WIDE), bf16))
        return run(kernel, ins, outs, scratch, name="attend_back", us=8)

    def cross_sum(own, theirs):
        def kernel(a, b, o):
            o[...] = (a[...].astype(f32) + b[...].astype(f32)).astype(bf16)

        return run(kernel, [own, theirs], [(own.shape, bf16, FAR)], name="cross_sum")[0]

    def proj_back(scal, dq, kv_parts, layer, w, x=None):
        n = len(w.arrays)

        def kernel(scal_r, q_r, a, p, c, *refs):
            refs = list(refs)
            if x is not None:
                x_r = refs.pop(0)
            piece_r, refs = refs[:n], refs[n:]
            own_o, snd_o, part_o, b_o = refs[:4]
            w_s, sems = refs[-2:]
            copies = w.copies(scal_r, piece_r, pl.ds(0, z.a_cols), w_s, sems)
            start_all(copies)
            both = []
            for e in range(2):
                at = slice(e * 2 * A, (e + 1) * 2 * A)
                total = a[:, at].astype(f32) + p[:, at].astype(f32) + c[:, at].astype(f32)
                both.append(jnp.concatenate([q_r[:, e * A : (e + 1) * A], total.astype(bf16)], 1))
                b_o[e : e + 1, :] = jnp.sum(both[e].astype(f32), 0, keepdims=True)
            odd = scal_r[8] == 1
            own_o[...] = jnp.where(odd, both[1], both[0])
            snd_o[...] = jnp.where(odd, both[0], both[1])
            send(snd_o)
            if x is not None:
                hat, _ = ln_parts(x_r[...].astype(f32))
            wait_all(copies)
            part = mm(both[0], weight(w_s, 0, 0, 3 * A), NT) + mm(both[1], weight(w_s, 1, 0, 3 * A), NT)
            part_o[...] = part.astype(bf16)
            if x is not None:
                send(part_o)
                refs[4][0:1, :] = jnp.sum(part * hat, 0, keepdims=True)
                refs[4][1:2, :] = jnp.sum(part, 0, keepdims=True)

        ins = [dq] + list(kv_parts)
        outs = [((R, 3 * A), bf16), ((R, 3 * A), bf16, FAR), ((R, D), bf16, FAR), ((2, 3 * A), f32)]
        if x is not None:
            ins.append(Far(x))
            outs.append(((2, D), f32))
        return run(kernel, ins, outs, weight_scratch(z.a_cols), w, scal, "project_back", 4)

    def proj_grads(scal, n1, n1_r, dp, dp_r, g1, g1_r, o, o_r, small):
        flat = [a for row in small for a in row]
        half = M // 2

        def kernel(scal_r, n_r, nr_r, p_r, pr_r, g_r, gr_r, o_i, or_i, *refs):
            parts, outs, all_s = refs[: len(flat)], refs[len(flat) : -1], refs[-1]
            first = mm(n_r[...], p_r[...], TN) + mm(nr_r[...], pr_r[...], TN)
            second = mm(g_r[...], o_i[...], TN) + mm(gr_r[...], or_i[...], TN)
            both = jnp.concatenate([first.astype(bf16), second.astype(bf16)], 1)
            all_s[:, :M, :] = both.reshape(S, M, z.a_cols)
            wide, units, heads = [], [], []
            for l in range(L):
                pre, mid, last, up, qv = (r[...] for r in parts[5 * l : 5 * l + 5])
                wide += [pre[0:1], mid[0:1], pre[1:2], mid[1:3], last]
                units.append(up)
                heads.append(qv)
            wide = jnp.concatenate(wide + [jnp.zeros((TAIL - 6 * L, D), f32)], 0)
            pad = TAIL - 2 * L
            units = jnp.concatenate(units + [jnp.zeros((pad, F), f32)], 0).astype(bf16)
            heads = jnp.concatenate(heads + [jnp.zeros((pad, 3 * A), f32)], 0)
            part = 2 * HD // S
            for t in range(S):
                side, place = divmod(t, S // 2)
                cuts = []
                for h in range(H):
                    at = side * 2 * A + h * HD + place * part
                    cuts.append(heads[:, at : at + part])
                up = mm(units, spread(t, S, F), NT)
                rest = jnp.zeros((TAIL, z.a_cols - u_at - F // S), f32)
                all_s[t, M:, :] = jnp.concatenate(
                    [wide[:, t * M : (t + 1) * M]] + cuts + [up, rest], 1
                ).astype(bf16)
            if S == 4:
                outs[3][...] = all_s[scal_r[12], :half, :]
                outs[4][...] = all_s[scal_r[12], half:, :]
                send(outs[3], outs[4])
                for o_, at in zip(outs[:3], (9, 11, 10)):
                    o_[...] = all_s[scal_r[at]]
            else:
                outs[0][...] = all_s[...]

        block = (M + TAIL, z.a_cols)
        outs = [((S,) + block, bf16, FAR)]
        if S == 4:
            outs = [(block, bf16, FAR)] * 3
            outs += [((half, z.a_cols), bf16, FAR), ((M + TAIL - half, z.a_cols), bf16, FAR)]
        return run(
            kernel,
            [Far(n1), Far(n1_r), dp, Far(dp_r), Far(g1), Far(g1_r), Far(o), Far(o_r)] + [Far(a) for a in flat],
            outs,
            [pltpu.VMEM((S,) + block, bf16)],
            scalars=scal,
            name="project_grads",
            us=3,
        )

    def own_grads(n1, n1_r, dp, dp_r, g1, g1_r, o, o_r):
        def kernel(n_r, nr_r, p_r, pr_r, g_r, gr_r, o_i, or_i, out):
            first = mm(n_r[...], p_r[...], TN) + mm(nr_r[...], pr_r[...], TN)
            second = mm(g_r[...], o_i[...], TN) + mm(gr_r[...], or_i[...], TN)
            both = jnp.concatenate([first.astype(bf16), second.astype(bf16)], 1)
            out[...] = both.reshape(S, M, z.a_cols)

        return run(
            kernel,
            [Far(n1), Far(n1_r), dp, Far(dp_r), Far(g1), Far(g1_r), Far(o), Far(o_r)],
            [((S, M, z.a_cols), bf16, FAR)],
            name="own_grads",
            us=3,
        )[0]

    def pass_on(up, down, low, high):
        half = M // 2

        def kernel(up_r, down_r, low_r, high_r, up_o, down_o):
            up_o[:half, :] = (up_r[:half, :].astype(f32) + low_r[...].astype(f32)).astype(bf16)
            up_o[half:, :] = up_r[half:, :]
            send(up_o)
            down_o[:half, :] = down_r[:half, :]
            down_o[half:, :] = (down_r[half:, :].astype(f32) + high_r[...].astype(f32)).astype(bf16)

        return run(
            kernel,
            [Far(up), Far(down), Far(low), Far(high)],
            [((M + TAIL, z.a_cols), bf16, FAR)] * 2,
            name="pass_on",
        )

    def join_rows(scal, mine, theirs):
        def kernel(scal_r, a, b, o):
            start = pl.multiple_of(scal_r[8] * R, 16)
            o[pl.ds(start, R), :] = a[...]
            o[pl.ds(pl.multiple_of(R - start, 16), R), :] = b[...]

        return run(kernel, [Far(mine), Far(theirs)], [((2 * R, D), bf16, FAR)], scalars=scal, name="join_rows")[0]

    def sum_blocks(own, others):
        def kernel(own_r, a_r, b_r, o):
            o[...] = (own_r[...].astype(f32) + a_r[...].astype(f32) + b_r[...].astype(f32)).astype(bf16)

        return run(
            kernel,
            [Far(a) for a in [own] + others],
            [((M + TAIL, z.a_cols), bf16, FAR)],
            name="sum_blocks",
        )[0]

    def feed_out(pairs):
        def kernel(*refs):
            up_o, down_o = refs[-2:]
            for l in range(L):
                total = refs[2 * l][...].astype(f32) + refs[2 * l + 1][...].astype(f32)
                up_o[l] = total[:, :F]
                down_o[l] = total[:, F:]

        return run(
            kernel,
            [Far(a) for p in pairs for a in p],
            [((L, M, F), f32, FAR), ((L, M, F), f32, FAR)],
            name="feed_out",
        )

    def proj_out(pairs):
        def kernel(*refs):
            qkv_o, out_o = refs[-2:]
            for l in range(L):
                total = refs[2 * l][...].astype(f32) + refs[2 * l + 1][...].astype(f32)
                if l == 0:
                    total = total[:M]
                for h in range(H):
                    cuts = [total[:, i * A + h * HD : i * A + (h + 1) * HD] for i in range(3)]
                    qkv_o[l, h] = jnp.concatenate(cuts, 1)
                out_o[l] = total[:, 3 * A :].T
        return run(
            kernel,
            [Far(a) for p in pairs for a in p],
            [((L, H, M, 3 * HD), f32, FAR), ((L, A, M), f32, FAR)],
            name="project_out",
        )

    def small_sum(mine, theirs):
        def kernel(a_r, b_r, o):
            o[...] = a_r[M:, :].astype(f32) + b_r[M:, :].astype(f32)

        return run(kernel, [Far(mine), Far(theirs)], [((TAIL, z.a_cols), f32, FAR)], name="small_sum")[0]

    def small_out(scal, mine, x_side, core_side, far_side):
        def kernel(scal_r, a_r, x_r, c_r, f_r, qvb_o, upb_o, gain_o, shift_o):
            both = a_r[...] + c_r[...]
            other = x_r[...] + f_r[...]
            odd = scal_r[8] == 1
            part, unit = 2 * HD // S, 64 // S
            for l in range(L):
                rows = both[6 * l : 6 * l + 6, :M]
                first, third = rows[0:1], rows[2:3]
                if l == 0:
                    first, third = first + other[0:1, :M], third + other[2:3, :M]
                gain_o[l] = jnp.concatenate([first, rows[1:2]], 0)
                shift_o[l] = jnp.concatenate([third, rows[3:6]], 0)
                bias = jnp.where(odd, both[2 * l + 1 : 2 * l + 2], both[2 * l : 2 * l + 1])
                for h in range(H):
                    qvb_o[h, l : l + 1, :] = bias[:, q_at + h * part : q_at + (h + 1) * part]
                for r in range(F // 64):
                    upb_o[r, l : l + 1, :] = bias[:, u_at + r * unit : u_at + (r + 1) * unit]

        return run(
            kernel,
            [Far(mine), Far(x_side), Far(core_side), Far(far_side)],
            [
                ((H, L, 2 * HD // S), f32),
                ((F // 64, L, 64 // S), f32),
                ((L, 2, M), f32),
                ((L, 4, M), f32),
            ],
            scalars=scal,
            name="small_out",
        )

    def input_back(x, dy, pa, pb, vec):
        def kernel(x_r, dy_r, pa_r, pb_r, vec_r, o, sums_o):
            dn = pa_r[...].astype(f32) + pb_r[...].astype(f32)
            dx, dgain, dshift = ln_back(x_r[...].astype(f32), vec_r[0:1, :], dn)
            o[...] = (dy_r[...] + dx).astype(bf16)
            sums_o[0:1, :] = dgain
            sums_o[1:2, :] = dshift

        return run(kernel, [Far(x), Far(dy), Far(pa), Far(pb), vec], [((R, D), bf16, FAR), ((2, D), f32)], name="input_back")

    return dict(locals())


def local(mesh):
    def fn(frames, cotangent, w_qkv, qv_bias, w_out, w_up, up_bias, w_down, norm_gains, shifts):
        z = Sizes(mesh, frames, w_qkv, w_up)
        assert frames.shape[0] == 1
        k = make(z)
        L, m, R, D, A, F, H, HD, S = z.layers, z.m, z.rows, z.width, z.att, z.hidden, z.heads, z.hd, z.shards
        core = lax.axis_index("tc")
        scal = ring_scalars(S)

        def part_a(l, *then):
            qkv = after(w_qkv[l], *then).reshape(m, H, 3, HD).transpose(0, 2, 1, 3).reshape(m, 3 * A)
            return jnp.concatenate([qkv, after(w_out[l], *then).reshape(A, m).T], -1)

        def part_b(l, *then):
            return jnp.concatenate([after(w_up[l], *then), after(w_down[l], *then).T], -1)

        message = k["pack_first"](
            w_qkv[0], w_out[0].reshape(A, m), qv_bias, up_bias, norm_gains, shifts
        )
        w_a = [Pieces(message, TAIL) if S == 4 else Gathered(message, S, TAIL)]
        w_b = [Gathered(after(part_b(0, message), *w_a[0].arrays[1:4]), S)]

        def my_rows(x):
            return lax.dynamic_slice_in_dim(x.reshape(2 * R, D), core * R, R, 0)

        kept = []
        x = my_rows(frames)
        for layer in range(L):
            if layer == 0:
                n1, q, kv, vec, qb, tails = k["proj"](scal, x, 0, w_a[0])
            else:
                n1, q, kv, x = k["proj"](scal, after(y, *hid[1:]), layer, w_a[layer], (vec, qb), (part, x_swap(part)))
            far = y_swap(kv)
            near = core_swap(kv)
            if layer + 1 < L:
                next_a, next_b = part_a(layer + 1, n1), part_b(layer + 1, n1)
            acc = k["attend_near"](q, (kv, near))
            kvs = (kv, near, far, core_swap(after(far, acc)))
            o0, o1, qa, o_own, o_snd, att_part = k["attend_far"](scal, q, kvs[2:], acc, w_a[layer])
            far = x_swap(att_part)
            n1_r, o_rcv = core_swap(n1), core_swap(o_snd)
            x = after(x, n1_r, o_rcv)
            if layer + 1 < L:
                w_a.append(Gathered(after(next_a, kvs[1]), S))
                w_b.append(Gathered(after(next_b, att_part), S))
            y, n2, *hid_gp, part = k["feed"](
                scal, x, att_part, far, vec, tails, layer, w_b[layer]
            )
            n2_r, hid_r, gp = core_swap(n2), core_swap(hid_gp[1]), hid_gp[2:]
            hid = (hid_gp[0], hid_r, n2_r)
            kept.append((x, n1, n1_r, kvs, qa, (o0, o1), o_own, o_rcv, y, n2, hid, gp))

        def whole_rows(mine):
            return k["join_rows"](scal, mine, core_swap(mine))[None]

        def scatter(grad):
            return lax.psum_scatter(grad.reshape(D, -1), "shard", scatter_dimension=0, tiled=True)

        y_last, part_last = y, part
        g = my_rows(cotangent)
        wide, d_qv, d_up = [None] * L, [None] * L, [None] * L
        sum_a, sum_b = [None] * L, [None] * L
        before = None
        for layer in reversed(range(L)):
            x, n1, n1_r, kvs, qa, os, o_own, o_rcv, y, n2, hid, gp = kept[layer]
            if before is None:
                swap_b, du, part, sum_g2 = k["feed_back"](scal, g, gp, layer, w_b[layer])
            else:
                gp = [after(gp[0], grad_a), gp[1]]
                swap_b, du, part, sum_g2, g, pre = k["feed_back"](scal, None, gp, layer, w_b[layer], before)
                wide[layer + 1] = [pre] + wide[layer + 1]
            far = x_swap(part)
            grad_b, d_up[layer] = k["feed_grads"](
                scal, n2, hid[2], hid[0], hid[1], swap_b, core_swap(swap_b), du
            )
            y = after(y, grad_b)
            if before is not None:
                sum_b[layer + 1] = (part_b_sum, y_swap(after(part_b_sum, part)))
                y = after(y, sum_b[layer + 1][1])
            if layer > 0:
                part_b_sum = scatter(after(grad_b, far))
            dy, g1, da, mid = k["middle_back"](
                scal, y, g, part, far, vec, os[0], os[1], layer, w_a[layer]
            )
            if layer == 0:
                part_b_sum = scatter(after(grad_b, da))
            g1_r = core_swap(g1)
            dqt, own, snd = k["attend_back"](qa, kvs[2:], da)
            cross = k["cross_sum"](own, core_swap(snd))
            dqt = after(dqt, cross, g1_r, *([part_a_sum] if layer == 0 else []))
            cross = y_swap(cross)
            dq, own, snd = k["attend_back"](qa, kvs[:2], da, dqt)
            snd = after(snd, cross)
            kv_parts = (own, core_swap(snd), cross)
            dp, dp_snd, part, d_qv[layer], *pre = k["proj_back"](
                scal, dq, kv_parts, layer, w_a[layer], *([x] if layer == 0 else [])
            )
            far = x_swap(part)
            swaps = (n1, n1_r, dp, core_swap(dp_snd), g1, g1_r, o_own, o_rcv)
            if layer > 0:
                grad_a = k["own_grads"](*swaps)
                part_a_sum = scatter(after(grad_a, far))
            else:
                sum_a[1] = (part_a_sum, y_swap(after(part_a_sum, part)))
                wide[0] = pre + [mid, sum_g2]
                small = [wide[l] + [d_up[l], d_qv[l]] for l in range(L)]
                blocks = k["proj_grads"](scal, *swaps, small)
            wide[layer] = pre + [mid, sum_g2]
            before = (x, dy, part, far, vec)
        grad_rows, _ = k["input_back"](x, after(dy, blocks[0]), part, far, vec)
        if S == 4:
            hops = [lax.ppermute(b, "shard", ring(s)) for b, s in zip(blocks[3:], (1, 3))]
            up, down = k["pass_on"](after(blocks[1], grad_rows, sum_a[1][1]), blocks[2], *hops)
            ready = up
            others = [lax.ppermute(up, "shard", ring(1)), lax.ppermute(down, "shard", ring(3))]
        else:
            ready = blocks[0]
        part_b_sum = after(part_b_sum, ready)
        sum_b[0] = (part_b_sum, y_swap(part_b_sum))
        far_last = x_swap(after(part_last, ready))
        frames_grad = whole_rows(grad_rows)
        block = after(blocks[0], sum_b[0][1], frames_grad)
        if S == 4:
            mine = k["sum_blocks"](block, others)
        else:
            mine = lax.psum_scatter(block, "shard", scatter_dimension=0, tiled=True)[0]
        theirs = y_swap(mine)
        sum_a[0] = (mine, theirs)
        out_frames = whole_rows(k["finish"](y_last, part_last, after(far_last, mine), vec)[0])
        outs_up, outs_down = k["feed_out"]([sum_b[0], (after(sum_b[1][0], mine), sum_b[1][1])])
        tiny = k["small_sum"](after(mine, outs_up, out_frames), theirs)
        tiny_x = x_swap(tiny)
        tiny_c, tiny_f = core_swap(tiny), core_swap(tiny_x)
        outs_qkv, outs_out = k["proj_out"]([(after(mine, tiny), theirs), sum_a[1]])
        g_qvb, g_upb, g_gains, g_shifts = k["small_out"](
            scal, after(tiny, outs_qkv), tiny_x, tiny_c, tiny_f
        )
        return (
            out_frames,
            frames_grad,
            outs_qkv.transpose(0, 2, 1, 3),
            g_qvb.transpose(1, 0, 2),
            outs_out.reshape(L, H, HD, m),
            outs_up,
            g_upb.transpose(1, 0, 2),
            outs_down.transpose(0, 2, 1),
            g_gains,
            g_shifts,
        )

    return fn


def solution(mesh):
    assert mesh.axis_names == ("shard", "ctx", "tp") and mesh.shape["tp"] == 4 and mesh.shape["ctx"] == 2
    split = Mesh(mesh.devices.reshape(mesh.shape["shard"], 2, 2, 2), ("shard", "ctx", "tx", "tc"))
    tp = ("tx", "tc")
    specs = (
        P("shard", "ctx", None),
        P("shard", "ctx", None),
        P(None, "shard", tp, None),
        P(None, tp, "shard"),
        P(None, tp, None, "shard"),
        P(None, "shard", tp),
        P(None, tp, "shard"),
        P(None, tp, "shard"),
        P(None, None, "shard"),
        P(None, None, "shard"),
    )
    return jax.shard_map(local(split), mesh=split, in_specs=specs, out_specs=specs, check_vma=False)
```

```python
import math

import jax
import jax.numpy as jnp
from jax import lax
from jax.experimental import pallas as pl
from jax.experimental.pallas import tpu as pltpu
from jax.sharding import Mesh
from jax.sharding import PartitionSpec as P

f32 = jnp.float32
bf16 = jnp.bfloat16
EPSILON = 1e-05
NN = (((1,), (0,)), ((), ()))
NT = (((1,), (1,)), ((), ()))
TN = (((0,), (0,)), ((), ()))
VMEM_MIB = {
    "attend_far": 13,
    "attend_near": 10,
    "attend_back": 14,
    "feed": 16,
    "feed_back": 16,
    "feed_grads": 12,
    "own_grads": 9,
    "feed_out": 7.6,
    "finish": 6,
    "input_back": 10,
    "middle_back": 11,
    "pack_first": 6,
    "pair_grads": 9,
    "project": 9.5,
    "project_back": 9.5,
    "project_grads": 13,
    "project_out": 5,
}
WIDE = 128
TAIL = 16
COST = 500_000_000


def mm(a, b, dims=NN):
    return lax.dot_general(a, b, dims, preferred_element_type=f32)


def core_swap(x):
    return lax.ppermute(x, "tc", [(0, 1), (1, 0)])


def x_swap(x):
    return lax.ppermute(x, "tx", [(0, 1), (1, 0)])


def y_swap(x):
    return lax.ppermute(x, "ctx", [(0, 1), (1, 0)])


def after(x, *others):
    return lax.optimization_barrier((x,) + others)[0]


def ring(shift):
    return [(i, (i + shift) % 4) for i in range(4)]


def ring_scalars(shards):
    me = lax.axis_index("shard").astype(jnp.int32)
    zero = jnp.int32(0)
    order = [me, (me + shards - 1) % shards, (me + 1) % shards, (me + 2) % shards]
    return jnp.stack([zero] * 8 + [lax.axis_index("tc").astype(jnp.int32)] + order + [zero] * 3)


class Pieces:
    def __init__(self, x, tail=0):
        self.rows = x.shape[0] - tail
        self.mine = [x] + [lax.ppermute(x, "shard", ring(s)) for s in (1, 3, 2)]
        self.arrays = self.mine + [core_swap(p) for p in self.mine]

    def copies(self, scal, refs, columns, dest, sems):
        out = []
        for k, ref in enumerate(refs):
            slot = scal[8] if k < 4 else 1 - scal[8]
            to = dest.at[slot, scal[9 + k % 4]]
            out.append(pltpu.make_async_copy(ref.at[pl.ds(0, self.rows), columns], to, sems.at[k]))
        return out

    def tails(self, scal, refs, dest, sems):
        out = []
        for k, ref in enumerate(refs):
            slot = scal[8] if k < 4 else 1 - scal[8]
            to = dest.at[slot, scal[9 + k % 4]]
            out.append(pltpu.make_async_copy(ref.at[pl.ds(self.rows, TAIL), :], to, sems.at[k]))
        return out


class Gathered:
    def __init__(self, x, shards, tail=0):
        self.rows = x.shape[0] - tail
        whole = lax.all_gather(x, ("shard", "tc"), axis=0, tiled=False)
        self.arrays = [whole.reshape((shards, 2) + x.shape)]

    def copies(self, scal, refs, columns, dest, sems):
        ref = refs[0]
        return [
            pltpu.make_async_copy(ref.at[:, c, pl.ds(0, self.rows), columns], dest.at[c], sems.at[c])
            for c in range(2)
        ]

    def tails(self, scal, refs, dest, sems):
        ref = refs[0]
        return [
            pltpu.make_async_copy(ref.at[:, c, pl.ds(self.rows, TAIL), :], dest.at[c], sems.at[c])
            for c in range(2)
        ]


def vmem():
    return pl.BlockSpec(memory_space=pltpu.VMEM)


class Far:
    def __init__(self, array):
        self.array = array


class Reading:
    def __init__(self, buffer, copy):
        self.buffer, self.copy, self.waited = buffer, copy, False

    def need(self):
        if not self.waited:
            self.copy.wait()
            self.waited = True
        return self.buffer

    def __getitem__(self, index):
        return self.need()[index]

    @property
    def shape(self):
        return self.buffer.shape


class Writing:
    def __init__(self, buffer, copy):
        self.buffer, self.copy, self.sent = buffer, copy, False

    def __setitem__(self, index, value):
        self.buffer[index] = value

    @property
    def at(self):
        return self.buffer.at

    def send(self):
        if not self.sent:
            self.copy.start()
            self.sent = True


def send(*refs):
    for r in refs:
        if isinstance(r, Writing):
            r.send()


def need(*refs):
    for r in refs:
        if isinstance(r, Reading):
            r.need()


FAR = "far"


def run(kernel, ins, outs, scratch=(), w=None, scalars=None, name=None, us=1.0):
    pieces = [] if w is None else w.arrays
    n_in, n_out, n_pieces = len(ins), len(outs), len(pieces)
    far_in = [i for i, a in enumerate(ins) if isinstance(a, Far)]
    far_out = [i for i, o in enumerate(outs) if len(o) == 3]
    any_space = pl.BlockSpec(memory_space=pl.ANY)
    specs, args = [], []
    if scalars is not None:
        specs.append(pl.BlockSpec(memory_space=pltpu.SMEM))
        args.append(scalars)
    for a in ins:
        if isinstance(a, Far):
            specs.append(any_space)
            args.append(pltpu.with_memory_space_constraint(a.array, pltpu.HBM))
        else:
            specs.append(vmem())
            args.append(a)
    for p in pieces:
        specs.append(any_space)
        args.append(pltpu.with_memory_space_constraint(p, pltpu.HBM))
    first = len(args) - n_in - n_pieces
    shapes = [
        pltpu.HBM(o[0], o[1]) if len(o) == 3 else jax.ShapeDtypeStruct(o[0], o[1]) for o in outs
    ]
    buffers = [pltpu.VMEM(ins[i].array.shape, ins[i].array.dtype) for i in far_in]
    buffers += [pltpu.VMEM(outs[i][0], outs[i][1]) for i in far_out]
    sems = [pltpu.SemaphoreType.DMA((len(buffers),))] if buffers else []

    def wrapped(*refs):
        refs = list(refs)
        n_all = len(args) + n_out + len(scratch)
        own, extra = refs[:n_all], refs[n_all:]
        reads, writes = [], []
        for k, i in enumerate(far_in):
            copy = pltpu.make_async_copy(own[first + i], extra[k], extra[-1].at[k])
            copy.start()
            own[first + i] = Reading(extra[k], copy)
            reads.append(own[first + i])
        for k, i in enumerate(far_out):
            k += len(far_in)
            at = len(args) + i
            own[at] = Writing(extra[k], pltpu.make_async_copy(extra[k], own[at], extra[-1].at[k]))
            writes.append(own[at])
        kernel(*own)
        for w in writes:
            w.send()
        for r in reads:
            r.need()
        for w in writes:
            w.copy.wait()

    return pl.pallas_call(
        wrapped,
        out_shape=shapes,
        in_specs=specs,
        out_specs=[any_space if len(o) == 3 else vmem() for o in outs],
        scratch_shapes=list(scratch) + buffers + sems,
        compiler_params=pltpu.CompilerParams(vmem_limit_bytes=int(VMEM_MIB.get(name, 4) * 1024 * 1024)),
        cost_estimate=pl.CostEstimate(flops=int(us * COST), bytes_accessed=1000, transcendentals=0),
        name=name,
    )(*args)


def spread(shard, shards, units):
    part = 64 // shards
    bits, low = part.bit_length() - 1, part - 1
    i = lax.broadcasted_iota(jnp.int32, (units // shards, units), 0)
    j = lax.broadcasted_iota(jnp.int32, (units // shards, units), 1)
    same = ((j >> 6) == (i >> bits)) & ((j & 63) == shard * part + (i & low))
    return jnp.where(same, 1.0, 0.0).astype(bf16)


def start_all(copies):
    for c in copies:
        c.start()


def wait_all(copies):
    for c in copies:
        c.wait()


def ln_parts(x):
    centred = x - jnp.mean(x, -1, keepdims=True)
    inv = lax.rsqrt(jnp.mean(centred * centred, -1, keepdims=True) + EPSILON)
    return centred * inv, inv


def ln_back(x, gain, dn):
    hat, inv = ln_parts(x)
    dhat = dn * gain
    dx = inv * (
        dhat
        - jnp.mean(dhat, -1, keepdims=True)
        - hat * jnp.mean(dhat * hat, -1, keepdims=True)
    )
    return dx, jnp.sum(dn * hat, 0, keepdims=True), jnp.sum(dn, 0, keepdims=True)


def split3(v):
    a = v.astype(bf16)
    r = v - a.astype(f32)
    b = r.astype(bf16)
    c = (r - b.astype(f32)).astype(bf16)
    return a, b, c


def beside(wide, column):
    a, b, c = split3(column)
    rows, size = wide.shape[0], wide.shape[1]
    return jnp.concatenate([wide, a, b, c, jnp.zeros((rows, WIDE - size - 3), bf16)], 1)


class Sizes:
    def __init__(self, mesh, frames, w_qkv, w_up):
        self.shards = mesh.shape["shard"]
        self.layers = w_qkv.shape[0]
        self.width = frames.shape[-1]
        self.rows = frames.shape[1] // 2
        self.heads = w_qkv.shape[2]
        self.hd = w_qkv.shape[3] // 3
        self.att = self.heads * self.hd
        self.hidden = w_up.shape[2]
        self.m = w_qkv.shape[1]
        self.a_cols = 4 * self.att
        self.b_cols = 2 * self.hidden


def make(z):
    R, D, A, H, HD, F = z.rows, z.width, z.att, z.heads, z.hd, z.hidden
    L, S, M = z.layers, z.shards, z.m
    coef = HD ** (-0.5) / math.log(2.0)
    scale = HD ** (-0.5)
    dma = pltpu.SemaphoreType.DMA
    q_at, u_at = M, M + 2 * A // S

    def weight_scratch(columns):
        return [pltpu.VMEM((2, S, M, columns), bf16), dma((8,))]

    def weight(w_s, c, start, stop):
        return w_s[c, :, :, start:stop].reshape(D, stop - start)

    def pack_first(w_qkv, w_out, qv_bias, up_bias, norm_gains, shifts):
        nq, nu = 2 * HD // S, 64 // S

        def kernel(w_r, o_r, qv_r, up_r, g_r, s_r, out):
            for side in range(3):
                cuts = [w_r[0, h][:, side * HD : (side + 1) * HD] for h in range(H)]
                out[:M, side * A : (side + 1) * A] = jnp.concatenate(cuts, 1)
            out[:M, 3 * A :] = o_r[0].astype(f32).T.astype(bf16)
            vecs = []
            for l in range(L):
                vecs += [g_r[l].astype(f32), s_r[l].astype(f32)]
            vecs = jnp.concatenate(vecs + [jnp.zeros((TAIL - 6 * L, M), f32)], 0)
            rows = []
            for l in range(L):
                cuts = [qv_r[h].astype(f32)[l : l + 1, :] for h in range(H)]
                cuts += [up_r[r].astype(f32)[l : l + 1, :] for r in range(F // 64)]
                rows.append(jnp.concatenate(cuts, 1))
            rows = jnp.concatenate(rows + [jnp.zeros((TAIL - L, H * nq + F // 64 * nu), f32)], 0)
            rest = jnp.zeros((TAIL, z.a_cols - M - rows.shape[1]), f32)
            out[M:, :] = jnp.concatenate([vecs, rows, rest], 1).astype(bf16)

        return run(
            kernel,
            [
                Far(a)
                for a in (
                    w_qkv.transpose(0, 2, 1, 3),
                    w_out.reshape(L, A, M),
                    qv_bias.transpose(1, 0, 2),
                    up_bias.transpose(1, 0, 2),
                    norm_gains,
                    shifts,
                )
            ],
            [((M + TAIL, z.a_cols), bf16, FAR)],
            name="pack_first",
        )[0]

    def proj(scal, x, layer, w, biases=None, prev=None):
        first = biases is None
        n = len(w.arrays)
        part = 2 * HD // S

        def kernel(*refs):
            it = iter(refs)
            scal_r, x_r = next(it), next(it)
            if not first:
                vec_r, qb_r, pa_r, pb_r = (next(it) for _ in range(4))
            piece_r = [next(it) for _ in range(n)]
            n_o, q_o, kv_o = (next(it) for _ in range(3))
            if first:
                vec_r, qb_r, tail_o = (next(it) for _ in range(3))
            else:
                x_o = next(it)
            w_s, sems = next(it), next(it)
            if first:
                tail_sems = next(it)
                tails = w.tails(scal_r, piece_r, tail_o, tail_sems)
                start_all(tails)
            copies = w.copies(scal_r, piece_r, pl.ds(0, z.a_cols), w_s, sems)
            start_all(copies)
            xv = x_r[...].astype(f32)
            if not first:
                at = 6 * (layer - 1) + 5
                xv = xv + (pa_r[...].astype(f32) + pb_r[...].astype(f32) + vec_r[at : at + 1, :])
                x_o[...] = xv
                send(x_o)
            hat, _ = ln_parts(xv)
            if first:
                wait_all(tails)
                vec_r[...] = jnp.concatenate([tail_o[0, t][:, :M] for t in range(S)], 1).astype(f32)
                for l in range(L):
                    for p in range(2):
                        rows = [tail_o[p, t].astype(f32)[l : l + 1, q_at:u_at] for t in range(S)]
                        seq = []
                        for side in range(2):
                            for h in range(H):
                                seq += [
                                    rows[t][:, h * part : (h + 1) * part]
                                    for t in range(side * S // 2, (side + 1) * S // 2)
                                ]
                            if side == 0:
                                seq.append(jnp.zeros((1, A), f32))
                        qb_r[2 * l + p : 2 * l + p + 1, :] = jnp.concatenate(seq, 1)
            g = 6 * layer
            nv = (hat * vec_r[g : g + 1, :] + vec_r[g + 2 : g + 3, :]).astype(bf16)
            n_o[...] = nv
            send(n_o)
            wait_all(copies)
            both = []
            for e in range(2):
                b = 2 * layer + e
                p = (mm(nv, weight(w_s, e, 0, 3 * A)) + qb_r[b : b + 1, :]).astype(bf16)
                kv_o[:, e * 2 * A : (e + 1) * 2 * A] = p[:, A:]
                both.append(p[:, :A])
            send(kv_o)
            q_o[...] = jnp.concatenate(both, 1)

        ins = [Far(x)] + ([] if first else list(biases) + [Far(prev[0]), prev[1]])
        outs = [((R, D), bf16, FAR), ((R, 2 * A), bf16), ((R, 4 * A), bf16, FAR)]
        scratch = weight_scratch(z.a_cols)
        if first:
            outs += [((TAIL, D), f32), ((2 * L, 3 * A), f32), ((2, S, TAIL, z.a_cols), bf16)]
            scratch += [dma((8,))]
        else:
            outs += [((R, D), f32, FAR)]
        return run(kernel, ins, outs, scratch, w, scal, "project", 3.5)

    def aug(block, offset, fill):
        return jnp.concatenate([block[:, offset : offset + HD], fill], 1)

    def head_lanes(j):
        e, h = divmod(j, H)
        return j * HD, e * 2 * A + h * HD, e * 2 * A + A + h * HD

    def load_heads(kv_refs, k_s, v_s):
        ones = jnp.ones((R, HD), bf16)
        for b, ref in enumerate(kv_refs):
            blk = ref[...]
            for j in range(2 * H):
                _, k_at, v_at = head_lanes(j)
                k_s[j, b * R : (b + 1) * R, :] = aug(blk, k_at, ones)
                v_s[j, b * R : (b + 1) * R, :] = aug(blk, v_at, ones)

    def attend_near(q, kvs):
        K = 2 * R

        def kernel(q_r, kv0, kv1, acc_o, q_s, k_s, v_s):
            zeros = jnp.zeros((R, HD), bf16)
            for j in range(2 * H):
                q_s[j] = aug(q_r[...], j * HD, zeros)
            load_heads((kv0, kv1), k_s, v_s)

            def head(j, carry):
                s = mm(q_s[j], k_s[j], NT)
                top = jnp.max(s, -1, keepdims=True)
                oe = mm(jnp.exp2((s - top) * coef).astype(bf16), v_s[j])
                acc_o[j] = jnp.concatenate(
                    [oe[:, : HD + 1], top, jnp.zeros((R, WIDE - HD - 2), f32)], 1
                )
                return carry

            lax.fori_loop(0, 2 * H, head, 0)

        return run(
            kernel,
            [q] + list(kvs),
            [((2 * H, R, WIDE), f32)],
            [pltpu.VMEM((2 * H, R, WIDE), bf16)] + [pltpu.VMEM((2 * H, K, WIDE), bf16)] * 2,
            name="attend_near",
            us=6,
        )[0]

    def attend_far(scal, q, kvs, acc, w):
        K = 2 * R
        n = len(w.arrays)

        def kernel(scal_r, q_r, kv2, kv3, acc_r, *refs):
            piece_r = refs[:n]
            o0_o, o1_o, qa_o, own_o, snd_o, part_o, q_s, k_s, v_s, o_s, w_s, sems = refs[n:]
            copies = w.copies(scal_r, piece_r, pl.ds(z.a_cols - 256, 256), w_s, sems)
            start_all(copies)
            zeros = jnp.zeros((R, HD), bf16)
            for j in range(2 * H):
                q_s[j] = aug(q_r[...], j * HD, zeros)
            load_heads((kv2, kv3), k_s, v_s)

            def head(j, carry):
                s = mm(q_s[j], k_s[j], NT)
                old = acc_r[j]
                old_top = old[:, HD + 1 : HD + 2]
                top = jnp.maximum(jnp.max(s, -1, keepdims=True), old_top)
                oe = mm(jnp.exp2((s - top) * coef).astype(bf16), v_s[j])
                oe = oe + old * jnp.exp2((old_top - top) * coef)
                total = oe[:, HD : HD + 1]
                o_s[j] = (oe[:, :HD] / total).astype(bf16)
                lse = top + jnp.log2(total) * (1.0 / coef)
                qa_o.buffer[j] = beside(q_s[j][:, :HD], -lse)
                return carry

            lax.fori_loop(0, 2 * H, head, 0)
            send(qa_o)
            o0 = jnp.concatenate([o_s[j] for j in range(H)], 1)
            o1 = jnp.concatenate([o_s[H + j] for j in range(H)], 1)
            wait_all(copies)
            part = mm(o0, weight(w_s, 0, 256 - A, 256), NT) + mm(o1, weight(w_s, 1, 256 - A, 256), NT)
            part_o[...] = part.astype(bf16)
            send(part_o)
            odd = scal_r[8] == 1
            o0_o[...] = o0
            o1_o[...] = o1
            own_o[...] = jnp.where(odd, o1, o0)
            snd_o[...] = jnp.where(odd, o0, o1)

        return run(
            kernel,
            [q] + list(kvs) + [acc],
            [((R, A), bf16, FAR)] * 2
            + [((2 * H, R, WIDE), bf16, FAR)]
            + [((R, A), bf16, FAR)] * 2
            + [((R, D), bf16, FAR)],
            [pltpu.VMEM((2 * H, R, WIDE), bf16)]
            + [pltpu.VMEM((2 * H, K, WIDE), bf16)] * 2
            + [pltpu.VMEM((2 * H, R, HD), bf16)]
            + weight_scratch(256),
            w,
            scal,
            "attend_far",
            8,
        )

    def feed(scal, x, pa, pb, vec, tails, layer, w):
        n = len(w.arrays)
        g = 6 * layer

        def kernel(scal_r, x_r, pa_r, pb_r, vec_r, tail_r, *refs):
            piece_r = refs[:n]
            y_o, n_o, *hid_gp, part_o, w_s, sems = refs[n:]
            copies = w.copies(scal_r, piece_r, pl.ds(0, 2 * F), w_s, sems)
            start_all(copies)
            y = x_r[...].astype(f32) + (
                pa_r[...].astype(f32) + pb_r[...].astype(f32) + vec_r[g + 3 : g + 4, :]
            )
            y_o[...] = y
            send(y_o)
            hat, _ = ln_parts(y)
            nv = (hat * vec_r[g + 1 : g + 2, :] + vec_r[g + 4 : g + 5, :]).astype(bf16)
            n_o[...] = nv
            send(n_o)
            bias = [None, None]
            for t in range(S):
                e = spread(t, S, F)
                for s in range(2):
                    add = mm(tail_r[s, t][:, u_at : u_at + F // S], e)
                    bias[s] = add if t == 0 else bias[s] + add
            part, hiddens = None, []
            for s in range(2):
                copies[s].wait()
                u = mm(nv, weight(w_s, s, 0, F)) + bias[s][layer : layer + 1, :]
                cdf = 0.5 * (1.0 + lax.erf(u * (0.5**0.5)))
                pdf = jnp.exp(-0.5 * u * u) * (1.0 / math.sqrt(2.0 * math.pi))
                hidden = (u * cdf).astype(bf16)
                hid_gp[2 + s][...] = (cdf + u * pdf).astype(bf16)
                send(hid_gp[2 + s])
                hiddens.append(hidden)
                t = mm(hidden, weight(w_s, s, F, 2 * F), NT)
                part = t if part is None else part + t
            part_o[...] = part.astype(bf16)
            send(part_o)
            odd = scal_r[8] == 1
            hid_gp[0][...] = jnp.where(odd, hiddens[1], hiddens[0])
            hid_gp[1][...] = jnp.where(odd, hiddens[0], hiddens[1])

        outs = [
            ((R, D), f32, FAR),
            ((R, D), bf16, FAR),
            ((R, F), bf16, FAR),
            ((R, F), bf16, FAR),
            ((R, F), bf16, FAR),
            ((R, F), bf16, FAR),
            ((R, D), bf16, FAR),
        ]
        return run(
            kernel, [Far(x), Far(pa), pb, vec, tails], outs, weight_scratch(2 * F), w, scal, "feed", 6
        )

    def finish(y, pa, pb, vec):
        at = 6 * (L - 1) + 5

        def kernel(y_r, pa_r, pb_r, vec_r, o):
            v = y_r[...] + (pa_r[...].astype(f32) + pb_r[...].astype(f32) + vec_r[at : at + 1, :])
            o[...] = v.astype(bf16)

        return run(kernel, [Far(y), Far(pa), Far(pb), vec], [((R, D), bf16, FAR)], name="finish")

    def feed_back(scal, grad, gp, layer, w, before=None):
        n = len(w.arrays)
        up = 6 * (layer + 1)

        def kernel(*refs):
            it = iter(refs)
            scal_r = next(it)
            if before is None:
                g_r = next(it)
            else:
                x_r, dy_r, pa_r, pb_r, vec_r = (next(it) for _ in range(5))
            gp_r = (next(it), next(it))
            piece_r = [next(it) for _ in range(n)]
            swap_o, du_o, part_o, sums_o = (next(it) for _ in range(4))
            if before is not None:
                g_o, pre_o = next(it), next(it)
            w_s, sems = next(it), next(it)
            copies = w.copies(scal_r, piece_r, pl.ds(0, 2 * F), w_s, sems)
            start_all(copies)
            if before is None:
                g = g_r[...].astype(f32)
            else:
                dn = pa_r[...].astype(f32) + pb_r[...].astype(f32)
                dx, dgain, dshift = ln_back(x_r[...], vec_r[up : up + 1, :], dn)
                g = dy_r[...] + dx
                g_o[...] = g
                pre_o[0:1, :] = dgain
                pre_o[1:2, :] = dshift
            g2 = g.astype(bf16)
            swap_o[:, :D] = g2
            sums_o[...] = jnp.sum(g2.astype(f32), 0, keepdims=True)
            part, dus = None, []
            for s in range(2):
                copies[s].wait()
                dh = mm(g2, weight(w_s, s, F, 2 * F))
                du = (gp_r[s][...].astype(f32) * dh).astype(bf16)
                dus.append(du)
                t = mm(du, weight(w_s, s, 0, F), NT)
                part = t if part is None else part + t
            part_o[...] = part.astype(bf16)
            send(part_o)
            odd = scal_r[8] == 1
            du_o[...] = jnp.where(odd, dus[1], dus[0])
            swap_o[:, D:] = jnp.where(odd, dus[0], dus[1])

        ins = [grad] if before is None else [Far(b) for b in before[:3]] + list(before[3:])
        ins += [Far(gp[0]), Far(gp[1])]
        outs = [((R, D + F), bf16, FAR), ((R, F), bf16), ((R, D), bf16, FAR), ((1, D), f32)]
        if before is not None:
            outs += [((R, D), f32), ((2, D), f32)]
        return run(kernel, ins, outs, weight_scratch(2 * F), w, scal, "feed_back", 6)

    def blocks_out(scal_r, full, outs):
        if S == 4:
            for o, at in zip(outs, (9, 11, 10, 12)):
                o[...] = full[scal_r[at]]
        else:
            outs[0][...] = full[...]

    def block_shapes(rows, columns):
        return [((rows, columns), bf16, FAR)] * 4 if S == 4 else [((S, rows, columns), bf16, FAR)]

    def feed_grads(scal, n2, n2_r, hid, hid_r, swap, swap_r, du):
        def kernel(scal_r, n_r, nr_r, h_r, hr_r, s_r, sr_r, du_r, g_o, b_o):
            other = sr_r[:, D:]
            g_o[:, :F] = (mm(n_r[...], du_r[...], TN) + mm(nr_r[...], other, TN)).astype(bf16)
            g_o[:, F:] = (mm(s_r[:, :D], h_r[...], TN) + mm(sr_r[:, :D], hr_r[...], TN)).astype(bf16)
            total = jnp.sum(du_r[...].astype(f32), 0, keepdims=True) + jnp.sum(
                other.astype(f32), 0, keepdims=True
            )
            odd = scal_r[8] == 1
            b_o[0:1, :] = jnp.where(odd, 0.0, total)
            b_o[1:2, :] = jnp.where(odd, total, 0.0)

        return run(
            kernel,
            [Far(n2), Far(n2_r), Far(hid), Far(hid_r), Far(swap), Far(swap_r), du],
            [((D, 2 * F), bf16, FAR), ((2, F), f32)],
            scalars=scal,
            name="feed_grads",
            us=3,
        )

    def middle_back(scal, y, g, pa, pb, vec, o0, o1, layer, w):
        n = len(w.arrays)
        gain = 6 * layer + 1

        def kernel(scal_r, y_r, g_r, pa_r, pb_r, vec_r, o0_r, o1_r, *refs):
            piece_r = refs[:n]
            dy_o, g1_o, d_o, sums_o, w_s, sems = refs[n:]
            copies = w.copies(scal_r, piece_r, pl.ds(z.a_cols - 256, 256), w_s, sems)
            start_all(copies)
            dn = pa_r[...].astype(f32) + pb_r[...].astype(f32)
            dx, dgain, dshift = ln_back(y_r[...], vec_r[gain : gain + 1, :], dn)
            dy = g_r[...].astype(f32) + dx
            dy_o[...] = dy
            send(dy_o)
            g1 = dy.astype(bf16)
            g1_o[...] = g1
            send(g1_o)
            sums_o[0:1, :] = dgain
            sums_o[1:2, :] = jnp.sum(g1.astype(f32), 0, keepdims=True)
            sums_o[2:3, :] = dshift
            wait_all(copies)
            for e, o_r in enumerate((o0_r, o1_r)):
                do = mm(g1, weight(w_s, e, 256 - A, 256)).astype(bf16)
                prod = do.astype(f32) * o_r[...].astype(f32)
                for h in range(H):
                    lanes = slice(h * HD, (h + 1) * HD)
                    d_o[e * H + h] = beside(do[:, lanes], -jnp.sum(prod[:, lanes], -1, keepdims=True))

        outs = [((R, D), f32, FAR), ((R, D), bf16, FAR), ((2 * H, R, WIDE), bf16), ((3, D), f32)]
        return run(
            kernel,
            [Far(y), g, Far(pa), pb, vec, Far(o0), Far(o1)],
            outs,
            weight_scratch(256),
            w,
            scal,
            "middle_back",
            4,
        )

    def attend_back(qa, kvs, da, before=None):
        K = 2 * R

        def kernel(qa_r, kv0, kv1, da_r, *refs):
            refs = list(refs)
            if before is not None:
                old_r = refs.pop(0)
            dq_o, e0, e1, k_s, v_s, dk_s, dv_s, *dq_s = refs
            need(qa_r)
            load_heads((kv0, kv1), k_s, v_s)

            def head(j, carry):
                qv = qa_r[j]
                dv_in = da_r[j]
                dqt = None
                for b in range(2):
                    at = slice(b * R, (b + 1) * R)
                    kb = k_s[j, at, :]
                    p = jnp.exp2(mm(kb, qv, NT) * coef)
                    ds = (p * mm(v_s[j, at, :], dv_in, NT)).astype(bf16)
                    dv_s[j, at, :] = mm(p.astype(bf16), dv_in).astype(bf16)
                    dk_s[j, at, :] = (mm(ds, qv) * scale).astype(bf16)
                    t = mm(kb, ds, TN)
                    dqt = t if dqt is None else dqt + t
                if before is None:
                    dq_o[j] = dqt
                else:
                    dq_s[0][j] = ((dqt + old_r[j]).T * scale).astype(bf16)
                return carry

            lax.fori_loop(0, 2 * H, head, 0)
            for b, e_o in ((1, e1), (0, e0)):
                at = slice(b * R, (b + 1) * R)
                cols = []
                for e in range(2):
                    cols += [dk_s[e * H + h, at, :HD] for h in range(H)]
                    cols += [dv_s[e * H + h, at, :HD] for h in range(H)]
                e_o[...] = jnp.concatenate(cols, 1)
                send(e_o)
            if before is not None:
                dq_o[...] = jnp.concatenate([dq_s[0][j][:, :HD] for j in range(2 * H)], 1)

        ins = [Far(qa)] + [Far(a) for a in kvs] + [da] if before is None else [qa] + list(kvs) + [da]
        outs = [((R, 4 * A), bf16), ((R, 4 * A), bf16, FAR)]
        scratch = [pltpu.VMEM((2 * H, K, WIDE), bf16)] * 4
        if before is None:
            outs = [((2 * H, WIDE, R), f32)] + outs
        else:
            ins.append(before)
            outs = [((R, 2 * A), bf16)] + outs
            scratch.append(pltpu.VMEM((2 * H, R, WIDE), bf16))
        return run(kernel, ins, outs, scratch, name="attend_back", us=8)

    def cross_sum(own, theirs):
        def kernel(a, b, o):
            o[...] = (a[...].astype(f32) + b[...].astype(f32)).astype(bf16)

        return run(kernel, [own, theirs], [(own.shape, bf16, FAR)], name="cross_sum")[0]

    def proj_back(scal, dq, kv_parts, layer, w, x=None):
        n = len(w.arrays)

        def kernel(scal_r, q_r, a, p, c, *refs):
            refs = list(refs)
            if x is not None:
                x_r = refs.pop(0)
            piece_r, refs = refs[:n], refs[n:]
            own_o, snd_o, part_o, b_o = refs[:4]
            w_s, sems = refs[-2:]
            copies = w.copies(scal_r, piece_r, pl.ds(0, z.a_cols), w_s, sems)
            start_all(copies)
            both = []
            for e in range(2):
                at = slice(e * 2 * A, (e + 1) * 2 * A)
                total = a[:, at].astype(f32) + p[:, at].astype(f32) + c[:, at].astype(f32)
                both.append(jnp.concatenate([q_r[:, e * A : (e + 1) * A], total.astype(bf16)], 1))
                b_o[e : e + 1, :] = jnp.sum(both[e].astype(f32), 0, keepdims=True)
            odd = scal_r[8] == 1
            own_o[...] = jnp.where(odd, both[1], both[0])
            snd_o[...] = jnp.where(odd, both[0], both[1])
            send(snd_o)
            if x is not None:
                hat, _ = ln_parts(x_r[...].astype(f32))
            wait_all(copies)
            part = mm(both[0], weight(w_s, 0, 0, 3 * A), NT) + mm(both[1], weight(w_s, 1, 0, 3 * A), NT)
            part_o[...] = part.astype(bf16)
            if x is not None:
                send(part_o)
                refs[4][0:1, :] = jnp.sum(part * hat, 0, keepdims=True)
                refs[4][1:2, :] = jnp.sum(part, 0, keepdims=True)

        ins = [dq] + list(kv_parts)
        outs = [((R, 3 * A), bf16), ((R, 3 * A), bf16, FAR), ((R, D), bf16, FAR), ((2, 3 * A), f32)]
        if x is not None:
            ins.append(Far(x))
            outs.append(((2, D), f32))
        return run(kernel, ins, outs, weight_scratch(z.a_cols), w, scal, "project_back", 4)

    def proj_grads(scal, n1, n1_r, dp, dp_r, g1, g1_r, o, o_r, small):
        flat = [a for row in small for a in row]
        half = M // 2

        def kernel(scal_r, n_r, nr_r, p_r, pr_r, g_r, gr_r, o_i, or_i, *refs):
            parts, outs, all_s = refs[: len(flat)], refs[len(flat) : -1], refs[-1]
            first = mm(n_r[...], p_r[...], TN) + mm(nr_r[...], pr_r[...], TN)
            second = mm(g_r[...], o_i[...], TN) + mm(gr_r[...], or_i[...], TN)
            both = jnp.concatenate([first.astype(bf16), second.astype(bf16)], 1)
            all_s[:, :M, :] = both.reshape(S, M, z.a_cols)
            wide, units, heads = [], [], []
            for l in range(L):
                pre, mid, last, up, qv = (r[...] for r in parts[5 * l : 5 * l + 5])
                wide += [pre[0:1], mid[0:1], pre[1:2], mid[1:3], last]
                units.append(up)
                heads.append(qv)
            wide = jnp.concatenate(wide + [jnp.zeros((TAIL - 6 * L, D), f32)], 0)
            pad = TAIL - 2 * L
            units = jnp.concatenate(units + [jnp.zeros((pad, F), f32)], 0).astype(bf16)
            heads = jnp.concatenate(heads + [jnp.zeros((pad, 3 * A), f32)], 0)
            part = 2 * HD // S
            for t in range(S):
                side, place = divmod(t, S // 2)
                cuts = []
                for h in range(H):
                    at = side * 2 * A + h * HD + place * part
                    cuts.append(heads[:, at : at + part])
                up = mm(units, spread(t, S, F), NT)
                rest = jnp.zeros((TAIL, z.a_cols - u_at - F // S), f32)
                all_s[t, M:, :] = jnp.concatenate(
                    [wide[:, t * M : (t + 1) * M]] + cuts + [up, rest], 1
                ).astype(bf16)
            if S == 4:
                outs[3][...] = all_s[scal_r[12], :half, :]
                outs[4][...] = all_s[scal_r[12], half:, :]
                send(outs[3], outs[4])
                for o_, at in zip(outs[:3], (9, 11, 10)):
                    o_[...] = all_s[scal_r[at]]
            else:
                outs[0][...] = all_s[...]

        block = (M + TAIL, z.a_cols)
        outs = [((S,) + block, bf16, FAR)]
        if S == 4:
            outs = [(block, bf16, FAR)] * 3
            outs += [((half, z.a_cols), bf16, FAR), ((M + TAIL - half, z.a_cols), bf16, FAR)]
        return run(
            kernel,
            [Far(n1), Far(n1_r), dp, Far(dp_r), Far(g1), Far(g1_r), Far(o), Far(o_r)] + [Far(a) for a in flat],
            outs,
            [pltpu.VMEM((S,) + block, bf16)],
            scalars=scal,
            name="project_grads",
            us=3,
        )

    def own_grads(n1, n1_r, dp, dp_r, g1, g1_r, o, o_r):
        def kernel(n_r, nr_r, p_r, pr_r, g_r, gr_r, o_i, or_i, out):
            first = mm(n_r[...], p_r[...], TN) + mm(nr_r[...], pr_r[...], TN)
            second = mm(g_r[...], o_i[...], TN) + mm(gr_r[...], or_i[...], TN)
            both = jnp.concatenate([first.astype(bf16), second.astype(bf16)], 1)
            out[...] = both.reshape(S, M, z.a_cols)

        return run(
            kernel,
            [Far(n1), Far(n1_r), dp, Far(dp_r), Far(g1), Far(g1_r), Far(o), Far(o_r)],
            [((S, M, z.a_cols), bf16, FAR)],
            name="own_grads",
            us=3,
        )[0]

    def pass_on(up, down, low, high):
        half = M // 2

        def kernel(up_r, down_r, low_r, high_r, up_o, down_o):
            up_o[:half, :] = (up_r[:half, :].astype(f32) + low_r[...].astype(f32)).astype(bf16)
            up_o[half:, :] = up_r[half:, :]
            send(up_o)
            down_o[:half, :] = down_r[:half, :]
            down_o[half:, :] = (down_r[half:, :].astype(f32) + high_r[...].astype(f32)).astype(bf16)

        return run(
            kernel,
            [Far(up), Far(down), Far(low), Far(high)],
            [((M + TAIL, z.a_cols), bf16, FAR)] * 2,
            name="pass_on",
        )

    def join_rows(scal, mine, theirs):
        def kernel(scal_r, a, b, o):
            start = pl.multiple_of(scal_r[8] * R, 16)
            o[pl.ds(start, R), :] = a[...]
            o[pl.ds(pl.multiple_of(R - start, 16), R), :] = b[...]

        return run(kernel, [Far(mine), Far(theirs)], [((2 * R, D), bf16, FAR)], scalars=scal, name="join_rows")[0]

    def sum_blocks(own, others):
        def kernel(own_r, a_r, b_r, o):
            o[...] = (own_r[...].astype(f32) + a_r[...].astype(f32) + b_r[...].astype(f32)).astype(bf16)

        return run(
            kernel,
            [Far(a) for a in [own] + others],
            [((M + TAIL, z.a_cols), bf16, FAR)],
            name="sum_blocks",
        )[0]

    def feed_out(pairs):
        def kernel(*refs):
            up_o, down_o = refs[-2:]
            for l in range(L):
                total = refs[2 * l][...].astype(f32) + refs[2 * l + 1][...].astype(f32)
                up_o[l] = total[:, :F]
                down_o[l] = total[:, F:]

        return run(
            kernel,
            [Far(a) for p in pairs for a in p],
            [((L, M, F), f32, FAR), ((L, M, F), f32, FAR)],
            name="feed_out",
        )

    def proj_out(pairs):
        def kernel(*refs):
            qkv_o, out_o = refs[-2:]
            for l in range(L):
                total = refs[2 * l][...].astype(f32) + refs[2 * l + 1][...].astype(f32)
                if l == 0:
                    total = total[:M]
                for h in range(H):
                    cuts = [total[:, i * A + h * HD : i * A + (h + 1) * HD] for i in range(3)]
                    qkv_o[l, h] = jnp.concatenate(cuts, 1)
                out_o[l] = total[:, 3 * A :].T
        return run(
            kernel,
            [Far(a) for p in pairs for a in p],
            [((L, H, M, 3 * HD), f32, FAR), ((L, A, M), f32, FAR)],
            name="project_out",
        )

    def small_sum(mine, theirs):
        def kernel(a_r, b_r, o):
            o[...] = a_r[M:, :].astype(f32) + b_r[M:, :].astype(f32)

        return run(kernel, [Far(mine), Far(theirs)], [((TAIL, z.a_cols), f32, FAR)], name="small_sum")[0]

    def small_out(scal, mine, x_side, core_side, far_side):
        def kernel(scal_r, a_r, x_r, c_r, f_r, qvb_o, upb_o, gain_o, shift_o):
            both = a_r[...] + c_r[...]
            other = x_r[...] + f_r[...]
            odd = scal_r[8] == 1
            part, unit = 2 * HD // S, 64 // S
            for l in range(L):
                rows = both[6 * l : 6 * l + 6, :M]
                first, third = rows[0:1], rows[2:3]
                if l == 0:
                    first, third = first + other[0:1, :M], third + other[2:3, :M]
                gain_o[l] = jnp.concatenate([first, rows[1:2]], 0)
                shift_o[l] = jnp.concatenate([third, rows[3:6]], 0)
                bias = jnp.where(odd, both[2 * l + 1 : 2 * l + 2], both[2 * l : 2 * l + 1])
                for h in range(H):
                    qvb_o[h, l : l + 1, :] = bias[:, q_at + h * part : q_at + (h + 1) * part]
                for r in range(F // 64):
                    upb_o[r, l : l + 1, :] = bias[:, u_at + r * unit : u_at + (r + 1) * unit]

        return run(
            kernel,
            [Far(mine), Far(x_side), Far(core_side), Far(far_side)],
            [
                ((H, L, 2 * HD // S), f32),
                ((F // 64, L, 64 // S), f32),
                ((L, 2, M), f32),
                ((L, 4, M), f32),
            ],
            scalars=scal,
            name="small_out",
        )

    def input_back(x, dy, pa, pb, vec):
        def kernel(x_r, dy_r, pa_r, pb_r, vec_r, o, sums_o):
            dn = pa_r[...].astype(f32) + pb_r[...].astype(f32)
            dx, dgain, dshift = ln_back(x_r[...].astype(f32), vec_r[0:1, :], dn)
            o[...] = (dy_r[...] + dx).astype(bf16)
            sums_o[0:1, :] = dgain
            sums_o[1:2, :] = dshift

        return run(kernel, [x, dy, pa, pb, vec], [((R, D), bf16, FAR), ((2, D), f32)], name="input_back")

    return dict(locals())


def local(mesh):
    def fn(frames, cotangent, w_qkv, qv_bias, w_out, w_up, up_bias, w_down, norm_gains, shifts):
        z = Sizes(mesh, frames, w_qkv, w_up)
        assert frames.shape[0] == 1
        k = make(z)
        L, m, R, D, A, F, H, HD, S = z.layers, z.m, z.rows, z.width, z.att, z.hidden, z.heads, z.hd, z.shards
        core = lax.axis_index("tc")
        scal = ring_scalars(S)

        def part_a(l, *then):
            qkv = after(w_qkv[l], *then).reshape(m, H, 3, HD).transpose(0, 2, 1, 3).reshape(m, 3 * A)
            return jnp.concatenate([qkv, after(w_out[l], *then).reshape(A, m).T], -1)

        def part_b(l, *then):
            return jnp.concatenate([after(w_up[l], *then), after(w_down[l], *then).T], -1)

        message = k["pack_first"](
            w_qkv, w_out, qv_bias, up_bias, norm_gains, shifts
        )
        w_a = [Pieces(message, TAIL) if S == 4 else Gathered(message, S, TAIL)]
        w_b = [Gathered(after(part_b(0, message), *w_a[0].arrays[1:4]), S)]

        def my_rows(x):
            return lax.dynamic_slice_in_dim(x.reshape(2 * R, D), core * R, R, 0)

        kept = []
        x = my_rows(frames)
        for layer in range(L):
            if layer == 0:
                n1, q, kv, vec, qb, tails = k["proj"](scal, x, 0, w_a[0])
            else:
                n1, q, kv, x = k["proj"](scal, after(y, *hid[1:]), layer, w_a[layer], (vec, qb), (part, x_swap(part)))
            far = y_swap(kv)
            near = core_swap(kv)
            if layer + 1 < L:
                next_a, next_b = part_a(layer + 1, n1), part_b(layer + 1, n1)
            acc = k["attend_near"](q, (kv, near))
            kvs = (kv, near, far, core_swap(after(far, acc)))
            o0, o1, qa, o_own, o_snd, att_part = k["attend_far"](scal, q, kvs[2:], acc, w_a[layer])
            far = x_swap(att_part)
            n1_r, o_rcv = core_swap(n1), core_swap(o_snd)
            x = after(x, n1_r, o_rcv)
            if layer + 1 < L:
                w_a.append(Gathered(after(next_a, kvs[1]), S))
                w_b.append(Gathered(after(next_b, att_part), S))
            y, n2, *hid_gp, part = k["feed"](
                scal, x, att_part, far, vec, tails, layer, w_b[layer]
            )
            n2_r, hid_r, gp = core_swap(n2), core_swap(hid_gp[1]), hid_gp[2:]
            hid = (hid_gp[0], hid_r, n2_r)
            kept.append((x, n1, n1_r, kvs, qa, (o0, o1), o_own, o_rcv, y, n2, hid, gp))

        def whole_rows(mine):
            return k["join_rows"](scal, mine, core_swap(mine))[None]

        def scatter(grad):
            return lax.psum_scatter(grad.reshape(D, -1), "shard", scatter_dimension=0, tiled=True)

        y_last, part_last = y, part
        g = my_rows(cotangent)
        wide, d_qv, d_up = [None] * L, [None] * L, [None] * L
        sum_a, sum_b = [None] * L, [None] * L
        before = None
        for layer in reversed(range(L)):
            x, n1, n1_r, kvs, qa, os, o_own, o_rcv, y, n2, hid, gp = kept[layer]
            if before is None:
                swap_b, du, part, sum_g2 = k["feed_back"](scal, g, gp, layer, w_b[layer])
            else:
                gp = [after(gp[0], grad_a), gp[1]]
                swap_b, du, part, sum_g2, g, pre = k["feed_back"](scal, None, gp, layer, w_b[layer], before)
                wide[layer + 1] = [pre] + wide[layer + 1]
            far = x_swap(part)
            grad_b, d_up[layer] = k["feed_grads"](
                scal, n2, hid[2], hid[0], hid[1], swap_b, core_swap(swap_b), du
            )
            y = after(y, grad_b)
            if before is not None:
                sum_b[layer + 1] = (part_b_sum, y_swap(after(part_b_sum, part)))
                y = after(y, sum_b[layer + 1][1])
            if layer > 0:
                part_b_sum = scatter(after(grad_b, far))
            dy, g1, da, mid = k["middle_back"](
                scal, y, g, part, far, vec, os[0], os[1], layer, w_a[layer]
            )
            if layer == 0:
                part_b_sum = scatter(after(grad_b, da))
            g1_r = core_swap(g1)
            dqt, own, snd = k["attend_back"](qa, kvs[2:], da)
            cross = k["cross_sum"](own, core_swap(snd))
            dqt = after(dqt, cross, g1_r, *([part_a_sum] if layer == 0 else []))
            cross = y_swap(cross)
            dq, own, snd = k["attend_back"](qa, kvs[:2], da, dqt)
            snd = after(snd, cross)
            kv_parts = (own, core_swap(snd), cross)
            dp, dp_snd, part, d_qv[layer], *pre = k["proj_back"](
                scal, dq, kv_parts, layer, w_a[layer], *([x] if layer == 0 else [])
            )
            far = x_swap(part)
            swaps = (n1, n1_r, dp, core_swap(dp_snd), g1, g1_r, o_own, o_rcv)
            if layer > 0:
                grad_a = k["own_grads"](*swaps)
                part_a_sum = scatter(after(grad_a, far))
            else:
                sum_a[1] = (part_a_sum, y_swap(after(part_a_sum, part)))
                wide[0] = pre + [mid, sum_g2]
                small = [wide[l] + [d_up[l], d_qv[l]] for l in range(L)]
                blocks = k["proj_grads"](scal, *swaps, small)
            wide[layer] = pre + [mid, sum_g2]
            before = (x, dy, part, far, vec)
        grad_rows, _ = k["input_back"](x, after(dy, blocks[0]), part, far, vec)
        if S == 4:
            hops = [lax.ppermute(b, "shard", ring(s)) for b, s in zip(blocks[3:], (1, 3))]
            up, down = k["pass_on"](after(blocks[1], grad_rows, sum_a[1][1]), blocks[2], *hops)
            ready = up
            others = [lax.ppermute(up, "shard", ring(1)), lax.ppermute(down, "shard", ring(3))]
        else:
            ready = blocks[0]
        part_b_sum = after(part_b_sum, ready)
        sum_b[0] = (part_b_sum, y_swap(part_b_sum))
        far_last = x_swap(after(part_last, ready))
        last_rows = k["finish"](y_last, part_last, far_last, vec)[0]
        frames_grad = whole_rows(grad_rows)
        block = after(blocks[0], sum_b[0][1], frames_grad, last_rows)
        if S == 4:
            mine = k["sum_blocks"](block, others)
        else:
            mine = lax.psum_scatter(block, "shard", scatter_dimension=0, tiled=True)[0]
        theirs = y_swap(mine)
        sum_a[0] = (mine, theirs)
        out_frames = whole_rows(after(last_rows, mine))
        outs_up, outs_down = k["feed_out"]([sum_b[0], (after(sum_b[1][0], mine), sum_b[1][1])])
        tiny = k["small_sum"](after(mine, outs_up, out_frames), theirs)
        tiny_x = x_swap(tiny)
        tiny_c = core_swap(tiny)
        outs_qkv, outs_out = k["proj_out"]([(after(mine, tiny), theirs), sum_a[1]])
        tiny_f = core_swap(after(tiny_x, outs_qkv))
        g_qvb, g_upb, g_gains, g_shifts = k["small_out"](
            scal, tiny, tiny_x, tiny_c, tiny_f
        )
        return (
            out_frames,
            frames_grad,
            outs_qkv.transpose(0, 2, 1, 3),
            g_qvb.transpose(1, 0, 2),
            outs_out.reshape(L, H, HD, m),
            outs_up,
            g_upb.transpose(1, 0, 2),
            outs_down.transpose(0, 2, 1),
            g_gains,
            g_shifts,
        )

    return fn


def solution(mesh):
    assert mesh.axis_names == ("shard", "ctx", "tp") and mesh.shape["tp"] == 4 and mesh.shape["ctx"] == 2
    split = Mesh(mesh.devices.reshape(mesh.shape["shard"], 2, 2, 2), ("shard", "ctx", "tx", "tc"))
    tp = ("tx", "tc")
    specs = (
        P("shard", "ctx", None),
        P("shard", "ctx", None),
        P(None, "shard", tp, None),
        P(None, tp, "shard"),
        P(None, tp, None, "shard"),
        P(None, "shard", tp),
        P(None, tp, "shard"),
        P(None, tp, "shard"),
        P(None, None, "shard"),
        P(None, None, "shard"),
    )
    return jax.shard_map(local(split), mesh=split, in_specs=specs, out_specs=specs, check_vma=False)
```

```python
import math

import jax
import jax.numpy as jnp
from jax import lax
from jax.experimental import pallas as pl
from jax.experimental.pallas import tpu as pltpu
from jax.sharding import Mesh
from jax.sharding import PartitionSpec as P

f32 = jnp.float32
bf16 = jnp.bfloat16
EPSILON = 1e-05
NN = (((1,), (0,)), ((), ()))
NT = (((1,), (1,)), ((), ()))
TN = (((0,), (0,)), ((), ()))
VMEM_MIB = {
    "attend_far": 13,
    "attend_near": 10,
    "attend_back": 14,
    "feed": 16,
    "feed_back": 16,
    "feed_grads": 12,
    "own_grads": 9,
    "feed_out": 7.6,
    "finish": 6,
    "input_back": 10,
    "middle_back": 11,
    "pack_first": 6,
    "pair_grads": 9,
    "project": 9.5,
    "project_back": 9.5,
    "project_grads": 13,
    "project_out": 5,
}
WIDE = 128
TAIL = 16
COST = 200_000_000


def mm(a, b, dims=NN):
    return lax.dot_general(a, b, dims, preferred_element_type=f32)


def core_swap(x):
    return lax.ppermute(x, "tc", [(0, 1), (1, 0)])


def x_swap(x):
    return lax.ppermute(x, "tx", [(0, 1), (1, 0)])


def y_swap(x):
    return lax.ppermute(x, "ctx", [(0, 1), (1, 0)])


def after(x, *others):
    return lax.optimization_barrier((x,) + others)[0]


def ring(shift):
    return [(i, (i + shift) % 4) for i in range(4)]


def ring_scalars(shards):
    me = lax.axis_index("shard").astype(jnp.int32)
    zero = jnp.int32(0)
    order = [me, (me + shards - 1) % shards, (me + 1) % shards, (me + 2) % shards]
    return jnp.stack([zero] * 8 + [lax.axis_index("tc").astype(jnp.int32)] + order + [zero] * 3)


class Pieces:
    def __init__(self, x, tail=0):
        self.rows = x.shape[0] - tail
        self.mine = [x] + [lax.ppermute(x, "shard", ring(s)) for s in (1, 3, 2)]
        self.arrays = self.mine + [core_swap(p) for p in self.mine]

    def copies(self, scal, refs, columns, dest, sems):
        out = []
        for k, ref in enumerate(refs):
            slot = scal[8] if k < 4 else 1 - scal[8]
            to = dest.at[slot, scal[9 + k % 4]]
            out.append(pltpu.make_async_copy(ref.at[pl.ds(0, self.rows), columns], to, sems.at[k]))
        return out

    def tails(self, scal, refs, dest, sems):
        out = []
        for k, ref in enumerate(refs):
            slot = scal[8] if k < 4 else 1 - scal[8]
            to = dest.at[slot, scal[9 + k % 4]]
            out.append(pltpu.make_async_copy(ref.at[pl.ds(self.rows, TAIL), :], to, sems.at[k]))
        return out


class Gathered:
    def __init__(self, x, shards, tail=0):
        self.rows = x.shape[0] - tail
        whole = lax.all_gather(x, ("shard", "tc"), axis=0, tiled=False)
        self.arrays = [whole.reshape((shards, 2) + x.shape)]

    def copies(self, scal, refs, columns, dest, sems):
        ref = refs[0]
        return [
            pltpu.make_async_copy(ref.at[:, c, pl.ds(0, self.rows), columns], dest.at[c], sems.at[c])
            for c in range(2)
        ]

    def tails(self, scal, refs, dest, sems):
        ref = refs[0]
        return [
            pltpu.make_async_copy(ref.at[:, c, pl.ds(self.rows, TAIL), :], dest.at[c], sems.at[c])
            for c in range(2)
        ]


def vmem():
    return pl.BlockSpec(memory_space=pltpu.VMEM)


class Far:
    def __init__(self, array):
        self.array = array


class Reading:
    def __init__(self, buffer, copy):
        self.buffer, self.copy, self.waited = buffer, copy, False

    def need(self):
        if not self.waited:
            self.copy.wait()
            self.waited = True
        return self.buffer

    def __getitem__(self, index):
        return self.need()[index]

    @property
    def shape(self):
        return self.buffer.shape


class Writing:
    def __init__(self, buffer, copy):
        self.buffer, self.copy, self.sent = buffer, copy, False

    def __setitem__(self, index, value):
        self.buffer[index] = value

    @property
    def at(self):
        return self.buffer.at

    def send(self):
        if not self.sent:
            self.copy.start()
            self.sent = True


def send(*refs):
    for r in refs:
        if isinstance(r, Writing):
            r.send()


def need(*refs):
    for r in refs:
        if isinstance(r, Reading):
            r.need()


FAR = "far"


def run(kernel, ins, outs, scratch=(), w=None, scalars=None, name=None, us=1.0):
    pieces = [] if w is None else w.arrays
    n_in, n_out, n_pieces = len(ins), len(outs), len(pieces)
    far_in = [i for i, a in enumerate(ins) if isinstance(a, Far)]
    far_out = [i for i, o in enumerate(outs) if len(o) == 3]
    any_space = pl.BlockSpec(memory_space=pl.ANY)
    specs, args = [], []
    if scalars is not None:
        specs.append(pl.BlockSpec(memory_space=pltpu.SMEM))
        args.append(scalars)
    for a in ins:
        if isinstance(a, Far):
            specs.append(any_space)
            args.append(pltpu.with_memory_space_constraint(a.array, pltpu.HBM))
        else:
            specs.append(vmem())
            args.append(a)
    for p in pieces:
        specs.append(any_space)
        args.append(pltpu.with_memory_space_constraint(p, pltpu.HBM))
    first = len(args) - n_in - n_pieces
    shapes = [
        pltpu.HBM(o[0], o[1]) if len(o) == 3 else jax.ShapeDtypeStruct(o[0], o[1]) for o in outs
    ]
    buffers = [pltpu.VMEM(ins[i].array.shape, ins[i].array.dtype) for i in far_in]
    buffers += [pltpu.VMEM(outs[i][0], outs[i][1]) for i in far_out]
    sems = [pltpu.SemaphoreType.DMA((len(buffers),))] if buffers else []

    def wrapped(*refs):
        refs = list(refs)
        n_all = len(args) + n_out + len(scratch)
        own, extra = refs[:n_all], refs[n_all:]
        reads, writes = [], []
        for k, i in enumerate(far_in):
            copy = pltpu.make_async_copy(own[first + i], extra[k], extra[-1].at[k])
            copy.start()
            own[first + i] = Reading(extra[k], copy)
            reads.append(own[first + i])
        for k, i in enumerate(far_out):
            k += len(far_in)
            at = len(args) + i
            own[at] = Writing(extra[k], pltpu.make_async_copy(extra[k], own[at], extra[-1].at[k]))
            writes.append(own[at])
        kernel(*own)
        for w in writes:
            w.send()
        for r in reads:
            r.need()
        for w in writes:
            w.copy.wait()

    return pl.pallas_call(
        wrapped,
        out_shape=shapes,
        in_specs=specs,
        out_specs=[any_space if len(o) == 3 else vmem() for o in outs],
        scratch_shapes=list(scratch) + buffers + sems,
        compiler_params=pltpu.CompilerParams(vmem_limit_bytes=int(VMEM_MIB.get(name, 4) * 1024 * 1024)),
        cost_estimate=pl.CostEstimate(flops=int(us * COST), bytes_accessed=1000, transcendentals=0),
        name=name,
    )(*args)


def spread(shard, shards, units):
    part = 64 // shards
    bits, low = part.bit_length() - 1, part - 1
    i = lax.broadcasted_iota(jnp.int32, (units // shards, units), 0)
    j = lax.broadcasted_iota(jnp.int32, (units // shards, units), 1)
    same = ((j >> 6) == (i >> bits)) & ((j & 63) == shard * part + (i & low))
    return jnp.where(same, 1.0, 0.0).astype(bf16)


def start_all(copies):
    for c in copies:
        c.start()


def wait_all(copies):
    for c in copies:
        c.wait()


def ln_parts(x):
    centred = x - jnp.mean(x, -1, keepdims=True)
    inv = lax.rsqrt(jnp.mean(centred * centred, -1, keepdims=True) + EPSILON)
    return centred * inv, inv


def ln_back(x, gain, dn):
    hat, inv = ln_parts(x)
    dhat = dn * gain
    dx = inv * (
        dhat
        - jnp.mean(dhat, -1, keepdims=True)
        - hat * jnp.mean(dhat * hat, -1, keepdims=True)
    )
    return dx, jnp.sum(dn * hat, 0, keepdims=True), jnp.sum(dn, 0, keepdims=True)


def split3(v):
    a = v.astype(bf16)
    r = v - a.astype(f32)
    b = r.astype(bf16)
    c = (r - b.astype(f32)).astype(bf16)
    return a, b, c


def beside(wide, column):
    a, b, c = split3(column)
    rows, size = wide.shape[0], wide.shape[1]
    return jnp.concatenate([wide, a, b, c, jnp.zeros((rows, WIDE - size - 3), bf16)], 1)


class Sizes:
    def __init__(self, mesh, frames, w_qkv, w_up):
        self.shards = mesh.shape["shard"]
        self.layers = w_qkv.shape[0]
        self.width = frames.shape[-1]
        self.rows = frames.shape[1] // 2
        self.heads = w_qkv.shape[2]
        self.hd = w_qkv.shape[3] // 3
        self.att = self.heads * self.hd
        self.hidden = w_up.shape[2]
        self.m = w_qkv.shape[1]
        self.a_cols = 4 * self.att
        self.b_cols = 2 * self.hidden


def make(z):
    R, D, A, H, HD, F = z.rows, z.width, z.att, z.heads, z.hd, z.hidden
    L, S, M = z.layers, z.shards, z.m
    coef = HD ** (-0.5) / math.log(2.0)
    scale = HD ** (-0.5)
    dma = pltpu.SemaphoreType.DMA
    q_at, u_at = M, M + 2 * A // S

    def weight_scratch(columns):
        return [pltpu.VMEM((2, S, M, columns), bf16), dma((8,))]

    def weight(w_s, c, start, stop):
        return w_s[c, :, :, start:stop].reshape(D, stop - start)

    def pack_first(w_qkv, w_out, qv_bias, up_bias, norm_gains, shifts):
        nq, nu = 2 * HD // S, 64 // S

        def kernel(w_r, o_r, qv_r, up_r, g_r, s_r, out):
            for side in range(3):
                cuts = [w_r[0, h][:, side * HD : (side + 1) * HD] for h in range(H)]
                out[:M, side * A : (side + 1) * A] = jnp.concatenate(cuts, 1)
            out[:M, 3 * A :] = o_r[0].astype(f32).T.astype(bf16)
            vecs = []
            for l in range(L):
                vecs += [g_r[l].astype(f32), s_r[l].astype(f32)]
            vecs = jnp.concatenate(vecs + [jnp.zeros((TAIL - 6 * L, M), f32)], 0)
            rows = []
            for l in range(L):
                cuts = [qv_r[h].astype(f32)[l : l + 1, :] for h in range(H)]
                cuts += [up_r[r].astype(f32)[l : l + 1, :] for r in range(F // 64)]
                rows.append(jnp.concatenate(cuts, 1))
            rows = jnp.concatenate(rows + [jnp.zeros((TAIL - L, H * nq + F // 64 * nu), f32)], 0)
            rest = jnp.zeros((TAIL, z.a_cols - M - rows.shape[1]), f32)
            out[M:, :] = jnp.concatenate([vecs, rows, rest], 1).astype(bf16)

        return run(
            kernel,
            [
                Far(a)
                for a in (
                    w_qkv.transpose(0, 2, 1, 3),
                    w_out.reshape(L, A, M),
                    qv_bias.transpose(1, 0, 2),
                    up_bias.transpose(1, 0, 2),
                    norm_gains,
                    shifts,
                )
            ],
            [((M + TAIL, z.a_cols), bf16, FAR)],
            name="pack_first",
        )[0]

    def proj(scal, x, layer, w, biases=None, prev=None):
        first = biases is None
        n = len(w.arrays)
        part = 2 * HD // S

        def kernel(*refs):
            it = iter(refs)
            scal_r, x_r = next(it), next(it)
            if not first:
                vec_r, qb_r, pa_r, pb_r = (next(it) for _ in range(4))
            piece_r = [next(it) for _ in range(n)]
            n_o, q_o, kv_o = (next(it) for _ in range(3))
            if first:
                vec_r, qb_r, tail_o = (next(it) for _ in range(3))
            else:
                x_o = next(it)
            w_s, sems = next(it), next(it)
            if first:
                tail_sems = next(it)
                tails = w.tails(scal_r, piece_r, tail_o, tail_sems)
                start_all(tails)
            copies = w.copies(scal_r, piece_r, pl.ds(0, z.a_cols), w_s, sems)
            start_all(copies)
            xv = x_r[...].astype(f32)
            if not first:
                at = 6 * (layer - 1) + 5
                xv = xv + (pa_r[...].astype(f32) + pb_r[...].astype(f32) + vec_r[at : at + 1, :])
                x_o[...] = xv
                send(x_o)
            hat, _ = ln_parts(xv)
            if first:
                wait_all(tails)
                vec_r[...] = jnp.concatenate([tail_o[0, t][:, :M] for t in range(S)], 1).astype(f32)
                for l in range(L):
                    for p in range(2):
                        rows = [tail_o[p, t].astype(f32)[l : l + 1, q_at:u_at] for t in range(S)]
                        seq = []
                        for side in range(2):
                            for h in range(H):
                                seq += [
                                    rows[t][:, h * part : (h + 1) * part]
                                    for t in range(side * S // 2, (side + 1) * S // 2)
                                ]
                            if side == 0:
                                seq.append(jnp.zeros((1, A), f32))
                        qb_r[2 * l + p : 2 * l + p + 1, :] = jnp.concatenate(seq, 1)
            g = 6 * layer
            nv = (hat * vec_r[g : g + 1, :] + vec_r[g + 2 : g + 3, :]).astype(bf16)
            n_o[...] = nv
            send(n_o)
            wait_all(copies)
            both = []
            for e in range(2):
                b = 2 * layer + e
                p = (mm(nv, weight(w_s, e, 0, 3 * A)) + qb_r[b : b + 1, :]).astype(bf16)
                kv_o[:, e * 2 * A : (e + 1) * 2 * A] = p[:, A:]
                both.append(p[:, :A])
            send(kv_o)
            q_o[...] = jnp.concatenate(both, 1)

        ins = [Far(x)] + ([] if first else list(biases) + [Far(prev[0]), prev[1]])
        outs = [((R, D), bf16, FAR), ((R, 2 * A), bf16), ((R, 4 * A), bf16, FAR)]
        scratch = weight_scratch(z.a_cols)
        if first:
            outs += [((TAIL, D), f32), ((2 * L, 3 * A), f32), ((2, S, TAIL, z.a_cols), bf16)]
            scratch += [dma((8,))]
        else:
            outs += [((R, D), f32, FAR)]
        return run(kernel, ins, outs, scratch, w, scal, "project", 3.5)

    def aug(block, offset, fill):
        return jnp.concatenate([block[:, offset : offset + HD], fill], 1)

    def head_lanes(j):
        e, h = divmod(j, H)
        return j * HD, e * 2 * A + h * HD, e * 2 * A + A + h * HD

    def load_heads(kv_refs, k_s, v_s):
        ones = jnp.ones((R, HD), bf16)
        for b, ref in enumerate(kv_refs):
            blk = ref[...]
            for j in range(2 * H):
                _, k_at, v_at = head_lanes(j)
                k_s[j, b * R : (b + 1) * R, :] = aug(blk, k_at, ones)
                v_s[j, b * R : (b + 1) * R, :] = aug(blk, v_at, ones)

    def attend_near(q, kvs):
        K = 2 * R

        def kernel(q_r, kv0, kv1, acc_o, q_s, k_s, v_s):
            zeros = jnp.zeros((R, HD), bf16)
            for j in range(2 * H):
                q_s[j] = aug(q_r[...], j * HD, zeros)
            load_heads((kv0, kv1), k_s, v_s)

            def head(j, carry):
                s = mm(q_s[j], k_s[j], NT)
                top = jnp.max(s, -1, keepdims=True)
                oe = mm(jnp.exp2((s - top) * coef).astype(bf16), v_s[j])
                acc_o[j] = jnp.concatenate(
                    [oe[:, : HD + 1], top, jnp.zeros((R, WIDE - HD - 2), f32)], 1
                )
                return carry

            lax.fori_loop(0, 2 * H, head, 0)

        return run(
            kernel,
            [q] + list(kvs),
            [((2 * H, R, WIDE), f32)],
            [pltpu.VMEM((2 * H, R, WIDE), bf16)] + [pltpu.VMEM((2 * H, K, WIDE), bf16)] * 2,
            name="attend_near",
            us=6,
        )[0]

    def attend_far(scal, q, kvs, acc, w):
        K = 2 * R
        n = len(w.arrays)

        def kernel(scal_r, q_r, kv2, kv3, acc_r, *refs):
            piece_r = refs[:n]
            o0_o, o1_o, qa_o, own_o, snd_o, part_o, q_s, k_s, v_s, o_s, w_s, sems = refs[n:]
            copies = w.copies(scal_r, piece_r, pl.ds(z.a_cols - 256, 256), w_s, sems)
            start_all(copies)
            zeros = jnp.zeros((R, HD), bf16)
            for j in range(2 * H):
                q_s[j] = aug(q_r[...], j * HD, zeros)
            load_heads((kv2, kv3), k_s, v_s)

            def head(j, carry):
                s = mm(q_s[j], k_s[j], NT)
                old = acc_r[j]
                old_top = old[:, HD + 1 : HD + 2]
                top = jnp.maximum(jnp.max(s, -1, keepdims=True), old_top)
                oe = mm(jnp.exp2((s - top) * coef).astype(bf16), v_s[j])
                oe = oe + old * jnp.exp2((old_top - top) * coef)
                total = oe[:, HD : HD + 1]
                o_s[j] = (oe[:, :HD] / total).astype(bf16)
                lse = top + jnp.log2(total) * (1.0 / coef)
                qa_o.buffer[j] = beside(q_s[j][:, :HD], -lse)
                return carry

            lax.fori_loop(0, 2 * H, head, 0)
            send(qa_o)
            o0 = jnp.concatenate([o_s[j] for j in range(H)], 1)
            o1 = jnp.concatenate([o_s[H + j] for j in range(H)], 1)
            wait_all(copies)
            part = mm(o0, weight(w_s, 0, 256 - A, 256), NT) + mm(o1, weight(w_s, 1, 256 - A, 256), NT)
            part_o[...] = part.astype(bf16)
            send(part_o)
            odd = scal_r[8] == 1
            o0_o[...] = o0
            o1_o[...] = o1
            own_o[...] = jnp.where(odd, o1, o0)
            snd_o[...] = jnp.where(odd, o0, o1)

        return run(
            kernel,
            [q] + list(kvs) + [acc],
            [((R, A), bf16, FAR)] * 2
            + [((2 * H, R, WIDE), bf16, FAR)]
            + [((R, A), bf16, FAR)] * 2
            + [((R, D), bf16, FAR)],
            [pltpu.VMEM((2 * H, R, WIDE), bf16)]
            + [pltpu.VMEM((2 * H, K, WIDE), bf16)] * 2
            + [pltpu.VMEM((2 * H, R, HD), bf16)]
            + weight_scratch(256),
            w,
            scal,
            "attend_far",
            8,
        )

    def feed(scal, x, pa, pb, vec, tails, layer, w):
        n = len(w.arrays)
        g = 6 * layer

        def kernel(scal_r, x_r, pa_r, pb_r, vec_r, tail_r, *refs):
            piece_r = refs[:n]
            y_o, n_o, *hid_gp, part_o, w_s, sems = refs[n:]
            copies = w.copies(scal_r, piece_r, pl.ds(0, 2 * F), w_s, sems)
            start_all(copies)
            y = x_r[...].astype(f32) + (
                pa_r[...].astype(f32) + pb_r[...].astype(f32) + vec_r[g + 3 : g + 4, :]
            )
            y_o[...] = y
            send(y_o)
            hat, _ = ln_parts(y)
            nv = (hat * vec_r[g + 1 : g + 2, :] + vec_r[g + 4 : g + 5, :]).astype(bf16)
            n_o[...] = nv
            send(n_o)
            bias = [None, None]
            for t in range(S):
                e = spread(t, S, F)
                for s in range(2):
                    add = mm(tail_r[s, t][:, u_at : u_at + F // S], e)
                    bias[s] = add if t == 0 else bias[s] + add
            part, hiddens = None, []
            for s in range(2):
                copies[s].wait()
                u = mm(nv, weight(w_s, s, 0, F)) + bias[s][layer : layer + 1, :]
                cdf = 0.5 * (1.0 + lax.erf(u * (0.5**0.5)))
                pdf = jnp.exp(-0.5 * u * u) * (1.0 / math.sqrt(2.0 * math.pi))
                hidden = (u * cdf).astype(bf16)
                hid_gp[2 + s][...] = (cdf + u * pdf).astype(bf16)
                send(hid_gp[2 + s])
                hiddens.append(hidden)
                t = mm(hidden, weight(w_s, s, F, 2 * F), NT)
                part = t if part is None else part + t
            part_o[...] = part.astype(bf16)
            send(part_o)
            odd = scal_r[8] == 1
            hid_gp[0][...] = jnp.where(odd, hiddens[1], hiddens[0])
            hid_gp[1][...] = jnp.where(odd, hiddens[0], hiddens[1])

        outs = [
            ((R, D), f32, FAR),
            ((R, D), bf16, FAR),
            ((R, F), bf16, FAR),
            ((R, F), bf16, FAR),
            ((R, F), bf16, FAR),
            ((R, F), bf16, FAR),
            ((R, D), bf16, FAR),
        ]
        return run(
            kernel, [Far(x), Far(pa), pb, vec, tails], outs, weight_scratch(2 * F), w, scal, "feed", 6
        )

    def finish(y, pa, pb, vec):
        at = 6 * (L - 1) + 5

        def kernel(y_r, pa_r, pb_r, vec_r, o):
            v = y_r[...] + (pa_r[...].astype(f32) + pb_r[...].astype(f32) + vec_r[at : at + 1, :])
            o[...] = v.astype(bf16)

        return run(kernel, [Far(y), Far(pa), Far(pb), vec], [((R, D), bf16, FAR)], name="finish")

    def feed_back(scal, grad, gp, layer, w, before=None):
        n = len(w.arrays)
        up = 6 * (layer + 1)

        def kernel(*refs):
            it = iter(refs)
            scal_r = next(it)
            if before is None:
                g_r = next(it)
            else:
                x_r, dy_r, pa_r, pb_r, vec_r = (next(it) for _ in range(5))
            gp_r = (next(it), next(it))
            piece_r = [next(it) for _ in range(n)]
            swap_o, du_o, part_o, sums_o = (next(it) for _ in range(4))
            if before is not None:
                g_o, pre_o = next(it), next(it)
            w_s, sems = next(it), next(it)
            copies = w.copies(scal_r, piece_r, pl.ds(0, 2 * F), w_s, sems)
            start_all(copies)
            if before is None:
                g = g_r[...].astype(f32)
            else:
                dn = pa_r[...].astype(f32) + pb_r[...].astype(f32)
                dx, dgain, dshift = ln_back(x_r[...], vec_r[up : up + 1, :], dn)
                g = dy_r[...] + dx
                g_o[...] = g
                pre_o[0:1, :] = dgain
                pre_o[1:2, :] = dshift
            g2 = g.astype(bf16)
            swap_o[:, :D] = g2
            sums_o[...] = jnp.sum(g2.astype(f32), 0, keepdims=True)
            wait_all(copies)
            odd = scal_r[8] == 1
            part = None
            for k in range(2):
                slot = scal_r[8] if k else 1 - scal_r[8]
                first, second = (gp_r[1][...], gp_r[0][...]) if k else (gp_r[0][...], gp_r[1][...])
                slope = jnp.where(odd, first, second).astype(f32)
                du = (slope * mm(g2, weight(w_s, slot, F, 2 * F))).astype(bf16)
                if k == 0:
                    swap_o[:, D:] = du
                    send(swap_o)
                else:
                    du_o[...] = du
                t = mm(du, weight(w_s, slot, 0, F), NT)
                part = t if part is None else part + t
            part_o[...] = part.astype(bf16)

        ins = [grad] if before is None else [Far(b) for b in before[:3]] + list(before[3:])
        ins += [Far(gp[0]), Far(gp[1])]
        outs = [((R, D + F), bf16, FAR), ((R, F), bf16), ((R, D), bf16, FAR), ((1, D), f32)]
        if before is not None:
            outs += [((R, D), f32), ((2, D), f32)]
        return run(kernel, ins, outs, weight_scratch(2 * F), w, scal, "feed_back", 6)

    def blocks_out(scal_r, full, outs):
        if S == 4:
            for o, at in zip(outs, (9, 11, 10, 12)):
                o[...] = full[scal_r[at]]
        else:
            outs[0][...] = full[...]

    def block_shapes(rows, columns):
        return [((rows, columns), bf16, FAR)] * 4 if S == 4 else [((S, rows, columns), bf16, FAR)]

    def feed_grads(scal, n2, n2_r, hid, hid_r, swap, swap_r, du):
        def kernel(scal_r, n_r, nr_r, h_r, hr_r, s_r, sr_r, du_r, g_o, b_o):
            other = sr_r[:, D:]
            g_o[:, :F] = (mm(n_r[...], du_r[...], TN) + mm(nr_r[...], other, TN)).astype(bf16)
            g_o[:, F:] = (mm(s_r[:, :D], h_r[...], TN) + mm(sr_r[:, :D], hr_r[...], TN)).astype(bf16)
            total = jnp.sum(du_r[...].astype(f32), 0, keepdims=True) + jnp.sum(
                other.astype(f32), 0, keepdims=True
            )
            odd = scal_r[8] == 1
            b_o[0:1, :] = jnp.where(odd, 0.0, total)
            b_o[1:2, :] = jnp.where(odd, total, 0.0)

        return run(
            kernel,
            [Far(n2), Far(n2_r), Far(hid), Far(hid_r), Far(swap), Far(swap_r), du],
            [((D, 2 * F), bf16, FAR), ((2, F), f32)],
            scalars=scal,
            name="feed_grads",
            us=3,
        )

    def middle_back(scal, y, g, pa, pb, vec, o0, o1, layer, w):
        n = len(w.arrays)
        gain = 6 * layer + 1

        def kernel(scal_r, y_r, g_r, pa_r, pb_r, vec_r, o0_r, o1_r, *refs):
            piece_r = refs[:n]
            dy_o, g1_o, d_o, sums_o, w_s, sems = refs[n:]
            copies = w.copies(scal_r, piece_r, pl.ds(z.a_cols - 256, 256), w_s, sems)
            start_all(copies)
            dn = pa_r[...].astype(f32) + pb_r[...].astype(f32)
            dx, dgain, dshift = ln_back(y_r[...], vec_r[gain : gain + 1, :], dn)
            dy = g_r[...].astype(f32) + dx
            dy_o[...] = dy
            send(dy_o)
            g1 = dy.astype(bf16)
            g1_o[...] = g1
            send(g1_o)
            sums_o[0:1, :] = dgain
            sums_o[1:2, :] = jnp.sum(g1.astype(f32), 0, keepdims=True)
            sums_o[2:3, :] = dshift
            wait_all(copies)
            for e, o_r in enumerate((o0_r, o1_r)):
                do = mm(g1, weight(w_s, e, 256 - A, 256)).astype(bf16)
                prod = do.astype(f32) * o_r[...].astype(f32)
                for h in range(H):
                    lanes = slice(h * HD, (h + 1) * HD)
                    d_o[e * H + h] = beside(do[:, lanes], -jnp.sum(prod[:, lanes], -1, keepdims=True))

        outs = [((R, D), f32, FAR), ((R, D), bf16, FAR), ((2 * H, R, WIDE), bf16), ((3, D), f32)]
        return run(
            kernel,
            [Far(y), g, Far(pa), pb, vec, Far(o0), Far(o1)],
            outs,
            weight_scratch(256),
            w,
            scal,
            "middle_back",
            4,
        )

    def attend_back(qa, kvs, da, before=None, ahead=False):
        K = 2 * R

        def kernel(qa_r, kv0, kv1, da_r, *refs):
            refs = list(refs)
            if before is not None:
                old_r = refs.pop(0)
            dq_o, e0, e1, k_s, v_s, dk_s, dv_s, *dq_s = refs
            need(qa_r)
            load_heads((kv0, kv1), k_s, v_s)

            def head(j, carry):
                qv = qa_r[j]
                dv_in = da_r[j]
                dqt = None
                for b in range(2):
                    at = slice(b * R, (b + 1) * R)
                    kb = k_s[j, at, :]
                    p = jnp.exp2(mm(kb, qv, NT) * coef)
                    ds = (p * mm(v_s[j, at, :], dv_in, NT)).astype(bf16)
                    dv_s[j, at, :] = mm(p.astype(bf16), dv_in).astype(bf16)
                    dk_s[j, at, :] = (mm(ds, qv) * scale).astype(bf16)
                    t = mm(kb, ds, TN)
                    dqt = t if dqt is None else dqt + t
                if before is None:
                    dq_o[j] = dqt
                else:
                    dq_s[0][j] = ((dqt + old_r[j]).T * scale).astype(bf16)
                return carry

            lax.fori_loop(0, 2 * H, head, 0)
            for b, e_o in ((1, e1), (0, e0)):
                at = slice(b * R, (b + 1) * R)
                cols = []
                for e in range(2):
                    cols += [dk_s[e * H + h, at, :HD] for h in range(H)]
                    cols += [dv_s[e * H + h, at, :HD] for h in range(H)]
                e_o[...] = jnp.concatenate(cols, 1)
                send(e_o)
            if before is not None:
                dq_o[...] = jnp.concatenate([dq_s[0][j][:, :HD] for j in range(2 * H)], 1)

        ins = [qa] + list(kvs) + [da]
        if before is None and not ahead:
            ins = [Far(a) for a in ins[:3]] + [da]
        outs = [((R, 4 * A), bf16), ((R, 4 * A), bf16, FAR)]
        scratch = [pltpu.VMEM((2 * H, K, WIDE), bf16)] * 4
        if before is None:
            outs = [((2 * H, WIDE, R), f32)] + outs
        else:
            ins.append(before)
            outs = [((R, 2 * A), bf16)] + outs
            scratch.append(pltpu.VMEM((2 * H, R, WIDE), bf16))
        return run(kernel, ins, outs, scratch, name="attend_back", us=8)

    def cross_sum(own, theirs):
        def kernel(a, b, o):
            o[...] = (a[...].astype(f32) + b[...].astype(f32)).astype(bf16)

        return run(kernel, [own, theirs], [(own.shape, bf16, FAR)], name="cross_sum")[0]

    def proj_back(scal, dq, kv_parts, layer, w, x=None):
        n = len(w.arrays)

        def kernel(scal_r, q_r, a, p, c, *refs):
            refs = list(refs)
            if x is not None:
                x_r = refs.pop(0)
            piece_r, refs = refs[:n], refs[n:]
            own_o, snd_o, part_o, b_o = refs[:4]
            w_s, sems = refs[-2:]
            copies = w.copies(scal_r, piece_r, pl.ds(0, z.a_cols), w_s, sems)
            start_all(copies)
            both = []
            for e in range(2):
                at = slice(e * 2 * A, (e + 1) * 2 * A)
                total = a[:, at].astype(f32) + p[:, at].astype(f32) + c[:, at].astype(f32)
                both.append(jnp.concatenate([q_r[:, e * A : (e + 1) * A], total.astype(bf16)], 1))
                b_o[e : e + 1, :] = jnp.sum(both[e].astype(f32), 0, keepdims=True)
            odd = scal_r[8] == 1
            own_o[...] = jnp.where(odd, both[1], both[0])
            snd_o[...] = jnp.where(odd, both[0], both[1])
            send(snd_o)
            if x is not None:
                hat, _ = ln_parts(x_r[...].astype(f32))
            wait_all(copies)
            part = mm(both[0], weight(w_s, 0, 0, 3 * A), NT) + mm(both[1], weight(w_s, 1, 0, 3 * A), NT)
            part_o[...] = part.astype(bf16)
            if x is not None:
                send(part_o)
                refs[4][0:1, :] = jnp.sum(part * hat, 0, keepdims=True)
                refs[4][1:2, :] = jnp.sum(part, 0, keepdims=True)

        ins = [dq] + list(kv_parts)
        outs = [((R, 3 * A), bf16), ((R, 3 * A), bf16, FAR), ((R, D), bf16, FAR), ((2, 3 * A), f32)]
        if x is not None:
            ins.append(Far(x))
            outs.append(((2, D), f32))
        return run(kernel, ins, outs, weight_scratch(z.a_cols), w, scal, "project_back", 4)

    def proj_grads(scal, n1, n1_r, dp, dp_r, g1, g1_r, o, o_r, small):
        flat = [a for row in small for a in row]
        half = M // 2

        def kernel(scal_r, n_r, nr_r, p_r, pr_r, g_r, gr_r, o_i, or_i, *refs):
            parts, outs, all_s = refs[: len(flat)], refs[len(flat) : -1], refs[-1]
            first = mm(n_r[...], p_r[...], TN) + mm(nr_r[...], pr_r[...], TN)
            second = mm(g_r[...], o_i[...], TN) + mm(gr_r[...], or_i[...], TN)
            both = jnp.concatenate([first.astype(bf16), second.astype(bf16)], 1)
            all_s[:, :M, :] = both.reshape(S, M, z.a_cols)
            wide, units, heads = [], [], []
            for l in range(L):
                pre, mid, last, up, qv = (r[...] for r in parts[5 * l : 5 * l + 5])
                wide += [pre[0:1], mid[0:1], pre[1:2], mid[1:3], last]
                units.append(up)
                heads.append(qv)
            wide = jnp.concatenate(wide + [jnp.zeros((TAIL - 6 * L, D), f32)], 0)
            pad = TAIL - 2 * L
            units = jnp.concatenate(units + [jnp.zeros((pad, F), f32)], 0).astype(bf16)
            heads = jnp.concatenate(heads + [jnp.zeros((pad, 3 * A), f32)], 0)
            part = 2 * HD // S
            for t in range(S):
                side, place = divmod(t, S // 2)
                cuts = []
                for h in range(H):
                    at = side * 2 * A + h * HD + place * part
                    cuts.append(heads[:, at : at + part])
                up = mm(units, spread(t, S, F), NT)
                rest = jnp.zeros((TAIL, z.a_cols - u_at - F // S), f32)
                all_s[t, M:, :] = jnp.concatenate(
                    [wide[:, t * M : (t + 1) * M]] + cuts + [up, rest], 1
                ).astype(bf16)
            if S == 4:
                outs[3][...] = all_s[scal_r[12], :half, :]
                outs[4][...] = all_s[scal_r[12], half:, :]
                send(outs[3], outs[4])
                for o_, at in zip(outs[:3], (9, 11, 10)):
                    o_[...] = all_s[scal_r[at]]
            else:
                outs[0][...] = all_s[...]

        block = (M + TAIL, z.a_cols)
        outs = [((S,) + block, bf16, FAR)]
        if S == 4:
            outs = [(block, bf16, FAR)] * 3
            outs += [((half, z.a_cols), bf16, FAR), ((M + TAIL - half, z.a_cols), bf16, FAR)]
        return run(
            kernel,
            [Far(n1), Far(n1_r), dp, Far(dp_r), Far(g1), Far(g1_r), Far(o), Far(o_r)] + [Far(a) for a in flat],
            outs,
            [pltpu.VMEM((S,) + block, bf16)],
            scalars=scal,
            name="project_grads",
            us=3,
        )

    def own_grads(n1, n1_r, dp, dp_r, g1, g1_r, o, o_r):
        def kernel(n_r, nr_r, p_r, pr_r, g_r, gr_r, o_i, or_i, out):
            first = mm(n_r[...], p_r[...], TN) + mm(nr_r[...], pr_r[...], TN)
            second = mm(g_r[...], o_i[...], TN) + mm(gr_r[...], or_i[...], TN)
            both = jnp.concatenate([first.astype(bf16), second.astype(bf16)], 1)
            out[...] = both.reshape(S, M, z.a_cols)

        return run(
            kernel,
            [Far(n1), Far(n1_r), dp, Far(dp_r), Far(g1), Far(g1_r), Far(o), Far(o_r)],
            [((S, M, z.a_cols), bf16, FAR)],
            name="own_grads",
            us=3,
        )[0]

    def pass_on(up, down, low, high):
        half = M // 2

        def kernel(up_r, down_r, low_r, high_r, up_o, down_o):
            up_o[:half, :] = (up_r[:half, :].astype(f32) + low_r[...].astype(f32)).astype(bf16)
            up_o[half:, :] = up_r[half:, :]
            send(up_o)
            down_o[:half, :] = down_r[:half, :]
            down_o[half:, :] = (down_r[half:, :].astype(f32) + high_r[...].astype(f32)).astype(bf16)

        return run(
            kernel,
            [Far(up), Far(down), Far(low), Far(high)],
            [((M + TAIL, z.a_cols), bf16, FAR)] * 2,
            name="pass_on",
        )

    def join_rows(scal, mine, theirs):
        def kernel(scal_r, a, b, o):
            start = pl.multiple_of(scal_r[8] * R, 16)
            o[pl.ds(start, R), :] = a[...]
            o[pl.ds(pl.multiple_of(R - start, 16), R), :] = b[...]

        return run(kernel, [Far(mine), Far(theirs)], [((2 * R, D), bf16, FAR)], scalars=scal, name="join_rows")[0]

    def sum_blocks(own, others):
        def kernel(own_r, a_r, b_r, o):
            o[...] = (own_r[...].astype(f32) + a_r[...].astype(f32) + b_r[...].astype(f32)).astype(bf16)

        return run(
            kernel,
            [Far(a) for a in [own] + others],
            [((M + TAIL, z.a_cols), bf16, FAR)],
            name="sum_blocks",
        )[0]

    def feed_out(pairs):
        def kernel(*refs):
            up_o, down_o = refs[-2:]
            for l in range(L):
                total = refs[2 * l][...].astype(f32) + refs[2 * l + 1][...].astype(f32)
                up_o[l] = total[:, :F]
                down_o[l] = total[:, F:]

        return run(
            kernel,
            [Far(a) for p in pairs for a in p],
            [((L, M, F), f32, FAR), ((L, M, F), f32, FAR)],
            name="feed_out",
        )

    def proj_out(pairs):
        def kernel(*refs):
            qkv_o, out_o = refs[-2:]
            for l in range(L):
                total = refs[2 * l][...].astype(f32) + refs[2 * l + 1][...].astype(f32)
                if l == 0:
                    total = total[:M]
                for h in range(H):
                    cuts = [total[:, i * A + h * HD : i * A + (h + 1) * HD] for i in range(3)]
                    qkv_o[l, h] = jnp.concatenate(cuts, 1)
                out_o[l] = total[:, 3 * A :].T
        return run(
            kernel,
            [Far(a) for p in pairs for a in p],
            [((L, H, M, 3 * HD), f32, FAR), ((L, A, M), f32, FAR)],
            name="project_out",
        )

    def small_sum(mine, theirs):
        def kernel(a_r, b_r, o):
            o[...] = a_r[M:, :].astype(f32) + b_r[M:, :].astype(f32)

        return run(kernel, [Far(mine), Far(theirs)], [((TAIL, z.a_cols), f32, FAR)], name="small_sum")[0]

    def small_out(scal, mine, x_side, core_side, far_side):
        def kernel(scal_r, a_r, x_r, c_r, f_r, qvb_o, upb_o, gain_o, shift_o):
            both = a_r[...] + c_r[...]
            other = x_r[...] + f_r[...]
            odd = scal_r[8] == 1
            part, unit = 2 * HD // S, 64 // S
            for l in range(L):
                rows = both[6 * l : 6 * l + 6, :M]
                first, third = rows[0:1], rows[2:3]
                if l == 0:
                    first, third = first + other[0:1, :M], third + other[2:3, :M]
                gain_o[l] = jnp.concatenate([first, rows[1:2]], 0)
                shift_o[l] = jnp.concatenate([third, rows[3:6]], 0)
                bias = jnp.where(odd, both[2 * l + 1 : 2 * l + 2], both[2 * l : 2 * l + 1])
                for h in range(H):
                    qvb_o[h, l : l + 1, :] = bias[:, q_at + h * part : q_at + (h + 1) * part]
                for r in range(F // 64):
                    upb_o[r, l : l + 1, :] = bias[:, u_at + r * unit : u_at + (r + 1) * unit]

        return run(
            kernel,
            [Far(mine), Far(x_side), Far(core_side), Far(far_side)],
            [
                ((H, L, 2 * HD // S), f32),
                ((F // 64, L, 64 // S), f32),
                ((L, 2, M), f32),
                ((L, 4, M), f32),
            ],
            scalars=scal,
            name="small_out",
        )

    def input_back(x, dy, pa, pb, vec):
        def kernel(x_r, dy_r, pa_r, pb_r, vec_r, o, sums_o):
            dn = pa_r[...].astype(f32) + pb_r[...].astype(f32)
            dx, dgain, dshift = ln_back(x_r[...].astype(f32), vec_r[0:1, :], dn)
            o[...] = (dy_r[...] + dx).astype(bf16)
            sums_o[0:1, :] = dgain
            sums_o[1:2, :] = dshift

        return run(kernel, [x, dy, pa, pb, vec], [((R, D), bf16, FAR), ((2, D), f32)], name="input_back")

    return dict(locals())


def local(mesh):
    def fn(frames, cotangent, w_qkv, qv_bias, w_out, w_up, up_bias, w_down, norm_gains, shifts):
        z = Sizes(mesh, frames, w_qkv, w_up)
        assert frames.shape[0] == 1
        k = make(z)
        L, m, R, D, A, F, H, HD, S = z.layers, z.m, z.rows, z.width, z.att, z.hidden, z.heads, z.hd, z.shards
        core = lax.axis_index("tc")
        scal = ring_scalars(S)

        def part_a(l, *then):
            qkv = after(w_qkv[l], *then).reshape(m, H, 3, HD).transpose(0, 2, 1, 3).reshape(m, 3 * A)
            return jnp.concatenate([qkv, after(w_out[l], *then).reshape(A, m).T], -1)

        def part_b(l, *then):
            return jnp.concatenate([after(w_up[l], *then), after(w_down[l], *then).T], -1)

        message = k["pack_first"](
            w_qkv, w_out, qv_bias, up_bias, norm_gains, shifts
        )
        w_a = [Pieces(message, TAIL) if S == 4 else Gathered(message, S, TAIL)]
        w_b = [Gathered(after(part_b(0, message), *w_a[0].arrays[1:4]), S)]

        def my_rows(x):
            return lax.dynamic_slice_in_dim(x.reshape(2 * R, D), core * R, R, 0)

        kept = []
        x = my_rows(frames)
        for layer in range(L):
            if layer == 0:
                n1, q, kv, vec, qb, tails = k["proj"](scal, x, 0, w_a[0])
            else:
                n1, q, kv, x = k["proj"](scal, after(y, *hid[1:]), layer, w_a[layer], (vec, qb), (part, x_swap(part)))
            far = y_swap(kv)
            near = core_swap(kv)
            if layer + 1 < L:
                next_a, next_b = part_a(layer + 1, n1), part_b(layer + 1, n1)
            acc = k["attend_near"](q, (kv, near))
            kvs = (kv, near, far, core_swap(after(far, acc)))
            o0, o1, qa, o_own, o_snd, att_part = k["attend_far"](scal, q, kvs[2:], acc, w_a[layer])
            far = x_swap(att_part)
            n1_r, o_rcv = core_swap(n1), core_swap(o_snd)
            x = after(x, n1_r, o_rcv)
            if layer + 1 < L:
                w_a.append(Gathered(after(next_a, kvs[1]), S))
                w_b.append(Gathered(after(next_b, att_part), S))
            y, n2, *hid_gp, part = k["feed"](
                scal, x, att_part, far, vec, tails, layer, w_b[layer]
            )
            n2_r, hid_r, gp = core_swap(n2), core_swap(hid_gp[1]), hid_gp[2:]
            hid = (hid_gp[0], hid_r, n2_r)
            kept.append((x, n1, n1_r, kvs, qa, (o0, o1), o_own, o_rcv, y, n2, hid, gp))

        def whole_rows(mine):
            return k["join_rows"](scal, mine, core_swap(mine))[None]

        def scatter(grad):
            return lax.psum_scatter(grad.reshape(D, -1), "shard", scatter_dimension=0, tiled=True)

        y_last, part_last = y, part
        g = my_rows(cotangent)
        wide, d_qv, d_up = [None] * L, [None] * L, [None] * L
        sum_a, sum_b = [None] * L, [None] * L
        before = None
        for layer in reversed(range(L)):
            x, n1, n1_r, kvs, qa, os, o_own, o_rcv, y, n2, hid, gp = kept[layer]
            if before is None:
                swap_b, du, part, sum_g2 = k["feed_back"](scal, g, gp, layer, w_b[layer])
            else:
                gp = [after(gp[0], grad_a), gp[1]]
                swap_b, du, part, sum_g2, g, pre = k["feed_back"](scal, None, gp, layer, w_b[layer], before)
                wide[layer + 1] = [pre] + wide[layer + 1]
            far = x_swap(part)
            grad_b, d_up[layer] = k["feed_grads"](
                scal, n2, hid[2], hid[0], hid[1], swap_b, core_swap(swap_b), du
            )
            y = after(y, grad_b)
            if before is not None:
                sum_b[layer + 1] = (part_b_sum, y_swap(after(part_b_sum, part)))
                y = after(y, sum_b[layer + 1][1])
            if layer > 0:
                part_b_sum = scatter(after(grad_b, far))
            dy, g1, da, mid = k["middle_back"](
                scal, y, g, part, far, vec, os[0], os[1], layer, w_a[layer]
            )
            if layer == 0:
                part_b_sum = scatter(after(grad_b, da))
            g1_r = core_swap(g1)
            dqt, own, snd = k["attend_back"](qa, kvs[2:], da, ahead=layer > 0)
            cross = k["cross_sum"](own, core_swap(snd))
            dqt = after(dqt, cross, g1_r, *([part_a_sum] if layer == 0 else []))
            cross = y_swap(cross)
            dq, own, snd = k["attend_back"](qa, kvs[:2], da, dqt)
            snd = after(snd, cross)
            kv_parts = (own, core_swap(snd), cross)
            dp, dp_snd, part, d_qv[layer], *pre = k["proj_back"](
                scal, dq, kv_parts, layer, w_a[layer], *([x] if layer == 0 else [])
            )
            far = x_swap(part)
            swaps = (n1, n1_r, dp, core_swap(dp_snd), g1, g1_r, o_own, o_rcv)
            if layer > 0:
                grad_a = k["own_grads"](*swaps)
                part_a_sum = scatter(after(grad_a, far))
            else:
                sum_a[1] = (part_a_sum, y_swap(after(part_a_sum, part)))
                wide[0] = pre + [mid, sum_g2]
                small = [wide[l] + [d_up[l], d_qv[l]] for l in range(L)]
                blocks = k["proj_grads"](scal, *swaps, small)
            wide[layer] = pre + [mid, sum_g2]
            before = (x, dy, part, far, vec)
        grad_rows, _ = k["input_back"](x, after(dy, blocks[0]), part, far, vec)
        if S == 4:
            hops = [lax.ppermute(b, "shard", ring(s)) for b, s in zip(blocks[3:], (1, 3))]
            up, down = k["pass_on"](after(blocks[1], grad_rows, sum_a[1][1]), blocks[2], *hops)
            ready = up
            others = [lax.ppermute(up, "shard", ring(1)), lax.ppermute(down, "shard", ring(3))]
        else:
            ready = blocks[0]
        part_b_sum = after(part_b_sum, ready)
        sum_b[0] = (part_b_sum, y_swap(part_b_sum))
        far_last = x_swap(after(part_last, ready))
        last_rows = k["finish"](y_last, part_last, far_last, vec)[0]
        frames_grad = whole_rows(grad_rows)
        block = after(blocks[0], sum_b[0][1], frames_grad, last_rows)
        if S == 4:
            mine = k["sum_blocks"](block, others)
        else:
            mine = lax.psum_scatter(block, "shard", scatter_dimension=0, tiled=True)[0]
        theirs = y_swap(mine)
        sum_a[0] = (mine, theirs)
        out_frames = whole_rows(after(last_rows, mine))
        outs_up, outs_down = k["feed_out"]([sum_b[0], (after(sum_b[1][0], mine), sum_b[1][1])])
        tiny = k["small_sum"](after(mine, outs_up, out_frames), theirs)
        tiny_x = x_swap(tiny)
        tiny_c = core_swap(tiny)
        outs_qkv, outs_out = k["proj_out"]([(after(mine, tiny), theirs), sum_a[1]])
        tiny_f = core_swap(after(tiny_x, outs_qkv))
        g_qvb, g_upb, g_gains, g_shifts = k["small_out"](
            scal, tiny, tiny_x, tiny_c, tiny_f
        )
        return (
            out_frames,
            frames_grad,
            outs_qkv.transpose(0, 2, 1, 3),
            g_qvb.transpose(1, 0, 2),
            outs_out.reshape(L, H, HD, m),
            outs_up,
            g_upb.transpose(1, 0, 2),
            outs_down.transpose(0, 2, 1),
            g_gains,
            g_shifts,
        )

    return fn


def solution(mesh):
    assert mesh.axis_names == ("shard", "ctx", "tp") and mesh.shape["tp"] == 4 and mesh.shape["ctx"] == 2
    split = Mesh(mesh.devices.reshape(mesh.shape["shard"], 2, 2, 2), ("shard", "ctx", "tx", "tc"))
    tp = ("tx", "tc")
    specs = (
        P("shard", "ctx", None),
        P("shard", "ctx", None),
        P(None, "shard", tp, None),
        P(None, tp, "shard"),
        P(None, tp, None, "shard"),
        P(None, "shard", tp),
        P(None, tp, "shard"),
        P(None, tp, "shard"),
        P(None, None, "shard"),
        P(None, None, "shard"),
    )
    return jax.shard_map(local(split), mesh=split, in_specs=specs, out_specs=specs, check_vma=False)
```

```python
import math

import jax
import jax.numpy as jnp
from jax import lax
from jax.experimental import pallas as pl
from jax.experimental.pallas import tpu as pltpu
from jax.sharding import Mesh
from jax.sharding import PartitionSpec as P

f32 = jnp.float32
bf16 = jnp.bfloat16
EPSILON = 1e-05
NN = (((1,), (0,)), ((), ()))
NT = (((1,), (1,)), ((), ()))
TN = (((0,), (0,)), ((), ()))
VMEM_MIB = {
    "attend_far": 13,
    "attend_near": 10,
    "attend_back": 14,
    "feed": 16,
    "feed_back": 16,
    "feed_grads": 12,
    "own_grads": 9,
    "feed_out": 7.6,
    "finish": 6,
    "input_back": 10,
    "middle_back": 11,
    "pack_first": 6,
    "pair_grads": 9,
    "project": 9.5,
    "project_back": 9.5,
    "project_grads": 13,
    "project_out": 5,
}
WIDE = 128
TAIL = 16
COST = 200_000_000


def mm(a, b, dims=NN):
    return lax.dot_general(a, b, dims, preferred_element_type=f32)


def core_swap(x):
    return lax.ppermute(x, "tc", [(0, 1), (1, 0)])


def x_swap(x):
    return lax.ppermute(x, "tx", [(0, 1), (1, 0)])


def y_swap(x):
    return lax.ppermute(x, "ctx", [(0, 1), (1, 0)])


def after(x, *others):
    return lax.optimization_barrier((x,) + others)[0]


def ring(shift):
    return [(i, (i + shift) % 4) for i in range(4)]


def ring_scalars(shards):
    me = lax.axis_index("shard").astype(jnp.int32)
    zero = jnp.int32(0)
    order = [me, (me + shards - 1) % shards, (me + 1) % shards, (me + 2) % shards]
    return jnp.stack([zero] * 8 + [lax.axis_index("tc").astype(jnp.int32)] + order + [zero] * 3)


class Pieces:
    def __init__(self, x, tail=0):
        self.rows = x.shape[0] - tail
        self.mine = [x] + [lax.ppermute(x, "shard", ring(s)) for s in (1, 3, 2)]
        self.arrays = self.mine + [core_swap(p) for p in self.mine]

    def copies(self, scal, refs, columns, dest, sems):
        out = []
        for k, ref in enumerate(refs):
            slot = scal[8] if k < 4 else 1 - scal[8]
            to = dest.at[slot, scal[9 + k % 4]]
            out.append(pltpu.make_async_copy(ref.at[pl.ds(0, self.rows), columns], to, sems.at[k]))
        return out

    def tails(self, scal, refs, dest, sems):
        out = []
        for k, ref in enumerate(refs):
            slot = scal[8] if k < 4 else 1 - scal[8]
            to = dest.at[slot, scal[9 + k % 4]]
            out.append(pltpu.make_async_copy(ref.at[pl.ds(self.rows, TAIL), :], to, sems.at[k]))
        return out


class Gathered:
    def __init__(self, x, shards, tail=0):
        self.rows = x.shape[0] - tail
        whole = lax.all_gather(x, ("shard", "tc"), axis=0, tiled=False)
        self.arrays = [whole.reshape((shards, 2) + x.shape)]

    def copies(self, scal, refs, columns, dest, sems):
        ref = refs[0]
        return [
            pltpu.make_async_copy(ref.at[:, c, pl.ds(0, self.rows), columns], dest.at[c], sems.at[c])
            for c in range(2)
        ]

    def tails(self, scal, refs, dest, sems):
        ref = refs[0]
        return [
            pltpu.make_async_copy(ref.at[:, c, pl.ds(self.rows, TAIL), :], dest.at[c], sems.at[c])
            for c in range(2)
        ]


def vmem():
    return pl.BlockSpec(memory_space=pltpu.VMEM)


class Far:
    def __init__(self, array):
        self.array = array


class Reading:
    def __init__(self, buffer, copy):
        self.buffer, self.copy, self.waited = buffer, copy, False

    def need(self):
        if not self.waited:
            self.copy.wait()
            self.waited = True
        return self.buffer

    def __getitem__(self, index):
        return self.need()[index]

    @property
    def shape(self):
        return self.buffer.shape


class Writing:
    def __init__(self, buffer, copy):
        self.buffer, self.copy, self.sent = buffer, copy, False

    def __setitem__(self, index, value):
        self.buffer[index] = value

    @property
    def at(self):
        return self.buffer.at

    def send(self):
        if not self.sent:
            self.copy.start()
            self.sent = True


def send(*refs):
    for r in refs:
        if isinstance(r, Writing):
            r.send()


def need(*refs):
    for r in refs:
        if isinstance(r, Reading):
            r.need()


FAR = "far"


def run(kernel, ins, outs, scratch=(), w=None, scalars=None, name=None, us=1.0):
    pieces = [] if w is None else w.arrays
    n_in, n_out, n_pieces = len(ins), len(outs), len(pieces)
    far_in = [i for i, a in enumerate(ins) if isinstance(a, Far)]
    far_out = [i for i, o in enumerate(outs) if len(o) == 3]
    any_space = pl.BlockSpec(memory_space=pl.ANY)
    specs, args = [], []
    if scalars is not None:
        specs.append(pl.BlockSpec(memory_space=pltpu.SMEM))
        args.append(scalars)
    for a in ins:
        if isinstance(a, Far):
            specs.append(any_space)
            args.append(pltpu.with_memory_space_constraint(a.array, pltpu.HBM))
        else:
            specs.append(vmem())
            args.append(a)
    for p in pieces:
        specs.append(any_space)
        args.append(pltpu.with_memory_space_constraint(p, pltpu.HBM))
    first = len(args) - n_in - n_pieces
    shapes = [
        pltpu.HBM(o[0], o[1]) if len(o) == 3 else jax.ShapeDtypeStruct(o[0], o[1]) for o in outs
    ]
    buffers = [pltpu.VMEM(ins[i].array.shape, ins[i].array.dtype) for i in far_in]
    buffers += [pltpu.VMEM(outs[i][0], outs[i][1]) for i in far_out]
    sems = [pltpu.SemaphoreType.DMA((len(buffers),))] if buffers else []

    def wrapped(*refs):
        refs = list(refs)
        n_all = len(args) + n_out + len(scratch)
        own, extra = refs[:n_all], refs[n_all:]
        reads, writes = [], []
        for k, i in enumerate(far_in):
            copy = pltpu.make_async_copy(own[first + i], extra[k], extra[-1].at[k])
            copy.start()
            own[first + i] = Reading(extra[k], copy)
            reads.append(own[first + i])
        for k, i in enumerate(far_out):
            k += len(far_in)
            at = len(args) + i
            own[at] = Writing(extra[k], pltpu.make_async_copy(extra[k], own[at], extra[-1].at[k]))
            writes.append(own[at])
        kernel(*own)
        for w in writes:
            w.send()
        for r in reads:
            r.need()
        for w in writes:
            w.copy.wait()

    return pl.pallas_call(
        wrapped,
        out_shape=shapes,
        in_specs=specs,
        out_specs=[any_space if len(o) == 3 else vmem() for o in outs],
        scratch_shapes=list(scratch) + buffers + sems,
        compiler_params=pltpu.CompilerParams(vmem_limit_bytes=int(VMEM_MIB.get(name, 4) * 1024 * 1024)),
        cost_estimate=pl.CostEstimate(flops=int(us * COST), bytes_accessed=1000, transcendentals=0),
        name=name,
    )(*args)


def spread(shard, shards, units):
    part = 64 // shards
    bits, low = part.bit_length() - 1, part - 1
    i = lax.broadcasted_iota(jnp.int32, (units // shards, units), 0)
    j = lax.broadcasted_iota(jnp.int32, (units // shards, units), 1)
    same = ((j >> 6) == (i >> bits)) & ((j & 63) == shard * part + (i & low))
    return jnp.where(same, 1.0, 0.0).astype(bf16)


def start_all(copies):
    for c in copies:
        c.start()


def wait_all(copies):
    for c in copies:
        c.wait()


def ln_parts(x):
    centred = x - jnp.mean(x, -1, keepdims=True)
    inv = lax.rsqrt(jnp.mean(centred * centred, -1, keepdims=True) + EPSILON)
    return centred * inv, inv


def ln_back(x, gain, dn):
    hat, inv = ln_parts(x)
    dhat = dn * gain
    dx = inv * (
        dhat
        - jnp.mean(dhat, -1, keepdims=True)
        - hat * jnp.mean(dhat * hat, -1, keepdims=True)
    )
    return dx, jnp.sum(dn * hat, 0, keepdims=True), jnp.sum(dn, 0, keepdims=True)


def split3(v):
    a = v.astype(bf16)
    r = v - a.astype(f32)
    b = r.astype(bf16)
    c = (r - b.astype(f32)).astype(bf16)
    return a, b, c


def beside(wide, column):
    a, b, c = split3(column)
    rows, size = wide.shape[0], wide.shape[1]
    return jnp.concatenate([wide, a, b, c, jnp.zeros((rows, WIDE - size - 3), bf16)], 1)


class Sizes:
    def __init__(self, mesh, frames, w_qkv, w_up):
        self.shards = mesh.shape["shard"]
        self.layers = w_qkv.shape[0]
        self.width = frames.shape[-1]
        self.rows = frames.shape[1] // 2
        self.heads = w_qkv.shape[2]
        self.hd = w_qkv.shape[3] // 3
        self.att = self.heads * self.hd
        self.hidden = w_up.shape[2]
        self.m = w_qkv.shape[1]
        self.a_cols = 4 * self.att
        self.b_cols = 2 * self.hidden


def make(z):
    R, D, A, H, HD, F = z.rows, z.width, z.att, z.heads, z.hd, z.hidden
    L, S, M = z.layers, z.shards, z.m
    coef = HD ** (-0.5) / math.log(2.0)
    scale = HD ** (-0.5)
    dma = pltpu.SemaphoreType.DMA
    q_at, u_at = M, M + 2 * A // S

    def weight_scratch(columns):
        return [pltpu.VMEM((2, S, M, columns), bf16), dma((8,))]

    def weight(w_s, c, start, stop):
        return w_s[c, :, :, start:stop].reshape(D, stop - start)

    def pack_first(w_qkv, w_out, qv_bias, up_bias, norm_gains, shifts):
        nq, nu = 2 * HD // S, 64 // S

        def kernel(w_r, o_r, qv_r, up_r, g_r, s_r, out):
            for side in range(3):
                cuts = [w_r[0, h][:, side * HD : (side + 1) * HD] for h in range(H)]
                out[:M, side * A : (side + 1) * A] = jnp.concatenate(cuts, 1)
            out[:M, 3 * A :] = o_r[0].astype(f32).T.astype(bf16)
            vecs = []
            for l in range(L):
                vecs += [g_r[l].astype(f32), s_r[l].astype(f32)]
            vecs = jnp.concatenate(vecs + [jnp.zeros((TAIL - 6 * L, M), f32)], 0)
            rows = []
            for l in range(L):
                cuts = [qv_r[h].astype(f32)[l : l + 1, :] for h in range(H)]
                cuts += [up_r[r].astype(f32)[l : l + 1, :] for r in range(F // 64)]
                rows.append(jnp.concatenate(cuts, 1))
            rows = jnp.concatenate(rows + [jnp.zeros((TAIL - L, H * nq + F // 64 * nu), f32)], 0)
            rest = jnp.zeros((TAIL, z.a_cols - M - rows.shape[1]), f32)
            out[M:, :] = jnp.concatenate([vecs, rows, rest], 1).astype(bf16)

        return run(
            kernel,
            [
                Far(a)
                for a in (
                    w_qkv.transpose(0, 2, 1, 3),
                    w_out.reshape(L, A, M),
                    qv_bias.transpose(1, 0, 2),
                    up_bias.transpose(1, 0, 2),
                    norm_gains,
                    shifts,
                )
            ],
            [((M + TAIL, z.a_cols), bf16, FAR)],
            name="pack_first",
        )[0]

    def proj(scal, x, layer, w, biases=None, prev=None):
        first = biases is None
        n = len(w.arrays)
        part = 2 * HD // S

        def kernel(*refs):
            it = iter(refs)
            scal_r, x_r = next(it), next(it)
            if not first:
                vec_r, qb_r, pa_r, pb_r = (next(it) for _ in range(4))
            piece_r = [next(it) for _ in range(n)]
            n_o, q_o, kv_o = (next(it) for _ in range(3))
            if first:
                vec_r, qb_r, tail_o = (next(it) for _ in range(3))
            else:
                x_o = next(it)
            w_s, sems = next(it), next(it)
            if first:
                tail_sems = next(it)
                tails = w.tails(scal_r, piece_r, tail_o, tail_sems)
                start_all(tails)
            copies = w.copies(scal_r, piece_r, pl.ds(0, z.a_cols), w_s, sems)
            start_all(copies)
            xv = x_r[...].astype(f32)
            if not first:
                at = 6 * (layer - 1) + 5
                xv = xv + (pa_r[...].astype(f32) + pb_r[...].astype(f32) + vec_r[at : at + 1, :])
                x_o[...] = xv
                send(x_o)
            hat, _ = ln_parts(xv)
            if first:
                wait_all(tails)
                vec_r[...] = jnp.concatenate([tail_o[0, t][:, :M] for t in range(S)], 1).astype(f32)
                for l in range(L):
                    for p in range(2):
                        rows = [tail_o[p, t].astype(f32)[l : l + 1, q_at:u_at] for t in range(S)]
                        seq = []
                        for side in range(2):
                            for h in range(H):
                                seq += [
                                    rows[t][:, h * part : (h + 1) * part]
                                    for t in range(side * S // 2, (side + 1) * S // 2)
                                ]
                            if side == 0:
                                seq.append(jnp.zeros((1, A), f32))
                        qb_r[2 * l + p : 2 * l + p + 1, :] = jnp.concatenate(seq, 1)
            g = 6 * layer
            nv = (hat * vec_r[g : g + 1, :] + vec_r[g + 2 : g + 3, :]).astype(bf16)
            n_o[...] = nv
            send(n_o)
            wait_all(copies)
            both = []
            for e in range(2):
                b = 2 * layer + e
                p = (mm(nv, weight(w_s, e, 0, 3 * A)) + qb_r[b : b + 1, :]).astype(bf16)
                kv_o[:, e * 2 * A : (e + 1) * 2 * A] = p[:, A:]
                both.append(p[:, :A])
            send(kv_o)
            q_o[...] = jnp.concatenate(both, 1)

        ins = [Far(x)] + ([] if first else list(biases) + [Far(prev[0]), prev[1]])
        outs = [((R, D), bf16, FAR), ((R, 2 * A), bf16), ((R, 4 * A), bf16, FAR)]
        scratch = weight_scratch(z.a_cols)
        if first:
            outs += [((TAIL, D), f32), ((2 * L, 3 * A), f32), ((2, S, TAIL, z.a_cols), bf16)]
            scratch += [dma((8,))]
        else:
            outs += [((R, D), f32, FAR)]
        return run(kernel, ins, outs, scratch, w, scal, "project", 3.5)

    def aug(block, offset, fill):
        return jnp.concatenate([block[:, offset : offset + HD], fill], 1)

    def head_lanes(j):
        e, h = divmod(j, H)
        return j * HD, e * 2 * A + h * HD, e * 2 * A + A + h * HD

    def load_heads(kv_refs, k_s, v_s):
        ones = jnp.ones((R, HD), bf16)
        for b, ref in enumerate(kv_refs):
            blk = ref[...]
            for j in range(2 * H):
                _, k_at, v_at = head_lanes(j)
                k_s[j, b * R : (b + 1) * R, :] = aug(blk, k_at, ones)
                v_s[j, b * R : (b + 1) * R, :] = aug(blk, v_at, ones)

    def attend_near(q, kvs):
        K = 2 * R

        def kernel(q_r, kv0, kv1, acc_o, q_s, k_s, v_s):
            zeros = jnp.zeros((R, HD), bf16)
            for j in range(2 * H):
                q_s[j] = aug(q_r[...], j * HD, zeros)
            load_heads((kv0, kv1), k_s, v_s)

            def head(j, carry):
                s = mm(q_s[j], k_s[j], NT)
                top = jnp.max(s, -1, keepdims=True)
                oe = mm(jnp.exp2((s - top) * coef).astype(bf16), v_s[j])
                acc_o[j] = jnp.concatenate(
                    [oe[:, : HD + 1], top, jnp.zeros((R, WIDE - HD - 2), f32)], 1
                )
                return carry

            lax.fori_loop(0, 2 * H, head, 0)

        return run(
            kernel,
            [q] + list(kvs),
            [((2 * H, R, WIDE), f32)],
            [pltpu.VMEM((2 * H, R, WIDE), bf16)] + [pltpu.VMEM((2 * H, K, WIDE), bf16)] * 2,
            name="attend_near",
            us=6,
        )[0]

    def attend_far(scal, q, kvs, acc, w):
        K = 2 * R
        n = len(w.arrays)

        def kernel(scal_r, q_r, kv2, kv3, acc_r, *refs):
            piece_r = refs[:n]
            o0_o, o1_o, qa_o, own_o, snd_o, part_o, q_s, k_s, v_s, o_s, w_s, sems = refs[n:]
            copies = w.copies(scal_r, piece_r, pl.ds(z.a_cols - 256, 256), w_s, sems)
            start_all(copies)
            zeros = jnp.zeros((R, HD), bf16)
            for j in range(2 * H):
                q_s[j] = aug(q_r[...], j * HD, zeros)
            load_heads((kv2, kv3), k_s, v_s)

            def head(j, carry):
                s = mm(q_s[j], k_s[j], NT)
                old = acc_r[j]
                old_top = old[:, HD + 1 : HD + 2]
                top = jnp.maximum(jnp.max(s, -1, keepdims=True), old_top)
                oe = mm(jnp.exp2((s - top) * coef).astype(bf16), v_s[j])
                oe = oe + old * jnp.exp2((old_top - top) * coef)
                total = oe[:, HD : HD + 1]
                o_s[j] = (oe[:, :HD] / total).astype(bf16)
                lse = top + jnp.log2(total) * (1.0 / coef)
                qa_o.buffer[j] = beside(q_s[j][:, :HD], -lse)
                return carry

            lax.fori_loop(0, 2 * H, head, 0)
            send(qa_o)
            o0 = jnp.concatenate([o_s[j] for j in range(H)], 1)
            o1 = jnp.concatenate([o_s[H + j] for j in range(H)], 1)
            wait_all(copies)
            part = mm(o0, weight(w_s, 0, 256 - A, 256), NT) + mm(o1, weight(w_s, 1, 256 - A, 256), NT)
            part_o[...] = part.astype(bf16)
            send(part_o)
            odd = scal_r[8] == 1
            o0_o[...] = o0
            o1_o[...] = o1
            own_o[...] = jnp.where(odd, o1, o0)
            snd_o[...] = jnp.where(odd, o0, o1)

        return run(
            kernel,
            [q] + list(kvs) + [acc],
            [((R, A), bf16, FAR)] * 2
            + [((2 * H, R, WIDE), bf16, FAR)]
            + [((R, A), bf16, FAR)] * 2
            + [((R, D), bf16, FAR)],
            [pltpu.VMEM((2 * H, R, WIDE), bf16)]
            + [pltpu.VMEM((2 * H, K, WIDE), bf16)] * 2
            + [pltpu.VMEM((2 * H, R, HD), bf16)]
            + weight_scratch(256),
            w,
            scal,
            "attend_far",
            8,
        )

    def feed(scal, x, pa, pb, vec, tails, layer, w):
        n = len(w.arrays)
        g = 6 * layer

        def kernel(scal_r, x_r, pa_r, pb_r, vec_r, tail_r, *refs):
            piece_r = refs[:n]
            y_o, n_o, *hid_gp, part_o, w_s, sems = refs[n:]
            copies = w.copies(scal_r, piece_r, pl.ds(0, 2 * F), w_s, sems)
            start_all(copies)
            y = x_r[...].astype(f32) + (
                pa_r[...].astype(f32) + pb_r[...].astype(f32) + vec_r[g + 3 : g + 4, :]
            )
            y_o[...] = y
            send(y_o)
            hat, _ = ln_parts(y)
            nv = (hat * vec_r[g + 1 : g + 2, :] + vec_r[g + 4 : g + 5, :]).astype(bf16)
            n_o[...] = nv
            send(n_o)
            bias = [None, None]
            for t in range(S):
                e = spread(t, S, F)
                for s in range(2):
                    add = mm(tail_r[s, t][:, u_at : u_at + F // S], e)
                    bias[s] = add if t == 0 else bias[s] + add
            part, hiddens = None, []
            for s in range(2):
                copies[s].wait()
                u = mm(nv, weight(w_s, s, 0, F)) + bias[s][layer : layer + 1, :]
                cdf = 0.5 * (1.0 + lax.erf(u * (0.5**0.5)))
                pdf = jnp.exp(-0.5 * u * u) * (1.0 / math.sqrt(2.0 * math.pi))
                hidden = (u * cdf).astype(bf16)
                hid_gp[2 + s][...] = (cdf + u * pdf).astype(bf16)
                send(hid_gp[2 + s])
                hiddens.append(hidden)
                t = mm(hidden, weight(w_s, s, F, 2 * F), NT)
                part = t if part is None else part + t
            part_o[...] = part.astype(bf16)
            send(part_o)
            odd = scal_r[8] == 1
            hid_gp[0][...] = jnp.where(odd, hiddens[1], hiddens[0])
            hid_gp[1][...] = jnp.where(odd, hiddens[0], hiddens[1])

        outs = [
            ((R, D), f32, FAR),
            ((R, D), bf16, FAR),
            ((R, F), bf16, FAR),
            ((R, F), bf16, FAR),
            ((R, F), bf16, FAR),
            ((R, F), bf16, FAR),
            ((R, D), bf16, FAR),
        ]
        return run(
            kernel, [Far(x), Far(pa), pb, vec, tails], outs, weight_scratch(2 * F), w, scal, "feed", 6
        )

    def finish(y, pa, pb, vec):
        at = 6 * (L - 1) + 5

        def kernel(y_r, pa_r, pb_r, vec_r, o):
            v = y_r[...] + (pa_r[...].astype(f32) + pb_r[...].astype(f32) + vec_r[at : at + 1, :])
            o[...] = v.astype(bf16)

        return run(kernel, [Far(y), Far(pa), pb, vec], [((R, D), bf16, FAR)], name="finish")

    def feed_back(scal, grad, gp, layer, w, before=None):
        n = len(w.arrays)
        up = 6 * (layer + 1)

        def kernel(*refs):
            it = iter(refs)
            scal_r = next(it)
            if before is None:
                g_r = next(it)
            else:
                x_r, dy_r, pa_r, pb_r, vec_r = (next(it) for _ in range(5))
            gp_r = (next(it), next(it))
            piece_r = [next(it) for _ in range(n)]
            swap_o, du_o, part_o, sums_o = (next(it) for _ in range(4))
            if before is not None:
                g_o, pre_o = next(it), next(it)
            w_s, sems = next(it), next(it)
            copies = w.copies(scal_r, piece_r, pl.ds(0, 2 * F), w_s, sems)
            start_all(copies)
            if before is None:
                g = g_r[...].astype(f32)
            else:
                dn = pa_r[...].astype(f32) + pb_r[...].astype(f32)
                dx, dgain, dshift = ln_back(x_r[...], vec_r[up : up + 1, :], dn)
                g = dy_r[...] + dx
                g_o[...] = g
                pre_o[0:1, :] = dgain
                pre_o[1:2, :] = dshift
            g2 = g.astype(bf16)
            swap_o[:, :D] = g2
            sums_o[...] = jnp.sum(g2.astype(f32), 0, keepdims=True)
            wait_all(copies)
            odd = scal_r[8] == 1
            part = None
            for k in range(2):
                slot = scal_r[8] if k else 1 - scal_r[8]
                first, second = (gp_r[1][...], gp_r[0][...]) if k else (gp_r[0][...], gp_r[1][...])
                slope = jnp.where(odd, first, second).astype(f32)
                du = (slope * mm(g2, weight(w_s, slot, F, 2 * F))).astype(bf16)
                if k == 0:
                    swap_o[:, D:] = du
                    send(swap_o)
                else:
                    du_o[...] = du
                t = mm(du, weight(w_s, slot, 0, F), NT)
                part = t if part is None else part + t
            part_o[...] = part.astype(bf16)

        ins = [grad] if before is None else [Far(b) for b in before[:3]] + list(before[3:])
        ins += [Far(gp[0]), Far(gp[1])]
        outs = [((R, D + F), bf16, FAR), ((R, F), bf16), ((R, D), bf16, FAR), ((1, D), f32)]
        if before is not None:
            outs += [((R, D), f32), ((2, D), f32)]
        return run(kernel, ins, outs, weight_scratch(2 * F), w, scal, "feed_back", 6)

    def blocks_out(scal_r, full, outs):
        if S == 4:
            for o, at in zip(outs, (9, 11, 10, 12)):
                o[...] = full[scal_r[at]]
        else:
            outs[0][...] = full[...]

    def block_shapes(rows, columns):
        return [((rows, columns), bf16, FAR)] * 4 if S == 4 else [((S, rows, columns), bf16, FAR)]

    def feed_grads(scal, n2, n2_r, hid, hid_r, swap, swap_r, du):
        def kernel(scal_r, n_r, nr_r, h_r, hr_r, s_r, sr_r, du_r, g_o, b_o):
            other = sr_r[:, D:]
            g_o[:, :F] = (mm(n_r[...], du_r[...], TN) + mm(nr_r[...], other, TN)).astype(bf16)
            g_o[:, F:] = (mm(s_r[:, :D], h_r[...], TN) + mm(sr_r[:, :D], hr_r[...], TN)).astype(bf16)
            total = jnp.sum(du_r[...].astype(f32), 0, keepdims=True) + jnp.sum(
                other.astype(f32), 0, keepdims=True
            )
            odd = scal_r[8] == 1
            b_o[0:1, :] = jnp.where(odd, 0.0, total)
            b_o[1:2, :] = jnp.where(odd, total, 0.0)

        return run(
            kernel,
            [Far(n2), Far(n2_r), Far(hid), Far(hid_r), Far(swap), Far(swap_r), du],
            [((D, 2 * F), bf16, FAR), ((2, F), f32)],
            scalars=scal,
            name="feed_grads",
            us=3,
        )

    def middle_back(scal, y, g, pa, pb, vec, o0, o1, layer, w):
        n = len(w.arrays)
        gain = 6 * layer + 1

        def kernel(scal_r, y_r, g_r, pa_r, pb_r, vec_r, o0_r, o1_r, *refs):
            piece_r = refs[:n]
            dy_o, g1_o, d_o, sums_o, w_s, sems = refs[n:]
            copies = w.copies(scal_r, piece_r, pl.ds(z.a_cols - 256, 256), w_s, sems)
            start_all(copies)
            dn = pa_r[...].astype(f32) + pb_r[...].astype(f32)
            dx, dgain, dshift = ln_back(y_r[...], vec_r[gain : gain + 1, :], dn)
            dy = g_r[...].astype(f32) + dx
            dy_o[...] = dy
            send(dy_o)
            g1 = dy.astype(bf16)
            g1_o[...] = g1
            send(g1_o)
            sums_o[0:1, :] = dgain
            sums_o[1:2, :] = jnp.sum(g1.astype(f32), 0, keepdims=True)
            sums_o[2:3, :] = dshift
            wait_all(copies)
            for e, o_r in enumerate((o0_r, o1_r)):
                do = mm(g1, weight(w_s, e, 256 - A, 256)).astype(bf16)
                prod = do.astype(f32) * o_r[...].astype(f32)
                for h in range(H):
                    lanes = slice(h * HD, (h + 1) * HD)
                    d_o[e * H + h] = beside(do[:, lanes], -jnp.sum(prod[:, lanes], -1, keepdims=True))

        outs = [((R, D), f32, FAR), ((R, D), bf16, FAR), ((2 * H, R, WIDE), bf16), ((3, D), f32)]
        return run(
            kernel,
            [Far(y), g, Far(pa), pb, vec, Far(o0), Far(o1)],
            outs,
            weight_scratch(256),
            w,
            scal,
            "middle_back",
            4,
        )

    def attend_back(qa, kvs, da, before=None, ahead=False):
        K = 2 * R

        def kernel(qa_r, kv0, kv1, da_r, *refs):
            refs = list(refs)
            if before is not None:
                old_r = refs.pop(0)
            dq_o, e0, e1, k_s, v_s, dk_s, dv_s, *dq_s = refs
            need(qa_r)
            load_heads((kv0, kv1), k_s, v_s)

            def head(j, carry):
                qv = qa_r[j]
                dv_in = da_r[j]
                dqt = None
                for b in range(2):
                    at = slice(b * R, (b + 1) * R)
                    kb = k_s[j, at, :]
                    p = jnp.exp2(mm(kb, qv, NT) * coef)
                    ds = (p * mm(v_s[j, at, :], dv_in, NT)).astype(bf16)
                    dv_s[j, at, :] = mm(p.astype(bf16), dv_in).astype(bf16)
                    dk_s[j, at, :] = (mm(ds, qv) * scale).astype(bf16)
                    t = mm(kb, ds, TN)
                    dqt = t if dqt is None else dqt + t
                if before is None:
                    dq_o[j] = dqt
                else:
                    dq_s[0][j] = ((dqt + old_r[j]).T * scale).astype(bf16)
                return carry

            lax.fori_loop(0, 2 * H, head, 0)
            for b, e_o in ((1, e1), (0, e0)):
                at = slice(b * R, (b + 1) * R)
                cols = []
                for e in range(2):
                    cols += [dk_s[e * H + h, at, :HD] for h in range(H)]
                    cols += [dv_s[e * H + h, at, :HD] for h in range(H)]
                e_o[...] = jnp.concatenate(cols, 1)
                send(e_o)
            if before is not None:
                dq_o[...] = jnp.concatenate([dq_s[0][j][:, :HD] for j in range(2 * H)], 1)

        ins = [qa] + list(kvs) + [da]
        if before is None and not ahead:
            ins = [Far(a) for a in ins[:3]] + [da]
        outs = [((R, 4 * A), bf16), ((R, 4 * A), bf16, FAR)]
        scratch = [pltpu.VMEM((2 * H, K, WIDE), bf16)] * 4
        if before is None:
            outs = [((2 * H, WIDE, R), f32)] + outs
        else:
            ins.append(before)
            outs = [((R, 2 * A), bf16)] + outs
            scratch.append(pltpu.VMEM((2 * H, R, WIDE), bf16))
        return run(kernel, ins, outs, scratch, name="attend_back", us=8)

    def cross_sum(own, theirs):
        def kernel(a, b, o):
            o[...] = (a[...].astype(f32) + b[...].astype(f32)).astype(bf16)

        return run(kernel, [own, theirs], [(own.shape, bf16, FAR)], name="cross_sum")[0]

    def proj_back(scal, dq, kv_parts, layer, w, x=None):
        n = len(w.arrays)

        def kernel(scal_r, q_r, a, p, c, *refs):
            refs = list(refs)
            if x is not None:
                x_r = refs.pop(0)
            piece_r, refs = refs[:n], refs[n:]
            own_o, snd_o, part_o, b_o = refs[:4]
            w_s, sems = refs[-2:]
            copies = w.copies(scal_r, piece_r, pl.ds(0, z.a_cols), w_s, sems)
            start_all(copies)
            both = []
            for e in range(2):
                at = slice(e * 2 * A, (e + 1) * 2 * A)
                total = a[:, at].astype(f32) + p[:, at].astype(f32) + c[:, at].astype(f32)
                both.append(jnp.concatenate([q_r[:, e * A : (e + 1) * A], total.astype(bf16)], 1))
                b_o[e : e + 1, :] = jnp.sum(both[e].astype(f32), 0, keepdims=True)
            odd = scal_r[8] == 1
            own_o[...] = jnp.where(odd, both[1], both[0])
            snd_o[...] = jnp.where(odd, both[0], both[1])
            send(snd_o)
            if x is not None:
                hat, _ = ln_parts(x_r[...].astype(f32))
            wait_all(copies)
            part = mm(both[0], weight(w_s, 0, 0, 3 * A), NT) + mm(both[1], weight(w_s, 1, 0, 3 * A), NT)
            part_o[...] = part.astype(bf16)
            if x is not None:
                send(part_o)
                refs[4][0:1, :] = jnp.sum(part * hat, 0, keepdims=True)
                refs[4][1:2, :] = jnp.sum(part, 0, keepdims=True)

        ins = [dq] + list(kv_parts)
        outs = [((R, 3 * A), bf16), ((R, 3 * A), bf16, FAR), ((R, D), bf16, FAR), ((2, 3 * A), f32)]
        if x is not None:
            ins.append(Far(x))
            outs.append(((2, D), f32))
        return run(kernel, ins, outs, weight_scratch(z.a_cols), w, scal, "project_back", 4)

    def proj_grads(scal, n1, n1_r, dp, dp_r, g1, g1_r, o, o_r, small):
        flat = [a for row in small for a in row]
        half = M // 2

        def kernel(scal_r, n_r, nr_r, p_r, pr_r, g_r, gr_r, o_i, or_i, *refs):
            parts, outs, all_s = refs[: len(flat)], refs[len(flat) : -1], refs[-1]
            first = mm(n_r[...], p_r[...], TN) + mm(nr_r[...], pr_r[...], TN)
            second = mm(g_r[...], o_i[...], TN) + mm(gr_r[...], or_i[...], TN)
            both = jnp.concatenate([first.astype(bf16), second.astype(bf16)], 1)
            all_s[:, :M, :] = both.reshape(S, M, z.a_cols)
            wide, units, heads = [], [], []
            for l in range(L):
                pre, mid, last, up, qv = (r[...] for r in parts[5 * l : 5 * l + 5])
                wide += [pre[0:1], mid[0:1], pre[1:2], mid[1:3], last]
                units.append(up)
                heads.append(qv)
            wide = jnp.concatenate(wide + [jnp.zeros((TAIL - 6 * L, D), f32)], 0)
            pad = TAIL - 2 * L
            units = jnp.concatenate(units + [jnp.zeros((pad, F), f32)], 0).astype(bf16)
            heads = jnp.concatenate(heads + [jnp.zeros((pad, 3 * A), f32)], 0)
            part = 2 * HD // S
            for t in range(S):
                side, place = divmod(t, S // 2)
                cuts = []
                for h in range(H):
                    at = side * 2 * A + h * HD + place * part
                    cuts.append(heads[:, at : at + part])
                up = mm(units, spread(t, S, F), NT)
                rest = jnp.zeros((TAIL, z.a_cols - u_at - F // S), f32)
                all_s[t, M:, :] = jnp.concatenate(
                    [wide[:, t * M : (t + 1) * M]] + cuts + [up, rest], 1
                ).astype(bf16)
            if S == 4:
                outs[3][...] = all_s[scal_r[12], :half, :]
                outs[4][...] = all_s[scal_r[12], half:, :]
                send(outs[3], outs[4])
                for o_, at in zip(outs[:3], (9, 11, 10)):
                    o_[...] = all_s[scal_r[at]]
            else:
                outs[0][...] = all_s[...]

        block = (M + TAIL, z.a_cols)
        outs = [((S,) + block, bf16, FAR)]
        if S == 4:
            outs = [(block, bf16, FAR)] * 3
            outs += [((half, z.a_cols), bf16, FAR), ((M + TAIL - half, z.a_cols), bf16, FAR)]
        return run(
            kernel,
            [Far(n1), Far(n1_r), dp, dp_r, Far(g1), Far(g1_r), Far(o), Far(o_r)] + [Far(a) for a in flat],
            outs,
            [pltpu.VMEM((S,) + block, bf16)],
            scalars=scal,
            name="project_grads",
            us=3,
        )

    def own_grads(n1, n1_r, dp, dp_r, g1, g1_r, o, o_r):
        def kernel(n_r, nr_r, p_r, pr_r, g_r, gr_r, o_i, or_i, out):
            first = mm(n_r[...], p_r[...], TN) + mm(nr_r[...], pr_r[...], TN)
            second = mm(g_r[...], o_i[...], TN) + mm(gr_r[...], or_i[...], TN)
            both = jnp.concatenate([first.astype(bf16), second.astype(bf16)], 1)
            out[...] = both.reshape(S, M, z.a_cols)

        return run(
            kernel,
            [Far(n1), Far(n1_r), dp, dp_r, Far(g1), Far(g1_r), Far(o), Far(o_r)],
            [((S, M, z.a_cols), bf16, FAR)],
            name="own_grads",
            us=3,
        )[0]

    def pass_on(up, down, low, high):
        half = M // 2

        def kernel(up_r, down_r, low_r, high_r, up_o, down_o):
            up_o[:half, :] = (up_r[:half, :].astype(f32) + low_r[...].astype(f32)).astype(bf16)
            up_o[half:, :] = up_r[half:, :]
            send(up_o)
            down_o[:half, :] = down_r[:half, :]
            down_o[half:, :] = (down_r[half:, :].astype(f32) + high_r[...].astype(f32)).astype(bf16)

        return run(
            kernel,
            [Far(up), Far(down), Far(low), Far(high)],
            [((M + TAIL, z.a_cols), bf16, FAR)] * 2,
            name="pass_on",
        )

    def join_rows(scal, mine, theirs):
        def kernel(scal_r, a, b, o):
            start = pl.multiple_of(scal_r[8] * R, 16)
            o[pl.ds(start, R), :] = a[...]
            o[pl.ds(pl.multiple_of(R - start, 16), R), :] = b[...]

        return run(kernel, [Far(mine), Far(theirs)], [((2 * R, D), bf16, FAR)], scalars=scal, name="join_rows")[0]

    def sum_blocks(own, others):
        def kernel(own_r, a_r, b_r, o):
            o[...] = (own_r[...].astype(f32) + a_r[...].astype(f32) + b_r[...].astype(f32)).astype(bf16)

        return run(
            kernel,
            [Far(a) for a in [own] + others],
            [((M + TAIL, z.a_cols), bf16, FAR)],
            name="sum_blocks",
        )[0]

    def feed_out(pairs):
        def kernel(*refs):
            up_o, down_o = refs[-2:]
            for l in range(L):
                total = refs[2 * l][...].astype(f32) + refs[2 * l + 1][...].astype(f32)
                up_o[l] = total[:, :F]
                down_o[l] = total[:, F:]

        return run(
            kernel,
            [Far(a) for p in pairs for a in p],
            [((L, M, F), f32, FAR), ((L, M, F), f32, FAR)],
            name="feed_out",
        )

    def proj_out(pairs):
        def kernel(*refs):
            qkv_o, out_o = refs[-2:]
            for l in range(L):
                total = refs[2 * l][...].astype(f32) + refs[2 * l + 1][...].astype(f32)
                if l == 0:
                    total = total[:M]
                for h in range(H):
                    cuts = [total[:, i * A + h * HD : i * A + (h + 1) * HD] for i in range(3)]
                    qkv_o[l, h] = jnp.concatenate(cuts, 1)
                out_o[l] = total[:, 3 * A :].T
        return run(
            kernel,
            [Far(a) for p in pairs for a in p],
            [((L, H, M, 3 * HD), f32, FAR), ((L, A, M), f32, FAR)],
            name="project_out",
        )

    def small_sum(mine, theirs):
        def kernel(a_r, b_r, o):
            o[...] = a_r[M:, :].astype(f32) + b_r[M:, :].astype(f32)

        return run(kernel, [Far(mine), theirs], [((TAIL, z.a_cols), f32, FAR)], name="small_sum")[0]

    def small_out(scal, mine, x_side, core_side, far_side):
        def kernel(scal_r, a_r, x_r, c_r, f_r, qvb_o, upb_o, gain_o, shift_o):
            both = a_r[...] + c_r[...]
            other = x_r[...] + f_r[...]
            odd = scal_r[8] == 1
            part, unit = 2 * HD // S, 64 // S
            for l in range(L):
                rows = both[6 * l : 6 * l + 6, :M]
                first, third = rows[0:1], rows[2:3]
                if l == 0:
                    first, third = first + other[0:1, :M], third + other[2:3, :M]
                gain_o[l] = jnp.concatenate([first, rows[1:2]], 0)
                shift_o[l] = jnp.concatenate([third, rows[3:6]], 0)
                bias = jnp.where(odd, both[2 * l + 1 : 2 * l + 2], both[2 * l : 2 * l + 1])
                for h in range(H):
                    qvb_o[h, l : l + 1, :] = bias[:, q_at + h * part : q_at + (h + 1) * part]
                for r in range(F // 64):
                    upb_o[r, l : l + 1, :] = bias[:, u_at + r * unit : u_at + (r + 1) * unit]

        return run(
            kernel,
            [Far(mine), Far(x_side), Far(core_side), Far(far_side)],
            [
                ((H, L, 2 * HD // S), f32),
                ((F // 64, L, 64 // S), f32),
                ((L, 2, M), f32),
                ((L, 4, M), f32),
            ],
            scalars=scal,
            name="small_out",
        )

    def input_back(x, dy, pa, pb, vec):
        def kernel(x_r, dy_r, pa_r, pb_r, vec_r, o, sums_o):
            dn = pa_r[...].astype(f32) + pb_r[...].astype(f32)
            dx, dgain, dshift = ln_back(x_r[...].astype(f32), vec_r[0:1, :], dn)
            o[...] = (dy_r[...] + dx).astype(bf16)
            sums_o[0:1, :] = dgain
            sums_o[1:2, :] = dshift

        return run(kernel, [x, dy, pa, pb, vec], [((R, D), bf16, FAR), ((2, D), f32)], name="input_back")

    return dict(locals())


def local(mesh):
    def fn(frames, cotangent, w_qkv, qv_bias, w_out, w_up, up_bias, w_down, norm_gains, shifts):
        z = Sizes(mesh, frames, w_qkv, w_up)
        assert frames.shape[0] == 1
        k = make(z)
        L, m, R, D, A, F, H, HD, S = z.layers, z.m, z.rows, z.width, z.att, z.hidden, z.heads, z.hd, z.shards
        core = lax.axis_index("tc")
        scal = ring_scalars(S)

        def part_a(l, *then):
            qkv = after(w_qkv[l], *then).reshape(m, H, 3, HD).transpose(0, 2, 1, 3).reshape(m, 3 * A)
            return jnp.concatenate([qkv, after(w_out[l], *then).reshape(A, m).T], -1)

        def part_b(l, *then):
            return jnp.concatenate([after(w_up[l], *then), after(w_down[l], *then).T], -1)

        message = k["pack_first"](
            w_qkv, w_out, qv_bias, up_bias, norm_gains, shifts
        )
        w_a = [Pieces(message, TAIL) if S == 4 else Gathered(message, S, TAIL)]
        w_b = [Gathered(after(part_b(0, message), *w_a[0].arrays[1:4]), S)]

        def my_rows(x):
            return lax.dynamic_slice_in_dim(x.reshape(2 * R, D), core * R, R, 0)

        kept = []
        x = my_rows(frames)
        for layer in range(L):
            if layer == 0:
                n1, q, kv, vec, qb, tails = k["proj"](scal, x, 0, w_a[0])
            else:
                n1, q, kv, x = k["proj"](scal, after(y, *hid[1:]), layer, w_a[layer], (vec, qb), (part, x_swap(part)))
            far = y_swap(kv)
            near = core_swap(kv)
            if layer + 1 < L:
                next_a, next_b = part_a(layer + 1, n1), part_b(layer + 1, n1)
            acc = k["attend_near"](q, (kv, near))
            kvs = (kv, near, far, core_swap(after(far, acc)))
            o0, o1, qa, o_own, o_snd, att_part = k["attend_far"](scal, q, kvs[2:], acc, w_a[layer])
            far = x_swap(att_part)
            n1_r, o_rcv = core_swap(n1), core_swap(o_snd)
            x = after(x, n1_r, o_rcv)
            if layer + 1 < L:
                w_a.append(Gathered(after(next_a, kvs[1]), S))
                w_b.append(Gathered(after(next_b, att_part), S))
            y, n2, *hid_gp, part = k["feed"](
                scal, x, att_part, far, vec, tails, layer, w_b[layer]
            )
            n2_r, hid_r, gp = core_swap(n2), core_swap(hid_gp[1]), hid_gp[2:]
            hid = (hid_gp[0], hid_r, n2_r)
            kept.append((x, n1, n1_r, kvs, qa, (o0, o1), o_own, o_rcv, y, n2, hid, gp))

        def whole_rows(mine):
            return k["join_rows"](scal, mine, core_swap(mine))[None]

        def scatter(grad):
            return lax.psum_scatter(grad.reshape(D, -1), "shard", scatter_dimension=0, tiled=True)

        y_last, part_last = y, part
        g = my_rows(cotangent)
        wide, d_qv, d_up = [None] * L, [None] * L, [None] * L
        sum_a, sum_b = [None] * L, [None] * L
        before = None
        for layer in reversed(range(L)):
            x, n1, n1_r, kvs, qa, os, o_own, o_rcv, y, n2, hid, gp = kept[layer]
            if before is None:
                swap_b, du, part, sum_g2 = k["feed_back"](scal, g, gp, layer, w_b[layer])
            else:
                gp = [after(gp[0], grad_a), gp[1]]
                swap_b, du, part, sum_g2, g, pre = k["feed_back"](scal, None, gp, layer, w_b[layer], before)
                wide[layer + 1] = [pre] + wide[layer + 1]
            far = x_swap(part)
            grad_b, d_up[layer] = k["feed_grads"](
                scal, n2, hid[2], hid[0], hid[1], swap_b, core_swap(swap_b), du
            )
            y = after(y, grad_b)
            if before is not None:
                sum_b[layer + 1] = (part_b_sum, y_swap(after(part_b_sum, part)))
                y = after(y, sum_b[layer + 1][1])
            if layer > 0:
                part_b_sum = scatter(after(grad_b, far))
            dy, g1, da, mid = k["middle_back"](
                scal, y, g, part, far, vec, os[0], os[1], layer, w_a[layer]
            )
            if layer == 0:
                part_b_sum = scatter(after(grad_b, da))
            g1_r = core_swap(g1)
            dqt, own, snd = k["attend_back"](qa, kvs[2:], da, ahead=layer > 0)
            cross = k["cross_sum"](own, core_swap(snd))
            dqt = after(dqt, cross, g1_r, *([part_a_sum] if layer == 0 else []))
            cross = y_swap(cross)
            dq, own, snd = k["attend_back"](qa, kvs[:2], da, dqt)
            snd = after(snd, cross)
            kv_parts = (own, core_swap(snd), cross)
            dp, dp_snd, part, d_qv[layer], *pre = k["proj_back"](
                scal, dq, kv_parts, layer, w_a[layer], *([x] if layer == 0 else [])
            )
            far = x_swap(part)
            swaps = (n1, n1_r, dp, core_swap(dp_snd), g1, g1_r, o_own, o_rcv)
            if layer > 0:
                grad_a = k["own_grads"](*swaps)
                part_a_sum = scatter(after(grad_a, far))
            else:
                sum_a[1] = (part_a_sum, y_swap(after(part_a_sum, part)))
                wide[0] = pre + [mid, sum_g2]
                small = [wide[l] + [d_up[l], d_qv[l]] for l in range(L)]
                blocks = k["proj_grads"](scal, *swaps, small)
            wide[layer] = pre + [mid, sum_g2]
            before = (x, dy, part, far, vec)
        grad_rows, _ = k["input_back"](x, after(dy, blocks[0]), part, far, vec)
        if S == 4:
            hops = [lax.ppermute(b, "shard", ring(s)) for b, s in zip(blocks[3:], (1, 3))]
            up, down = k["pass_on"](after(blocks[1], grad_rows, sum_a[1][1]), blocks[2], *hops)
            ready = up
            others = [lax.ppermute(up, "shard", ring(1)), lax.ppermute(down, "shard", ring(3))]
        else:
            ready = blocks[0]
        part_b_sum = after(part_b_sum, ready)
        sum_b[0] = (part_b_sum, y_swap(part_b_sum))
        far_last = x_swap(after(part_last, ready))
        last_rows = k["finish"](y_last, part_last, far_last, vec)[0]
        frames_grad = whole_rows(grad_rows)
        block = after(blocks[0], sum_b[0][1], frames_grad, last_rows)
        if S == 4:
            mine = k["sum_blocks"](block, others)
        else:
            mine = lax.psum_scatter(block, "shard", scatter_dimension=0, tiled=True)[0]
        theirs = y_swap(mine)
        sum_a[0] = (mine, theirs)
        out_frames = whole_rows(after(last_rows, mine))
        outs_up, outs_down = k["feed_out"]([sum_b[0], (after(sum_b[1][0], mine), sum_b[1][1])])
        tiny = k["small_sum"](after(mine, outs_up, out_frames), theirs)
        tiny_x = x_swap(tiny)
        tiny_c = core_swap(tiny)
        outs_qkv, outs_out = k["proj_out"]([(after(mine, tiny), theirs), sum_a[1]])
        tiny_f = core_swap(after(tiny_x, outs_qkv))
        g_qvb, g_upb, g_gains, g_shifts = k["small_out"](
            scal, tiny, tiny_x, tiny_c, tiny_f
        )
        return (
            out_frames,
            frames_grad,
            outs_qkv.transpose(0, 2, 1, 3),
            g_qvb.transpose(1, 0, 2),
            outs_out.reshape(L, H, HD, m),
            outs_up,
            g_upb.transpose(1, 0, 2),
            outs_down.transpose(0, 2, 1),
            g_gains,
            g_shifts,
        )

    return fn


def solution(mesh):
    assert mesh.axis_names == ("shard", "ctx", "tp") and mesh.shape["tp"] == 4 and mesh.shape["ctx"] == 2
    split = Mesh(mesh.devices.reshape(mesh.shape["shard"], 2, 2, 2), ("shard", "ctx", "tx", "tc"))
    tp = ("tx", "tc")
    specs = (
        P("shard", "ctx", None),
        P("shard", "ctx", None),
        P(None, "shard", tp, None),
        P(None, tp, "shard"),
        P(None, tp, None, "shard"),
        P(None, "shard", tp),
        P(None, tp, "shard"),
        P(None, tp, "shard"),
        P(None, None, "shard"),
        P(None, None, "shard"),
    )
    return jax.shard_map(local(split), mesh=split, in_specs=specs, out_specs=specs, check_vma=False)
```
